32 devices in a mesh: island: 16 (over z, x, core), fsdp: 2 (over y).
Axes of the slice: x: 2, y: 2, z: 4, core: 2. Of those that a mesh axis runs over, the one named last changes fastest.
Arguments:
- activations: bfloat16 [4096, 8192], P(('island', 'fsdp')), may hold values from -6 to 6
- cotangent: bfloat16 [4096, 1024], P(('island', 'fsdp')), may hold values from -6 to 6
- inner_weight: bfloat16 [16, 8192, 1024], P('island', 'fsdp'), may hold values from -0.09375 to 0.09375
- outer_weight: float32 [8192, 1024], P(('fsdp', 'island')), may hold values from -0.0625 to 0.0625
- outer_momentum: float32 [8192, 1024], P(('fsdp', 'island')), may hold values from -0.06 to 0.06
- next_activations: bfloat16 [4096, 8192], P(('island', 'fsdp')), may hold values from -6 to 6
Outputs:
- input_grad: bfloat16 [4096, 8192], P(('island', 'fsdp'))
- next_keys: bfloat16 [4096, 1024], P(('island', 'fsdp'))
- new_outer: float32 [8192, 1024], P(('fsdp', 'island'))
- new_momentum: float32 [8192, 1024], P(('fsdp', 'island'))
The draws below stay inside these ranges and needn't reach their ends.
All inputs are finite; a program needn't handle non-finite values.
Results may differ from the reference program's by a relative error of at most 0.0049.
Values may be sent and summed in bfloat16 or wider, within the bound.
No kernel may reach another device: no remote copies, remote signals or barrier semaphores. Data moves between devices by JAX's collectives and lax.ppermute only.
A program may use at most 128 MiB of HBM per device.

```python
import jax
import jax.numpy as jnp
from jax import lax

D = 8192
KV = 1024
TOK_DEV = 128
TOKENS = 4096
N_ISLAND = 16
N_FSDP = 2


def raised(drawn, own_key, source, target, shards_of, factor):
    owner, partner = [(jnp.arange(drawn.shape[position]) // (drawn.shape[position] // shards_of)).reshape([-1 if axis == position else 1 for axis in range(drawn.ndim)]) for position in (source, target)]
    chosen = jax.random.permutation(own_key, shards_of)[partner]
    strong = (owner == chosen) | (owner == (partner + shards_of // 2) % shards_of)
    return jnp.where(strong, factor * drawn, drawn)


def levels(rng, extent, split, low, high):
    def one(dim, blocks):
        steps = jax.random.uniform(jax.random.fold_in(jax.random.fold_in(rng, 6), dim), (blocks,), jnp.float32, low / len(split), high / len(split))
        return jnp.repeat(jnp.exp(steps), extent[dim] // blocks).reshape((-1,) + (1,) * (len(extent) - dim - 1))

    loudness = one(*split[0])
    for cut in split[1:]:
        loudness = loudness * one(*cut)
    return loudness


def gaussian(key, shape, deviation, bound, split=(), kind=jnp.bfloat16):
    values = jax.random.normal(key, shape, jnp.float32) * deviation
    if len(split) > 0:
        values = levels(key, shape, split, -0.22, 0.18) * values
    return jnp.clip(values, min=-bound, max=bound).astype(kind)


def noise_with(own_key, dims, spread, reach, cuts, heavy, kind=jnp.bfloat16):
    array = spread * jax.random.normal(own_key, dims, jnp.float32)
    if cuts:
        array = array * levels(own_key, dims, cuts, -0.22, 0.18)
    return jnp.clip(raised(array, jax.random.fold_in(own_key, 3), *heavy), -reach, reach).astype(kind)


def setup_inputs(seed: int = 0) -> dict:
    arg_keys = jax.random.split(jax.random.key(seed), 7)
    return {
        "activations": gaussian(arg_keys[0], (TOKENS, D), 1.0, 6.0, ((0, 32),)),
        "cotangent": gaussian(arg_keys[1], (TOKENS, KV), 1.0, 6.0, ((0, 32),)),
        "inner_weight": noise_with(arg_keys[2], (N_ISLAND, D, KV), D ** -0.5, 0.09375, ((0, 16), (1, 2)), (0, 1, 16, 2.0)),
        "outer_weight": gaussian(arg_keys[3], (D, KV), D ** -0.5, 0.0625, ((0, 32),), jnp.float32),
        "outer_momentum": gaussian(arg_keys[4], (D, KV), 0.01, 0.06, ((0, 32),), jnp.float32),
        "next_activations": gaussian(arg_keys[5], (TOKENS, D), 1.0, 6.0, ((0, 32),)),
    }


inner_rate = 1.2
outer_rate = 0.7
nesterov = 0.9


def reference(activations, cotangent, inner_weight, outer_weight, outer_momentum, next_activations):
    island_acts = activations.reshape(N_ISLAND, TOK_DEV * N_FSDP, D)
    island_cots = cotangent.reshape(N_ISLAND, TOK_DEV * N_FSDP, KV)

    def island_step(running, slices_now):
        inputs_now, cot_now, weight_now = slices_now
        weight_grad = lax.dot_general(inputs_now, cot_now, (((0,), (0,)), ((), ())), preferred_element_type=jnp.float32) / (TOK_DEV * N_FSDP)
        inner_new = weight_now.astype(jnp.float32) - inner_rate * weight_grad
        grad_rows = lax.dot_general(cot_now, weight_now, (((1,), (1,)), ((), ())), preferred_element_type=jnp.float32).astype(jnp.bfloat16)
        return running + inner_new, grad_rows

    running, grad_rows = lax.scan(island_step, jnp.zeros((D, KV), jnp.float32), (island_acts, island_cots, inner_weight))
    input_grad = grad_rows.reshape(TOKENS, D)
    pseudo_grad = outer_weight - running / N_ISLAND
    new_momentum = nesterov * outer_momentum + pseudo_grad
    new_outer = outer_weight - outer_rate * (pseudo_grad + nesterov * new_momentum)
    next_weight = new_outer.astype(jnp.bfloat16)
    next_keys = jnp.dot(next_activations, next_weight, preferred_element_type=jnp.float32).astype(jnp.bfloat16)
    return input_grad, next_keys, new_outer, new_momentum
```

```python
import functools

import jax
import jax.numpy as jnp
from jax import lax
from jax.experimental import pallas as pl
from jax.experimental.pallas import tpu as pltpu
from jax.sharding import Mesh, PartitionSpec as P

inner_rate = 1.2
outer_rate = 0.7
nesterov = 0.9
CORES = 2
PAIR = 2

bf16, f32 = jnp.bfloat16, jnp.float32


def ring(count, shift):
    return [(i, (i + shift) % count) for i in range(count)]


def inner_kernel(fsdp, share, scale, place, *refs):
    acts, cots = refs[:fsdp], refs[fsdp : 2 * fsdp]
    weight, give, keep, total = refs[2 * fsdp :]
    core = place[2]
    grad = None
    for a, g in zip(acts, cots):
        term = lax.dot_general(a[...], g[...], (((0,), (0,)), ((), ())), preferred_element_type=f32)
        grad = term if grad is None else grad + term
    total[...] = weight[...].astype(f32) - scale * grad
    for x in range(PAIR):
        here = pl.ds(x * share, share)
        theirs = pl.multiple_of((x * CORES + 1 - core) * share, share)
        ours = pl.multiple_of((x * CORES + core) * share, share)
        give[here, :] = total[pl.ds(theirs, share), :].astype(bf16)
        keep[here, :] = total[pl.ds(ours, share), :]


def inner_block(place, acts, cots, weight, share, tile=256):
    fsdp = len(acts)
    tok, kv = cots[0].shape
    block = PAIR * CORES * share
    half = PAIR * share
    spec = pltpu.PrefetchScalarGridSpec(
        num_scalar_prefetch=1,
        grid=(kv // tile,),
        in_specs=[pl.BlockSpec((tok, block), lambda i, p: (0, p[0]))]
        + [pl.BlockSpec((tok, block), lambda i, p: (0, 0))] * (fsdp - 1)
        + [pl.BlockSpec((tok, tile), lambda i, p: (0, i))] * fsdp
        + [pl.BlockSpec((block, tile), lambda i, p: (p[1], i))],
        out_specs=[pl.BlockSpec((half, tile), lambda i, p: (0, i))] * 2,
        scratch_shapes=[pltpu.VMEM((block, tile), f32)],
    )
    return pl.pallas_call(
        functools.partial(inner_kernel, fsdp, share, inner_rate / (tok * fsdp)),
        out_shape=[jax.ShapeDtypeStruct((half, kv), bf16), jax.ShapeDtypeStruct((half, kv), f32)],
        grid_spec=spec,
        compiler_params=pltpu.CompilerParams(vmem_limit_bytes=32 * 1024 * 1024),
        cost_estimate=pl.CostEstimate(
            flops=2 * tok * fsdp * block * kv, bytes_accessed=block * kv * 5 + 2 * tok * fsdp * (block + kv), transcendentals=0
        ),
    )(place, *acts, *cots, weight)


def local(activations, cotangent, inner_weight, outer_weight, outer_momentum, next_activations):
    fsdp, nz = lax.axis_size("fsdp"), lax.axis_size("z")
    f, z, x, c = (lax.axis_index(a) for a in ("fsdp", "z", "x", "core"))
    tok, d = activations.shape
    kv = cotangent.shape[1]
    width = d // fsdp
    block = width // nz
    share = block // (PAIR * CORES)
    own_weight = inner_weight[0]

    def columns(array, start, size):
        return lax.dynamic_slice_in_dim(array, start, size, axis=1)

    cots = [cotangent] + [lax.ppermute(cotangent, "fsdp", ring(fsdp, s)) for s in range(1, fsdp)]

    kept = []
    for j in range(nz):
        b = z ^ (nz - 1 - j)
        acts = [activations]
        for s in range(1, fsdp):
            mine = columns(activations, ((f + s) % fsdp) * width + b * block, block)
            acts.append(lax.ppermute(mine, "fsdp", ring(fsdp, s)))
        place = jnp.stack([f * nz + b, b, c]).astype(jnp.int32)
        give, keep = inner_block(place, acts, cots, own_weight, share)
        other = lax.ppermute(give, "core", ring(CORES, 1))

        def rows(array, index):
            return lax.dynamic_slice_in_dim(array, index * share, share, axis=0).astype(f32)

        over_x = (rows(keep, 1 - x) + rows(other, 1 - x)).astype(bf16)
        here = rows(keep, x) + rows(other, x)
        kept.append(here + lax.ppermute(over_x, "x", ring(PAIR, 1)).astype(f32))

    def kept_at(b, slots):
        chosen = kept[slots[0]]
        for j in slots[1:]:
            chosen = jnp.where(b == z ^ (nz - 1 - j), kept[j], chosen)
        return chosen

    up = down = None
    for t in range(1, nz):
        dist = nz - t
        slots_up = sorted({nz - 1 - ((i + dist) ^ i) for i in range(t)})
        slots_down = sorted({nz - 1 - ((i - dist) ^ i) for i in range(dist, nz)})
        send_up, send_down = kept_at(z + dist, slots_up), kept_at(z - dist, slots_down)
        if up is not None:
            send_up, send_down = send_up + up.astype(f32), send_down + down.astype(f32)
        up = lax.ppermute(send_up.astype(bf16), "z", [(i, i + 1) for i in range(t)])
        down = lax.ppermute(send_down.astype(bf16), "z", [(i, i - 1) for i in range(dist, nz)])
    summed = kept[nz - 1] + (up.astype(f32) + down.astype(f32))

    grad_rows = lax.dot_general(
        jnp.concatenate(cots, axis=0), own_weight, (((1,), (1,)), ((), ())), preferred_element_type=f32
    ).astype(bf16)
    input_grad = jnp.zeros((tok, d), bf16)
    for s in range(fsdp):
        part = grad_rows[s * tok : (s + 1) * tok]
        if s:
            part = lax.ppermute(part, "fsdp", ring(fsdp, -s))
        input_grad = lax.dynamic_update_slice_in_dim(input_grad, part, ((f + s) % fsdp) * width, axis=1)

    nexts = [columns(next_activations, f * width, width)]
    for s in range(1, fsdp):
        mine = columns(next_activations, ((f + s) % fsdp) * width, width)
        nexts.append(lax.ppermute(mine, "fsdp", ring(fsdp, s)))
    nexts = jnp.concatenate(nexts, axis=0).reshape(fsdp * tok, nz * PAIR, CORES, share)

    def of_core(core):
        return lax.dynamic_index_in_dim(nexts, core, 2, keepdims=False).reshape(fsdp * tok, nz * PAIR * share)

    nexts = jnp.concatenate([of_core(c), lax.ppermute(of_core(1 - c), "core", ring(CORES, 1))], axis=0)

    pseudo_grad = outer_weight - summed / (nz * PAIR * CORES)
    new_momentum = nesterov * outer_momentum + pseudo_grad
    new_outer = outer_weight - outer_rate * (pseudo_grad + nesterov * new_momentum)
    weight_rows = lax.all_gather(new_outer.astype(bf16), ("z", "x"), axis=0, tiled=True)

    partial = jnp.dot(nexts, weight_rows, preferred_element_type=f32)
    rows = fsdp * tok
    mine = partial[:rows] + lax.ppermute(partial[rows:].astype(bf16), "core", ring(CORES, 1)).astype(f32)
    keys = mine[:tok]
    for s in range(1, fsdp):
        keys = keys + lax.ppermute(mine[s * tok : (s + 1) * tok].astype(bf16), "fsdp", ring(fsdp, -s)).astype(f32)
    return (input_grad, keys.astype(bf16), new_outer, new_momentum)


def solution(mesh):
    fsdp = mesh.shape["fsdp"]
    nz = mesh.shape["island"] // (PAIR * CORES)
    split = Mesh(mesh.devices.reshape(nz, PAIR, CORES, fsdp), ("z", "x", "core", "fsdp"))
    island = ("z", "x", "core")
    tokens = P(island + ("fsdp",), None)
    width = P(("fsdp",) + island, None)
    in_specs = (tokens, tokens, P(island, "fsdp", None), width, width, tokens)
    out_specs = (tokens, tokens, width, width)
    return jax.shard_map(local, mesh=split, in_specs=in_specs, out_specs=out_specs, check_vma=False)
```

```python
import functools

import jax
import jax.numpy as jnp
from jax import lax
from jax.experimental import pallas as pl
from jax.experimental.pallas import tpu as pltpu
from jax.sharding import Mesh, PartitionSpec as P

inner_rate = 1.2
outer_rate = 0.7
nesterov = 0.9
CORES = 2
PAIR = 2
LANES = 128

bf16, f32 = jnp.bfloat16, jnp.float32
VMEM, HBM = pl.BlockSpec(memory_space=pltpu.VMEM), pl.BlockSpec(memory_space=pltpu.HBM)
SMEM = pl.BlockSpec(memory_space=pltpu.SMEM)
MIB = 1024 * 1024


def ring(count, shift):
    return [(i, (i + shift) % count) for i in range(count)]


def strip(axis, start, size):
    return (pl.ds(start, size), slice(None)) if axis == 0 else (slice(None), pl.ds(start, size))


def in_hbm(array):
    return pltpu.with_memory_space_constraint(array, pltpu.HBM)


def pack_kernel(plan, starts, *refs):
    sources, outs, done = refs[: len(plan)], refs[len(plan) : -1], refs[-1]
    copies, o = [], 0
    for source, (axis, size, counts) in zip(sources, plan):
        for count in counts:
            for i in range(count):
                n = len(copies)
                part = source.at[strip(axis, pl.multiple_of(starts[n], size), size)]
                copies.append(pltpu.make_async_copy(part, outs[o].at[strip(axis, i * size, size)], done.at[n]))
            o += 1
    for copy in copies:
        copy.start()
    for copy in copies:
        copy.wait()


def pack(items, after=()):
    result, rest = {}, []
    for n, (array, axis, size, groups) in enumerate(items):
        if axis == 1 and size % LANES:
            strips = [[lax.dynamic_slice_in_dim(array, at, size, axis=axis) for at in group] for group in groups]
            result[n] = [jnp.concatenate(group, axis=axis) for group in strips]
        else:
            rest.append((n, array, axis, size, groups))
    if not rest:
        return [result[n] for n in range(len(items))], list(after)
    starts = jnp.stack([at for item in rest for group in item[4] for at in group]).astype(jnp.int32)
    if after:
        starts, *after = lax.optimization_barrier((starts, *after))
    plan, shapes = [], []
    for _, array, axis, size, groups in rest:
        counts = [len(group) for group in groups]
        plan.append((axis, size, counts))
        for n in counts:
            shape = (n * size, array.shape[1]) if axis == 0 else (array.shape[0], n * size)
            shapes.append(jax.ShapeDtypeStruct(shape, array.dtype))
    moved = sum(4 * shape.size for shape in shapes)
    outs = pl.pallas_call(
        functools.partial(pack_kernel, plan),
        out_shape=shapes,
        in_specs=[SMEM] + [HBM] * len(rest),
        out_specs=[pl.BlockSpec(memory_space=pl.ANY)] * len(shapes),
        scratch_shapes=[pltpu.SemaphoreType.DMA((starts.shape[0],))],
        compiler_params=pltpu.CompilerParams(vmem_limit_bytes=4 * MIB),
        cost_estimate=pl.CostEstimate(flops=0, bytes_accessed=moved, transcendentals=0),
    )(starts, *[in_hbm(item[1]) for item in rest])
    for n, *_, groups in rest:
        result[n], outs = outs[: len(groups)], outs[len(groups) :]
    return [result[n] for n in range(len(items))], list(after)


def inner_kernel(pieces, share, scale, act_at, other_at, place, *refs):
    acts, cots = refs[:pieces], refs[pieces : 2 * pieces]
    own, other, give, keep, rows, total, done = refs[2 * pieces :]
    copies = []
    for i in range(PAIR):
        for n, (weight, at) in enumerate(((own, place[i] * share), (other, other_at + i * share))):
            source = weight.at[pl.ds(pl.multiple_of(at, share), share), :]
            copies.append(pltpu.make_async_copy(source, rows.at[n, i], done.at[n, i]))
    for copy in copies:
        copy.start()
    left = jnp.concatenate([a[:, act_at : act_at + PAIR * share] for a in acts], axis=0)
    right = jnp.concatenate([g[...] for g in cots], axis=0)
    total[...] = lax.dot_general(left, right, (((0,), (0,)), ((), ())), preferred_element_type=f32)
    for copy in copies:
        copy.wait()
    x = place[PAIR]

    def inner_new(i):
        grad = total[pl.ds(pl.multiple_of(i * share, share), share), :]
        return (rows[0, i].astype(f32) + rows[1, i].astype(f32)) - scale * grad

    give[...] = inner_new(1 - x).astype(bf16)
    keep[...] = inner_new(x)


def inner_block(place, acts, act_at, cots, own, other, other_at, share):
    pieces = len(acts)
    tok, kv = cots[0].shape
    if act_at % LANES or PAIR * share % LANES:
        acts, act_at = [a[:, act_at : act_at + PAIR * share] for a in acts], 0
    return pl.pallas_call(
        functools.partial(inner_kernel, pieces, share, inner_rate / (tok * pieces // CORES), act_at, other_at),
        out_shape=[jax.ShapeDtypeStruct((share, kv), bf16), jax.ShapeDtypeStruct((share, kv), f32)],
        in_specs=[SMEM] + [VMEM] * (2 * pieces) + [HBM] * 2,
        out_specs=[VMEM] * 2,
        scratch_shapes=[
            pltpu.VMEM((CORES, PAIR, share, kv), bf16),
            pltpu.VMEM((PAIR * share, kv), f32),
            pltpu.SemaphoreType.DMA((CORES, PAIR)),
        ],
        compiler_params=pltpu.CompilerParams(vmem_limit_bytes=24 * MIB),
        cost_estimate=pl.CostEstimate(flops=pieces * tok * share * kv, bytes_accessed=share * kv, transcendentals=0),
    )(place, *acts, *cots, in_hbm(own), other)


def keys_kernel(acts_count, at, *refs):
    acts, (*blocks, out) = refs[:acts_count], refs[acts_count:]
    if at:
        *blocks, before = blocks
    weight = jnp.concatenate([w[...] for w in blocks], axis=0)
    left = jnp.concatenate([a[:, at : at + weight.shape[0]] for a in acts], axis=0)
    product = jnp.dot(left, weight, preferred_element_type=f32)
    out[...] = before[...] + product if at else product


def keys_part(acts, blocks, at, before=()):
    rows, kv = len(acts) * acts[0].shape[0], blocks[0].shape[1]
    depth = sum(w.shape[0] for w in blocks)
    if at % LANES:
        acts = [a[:, at:] for a in acts]
        return before[0] + keys_part(acts, blocks, 0)
    return pl.pallas_call(
        functools.partial(keys_kernel, len(acts), at),
        out_shape=jax.ShapeDtypeStruct((rows, kv), f32),
        in_specs=[VMEM] * (len(acts) + len(blocks) + len(before)),
        out_specs=VMEM,
        compiler_params=pltpu.CompilerParams(vmem_limit_bytes=24 * MIB),
        cost_estimate=pl.CostEstimate(flops=2 * rows * depth * kv, bytes_accessed=rows * kv, transcendentals=0),
    )(*acts, *blocks, *before)


def core_sum_kernel(fsdp, tok, keep, came, to_x, stay_x, stay_f, *to_f):
    half = keep.shape[1] // 2
    total = keep[...] + came[...]
    rows = fsdp * tok
    stay_x[...] = total[:rows, :half]
    to_x[...] = total[rows:, :half].astype(bf16)
    for i in range(PAIR):
        here = slice(i * tok, (i + 1) * tok)
        stay_f[here, :] = total[i * rows : i * rows + tok, half:]
        for s in range(1, fsdp):
            to_f[s - 1][here, :] = total[i * rows + s * tok : i * rows + (s + 1) * tok, half:].astype(bf16)


def second_sum_kernel(fsdp, tok, *refs):
    stay_x, stay_f, from_x, *from_f = refs[: fsdp + 2]
    left, right, to_x, *to_f = refs[fsdp + 2 :]
    first = stay_x[...] + from_x[...].astype(f32)
    left[...] = first[:tok]
    for s in range(1, fsdp):
        to_f[s - 1][...] = first[s * tok : (s + 1) * tok].astype(bf16)
    second = stay_f[...]
    for came in from_f:
        second = second + came[...].astype(f32)
    right[...] = second[:tok]
    to_x[...] = second[tok:].astype(bf16)


def last_sum_kernel(left, right, from_x, *refs):
    *from_f, keys = refs
    half = left.shape[1]
    first = left[...]
    for came in from_f:
        first = first + came[...].astype(f32)
    keys[:, :half] = first.astype(bf16)
    keys[:, half:] = (right[...] + from_x[...].astype(f32)).astype(bf16)


def small_call(kernel, shapes, *args):
    size = sum(shape.size for shape in shapes)
    return pl.pallas_call(
        kernel,
        out_shape=shapes,
        in_specs=[VMEM] * len(args),
        out_specs=[VMEM] * len(shapes),
        compiler_params=pltpu.CompilerParams(vmem_limit_bytes=24 * MIB),
        cost_estimate=pl.CostEstimate(flops=size, bytes_accessed=8 * size, transcendentals=0),
    )(*args)


def join_kernel(starts, *refs):
    *parts, out, done = refs
    copies = []
    for n, part in enumerate(parts):
        width = part.shape[1]
        here = out.at[:, pl.ds(pl.multiple_of(starts[n], width), width)]
        copies.append(pltpu.make_async_copy(part, here, done.at[n]))
    for copy in copies:
        copy.start()
    for copy in copies:
        copy.wait()


def join(parts, starts):
    rows, width = parts[0].shape
    return pl.pallas_call(
        join_kernel,
        out_shape=jax.ShapeDtypeStruct((rows, width * len(parts)), parts[0].dtype),
        in_specs=[SMEM] + [pl.BlockSpec(memory_space=pl.ANY)] * len(parts),
        out_specs=HBM,
        scratch_shapes=[pltpu.SemaphoreType.DMA((len(parts),))],
        compiler_params=pltpu.CompilerParams(vmem_limit_bytes=4 * MIB),
        cost_estimate=pl.CostEstimate(flops=0, bytes_accessed=4 * rows * width * len(parts), transcendentals=0),
    )(jnp.stack(starts).astype(jnp.int32), *parts)


def local(activations, cotangent, inner_weight, outer_weight, outer_momentum, next_activations):
    fsdp, nz = lax.axis_size("fsdp"), lax.axis_size("z")
    f, z, x, c = (lax.axis_index(a) for a in ("fsdp", "z", "x", "core"))
    tok, d = activations.shape
    kv = cotangent.shape[1]
    width = d // fsdp
    block = width // nz
    share = block // (PAIR * CORES)
    own_weight = inner_weight[0]
    swap = ring(CORES, 1)

    def column(b, i, k, s):
        return ((f + s) % fsdp) * width + b * block + i * CORES * share + ((c + k) % CORES) * share

    def pair_ring(k, s):
        at = lambda i, j: (i % CORES) * fsdp + j % fsdp
        return [(at(i, j), at(i + k, j + s)) for i in range(CORES) for j in range(fsdp)]

    shifts = [(k, s) for s in range(fsdp) for k in range(CORES)]
    stages = [[nz - 1], list(range(nz - 2, -1, -1))]

    cots = {(0, 0): cotangent}
    for s in range(1, fsdp):
        cots[0, s] = lax.ppermute(cotangent, "fsdp", ring(fsdp, s))
    packed, after = [], []
    for ms in stages:
        columns = [[column(z ^ m, i, k, s) for m in ms for i in range(PAIR)] for k, s in shifts]
        rows = [((z ^ m) * PAIR * CORES + i * CORES + 1 - c) * share for m in ms for i in range(PAIR)]
        (mine, (weight,)), after = pack([(activations, 1, share, columns), (own_weight, 0, share, [rows])], after)
        if packed:
            packed[-1] = (after[:-1], after[-1])
        packed.append((mine, weight))
        after = [*mine, weight]
    acts, other = [], []
    for mine, weight in packed:
        came = []
        for (k, s), part in zip(shifts, mine):
            came.append(part if (k, s) == (0, 0) else lax.ppermute(part, ("core", "fsdp"), pair_ring(k, s)))
        acts.append(came)
        other.append(lax.ppermute(weight, "core", swap))
    cots[1, 0] = lax.ppermute(cotangent, "core", swap)
    for s in range(1, fsdp):
        cots[1, s] = lax.ppermute(cots[0, s], "core", swap)

    total = {}
    given = None
    for stage, ms in enumerate(stages):
        for n, m in enumerate(ms):
            place = jnp.stack([((z ^ m) * PAIR + i) * CORES + c for i in range(PAIR)] + [x]).astype(jnp.int32)
            at = n * PAIR * share
            ordered = [cots[k, s] for k, s in shifts]
            if given is not None:
                place, _ = lax.optimization_barrier((place, given))
            given, keep = inner_block(place, acts[stage], at, ordered, own_weight, other[stage], at, share)
            held = keep + lax.ppermute(given, "x", ring(PAIR, 1)).astype(f32)
            total[m] = held if m not in total else held + total[m]
            if m:
                low = m & -m
                came = lax.ppermute(total[m].astype(bf16), "z", [(i, i ^ low) for i in range(nz)]).astype(f32)
                total[m ^ low] = came if m ^ low not in total else total[m ^ low] + came
    summed = total[0]

    grad_rows = lax.dot_general(
        jnp.concatenate([cots[0, s] for s in range(fsdp)], axis=0),
        own_weight,
        (((1,), (1,)), ((), ())),
        preferred_element_type=f32,
    ).astype(bf16)
    parts = [grad_rows[:tok]]
    for s in range(1, fsdp):
        parts.append(lax.ppermute(grad_rows[s * tok : (s + 1) * tok], "fsdp", ring(fsdp, -s)))

    far = [(i, k, s) for k in range(CORES) for i in range(PAIR) for s in range(fsdp)]
    at = lambda i, k, s: ((i % PAIR) * CORES + k % CORES) * fsdp + s % fsdp
    every = [(i, k, s) for i in range(PAIR) for k in range(CORES) for s in range(fsdp)]
    groups = [[column(z ^ m, (x + i) % PAIR, k, s) for m in range(nz)] for i, k, s in far]
    (mine,), _ = pack([(next_activations, 1, share, groups)])
    mine = dict(zip(far, mine))
    nexts = {}

    def send_next(i, k, s):
        pairs = [(at(*e), at(e[0] + i, e[1] + k, e[2] + s)) for e in every]
        nexts[i, k, s] = lax.ppermute(mine[i, k, s], ("x", "core", "fsdp"), pairs) if i or k or s else mine[i, k, s]

    near, away = [e for e in far if e[0] == 0], [e for e in far if e[0]]
    for e in near:
        send_next(*e)
    held = [summed, *parts, *[nexts[e] for e in near], *[mine[e] for e in away]]
    summed, *held = lax.optimization_barrier(held)
    parts, held = held[: len(parts)], held[len(parts) :]
    nexts.update(zip(near, held))
    mine.update(zip(away, held[len(near) :]))

    pseudo_grad = outer_weight - summed / (nz * PAIR * CORES)
    new_momentum = nesterov * outer_momentum + pseudo_grad
    new_outer = outer_weight - outer_rate * (pseudo_grad + nesterov * new_momentum)

    rows = [new_outer.astype(bf16)]
    for m in range(1, nz):
        low = m & -m
        source = rows[m ^ low]
        if m == nz - 1:
            input_grad = join(parts, [((f + s) % fsdp) * width for s in range(fsdp)])
            for e in away:
                send_next(*e)
            source, input_grad, *came = lax.optimization_barrier((source, input_grad, *[nexts[e] for e in away]))
            nexts.update(zip(away, came))
        rows.append(lax.ppermute(source, "z", [(i, i ^ low) for i in range(nz)]))

    half = len(far) // CORES
    near, away = [nexts[e] for e in far[:half]], [nexts[e] for e in far[half:]]
    give, keep = keys_part(away, rows[:-1], 0), keys_part(near, rows[:-1], 0)
    last = (nz - 1) * share
    give = keys_part(away, rows[-1:], last, [give])
    keep = keys_part(near, rows[-1:], last, [keep])
    came = lax.ppermute(give, "core", swap)
    shape = lambda n, kind: jax.ShapeDtypeStruct((n, kv // 2), kind)
    to_x, stay_x, stay_f, *to_f = small_call(
        functools.partial(core_sum_kernel, fsdp, tok),
        [shape(fsdp * tok, bf16), shape(fsdp * tok, f32), shape(PAIR * tok, f32)] + [shape(PAIR * tok, bf16)] * (fsdp - 1),
        keep,
        came,
    )

    def home(to_x, to_f):
        from_x = lax.ppermute(to_x, "x", ring(PAIR, 1))
        return [from_x] + [lax.ppermute(part, "fsdp", ring(fsdp, -s - 1)) for s, part in enumerate(to_f)]

    left, right, to_x, *to_f = small_call(
        functools.partial(second_sum_kernel, fsdp, tok),
        [shape(tok, f32)] * 2 + [shape(tok, bf16)] * fsdp,
        stay_x,
        stay_f,
        *home(to_x, to_f),
    )
    (keys,) = small_call(
        last_sum_kernel, [jax.ShapeDtypeStruct((tok, kv), bf16)], left, right, *home(to_x, to_f)
    )
    return (input_grad, keys, new_outer, new_momentum)


def solution(mesh):
    fsdp = mesh.shape["fsdp"]
    nz = mesh.shape["island"] // (PAIR * CORES)
    split = Mesh(mesh.devices.reshape(nz, PAIR, CORES, fsdp), ("z", "x", "core", "fsdp"))
    island = ("z", "x", "core")
    tokens = P(island + ("fsdp",), None)
    width = P(("fsdp",) + island, None)
    in_specs = (tokens, tokens, P(island, "fsdp", None), width, width, tokens)
    out_specs = (tokens, tokens, width, width)
    return jax.shard_map(local, mesh=split, in_specs=in_specs, out_specs=out_specs, check_vma=False)
```

```python
import functools

import jax
import jax.numpy as jnp
from jax import lax
from jax.experimental import pallas as pl
from jax.experimental.pallas import tpu as pltpu
from jax.sharding import Mesh, PartitionSpec as P

inner_rate = 1.2
outer_rate = 0.7
nesterov = 0.9
CORES = 2
PAIR = 2
LANES = 128

bf16, f32 = jnp.bfloat16, jnp.float32
VMEM, HBM = pl.BlockSpec(memory_space=pltpu.VMEM), pl.BlockSpec(memory_space=pltpu.HBM)
SMEM = pl.BlockSpec(memory_space=pltpu.SMEM)
MIB = 1024 * 1024


def ring(count, shift):
    return [(i, (i + shift) % count) for i in range(count)]


def strip(axis, start, size):
    return (pl.ds(start, size), slice(None)) if axis == 0 else (slice(None), pl.ds(start, size))


def in_hbm(array):
    return pltpu.with_memory_space_constraint(array, pltpu.HBM)


def pack_kernel(plan, starts, *refs):
    sources, outs, done = refs[: len(plan)], refs[len(plan) : -1], refs[-1]
    copies, o = [], 0
    for source, (axis, size, counts) in zip(sources, plan):
        for count in counts:
            for i in range(count):
                n = len(copies)
                part = source.at[strip(axis, pl.multiple_of(starts[n], size), size)]
                copies.append(pltpu.make_async_copy(part, outs[o].at[strip(axis, i * size, size)], done.at[n]))
            o += 1
    for copy in copies:
        copy.start()
    for copy in copies:
        copy.wait()


def pack(items, after=()):
    result, rest = {}, []
    for n, (array, axis, size, groups) in enumerate(items):
        if axis == 1 and size % LANES:
            strips = [[lax.dynamic_slice_in_dim(array, at, size, axis=axis) for at in group] for group in groups]
            result[n] = [jnp.concatenate(group, axis=axis) for group in strips]
        else:
            rest.append((n, array, axis, size, groups))
    if not rest:
        return [result[n] for n in range(len(items))], list(after)
    starts = jnp.stack([at for item in rest for group in item[4] for at in group]).astype(jnp.int32)
    if after:
        starts, *after = lax.optimization_barrier((starts, *after))
    plan, shapes = [], []
    for _, array, axis, size, groups in rest:
        counts = [len(group) for group in groups]
        plan.append((axis, size, counts))
        for n in counts:
            shape = (n * size, array.shape[1]) if axis == 0 else (array.shape[0], n * size)
            shapes.append(jax.ShapeDtypeStruct(shape, array.dtype))
    moved = sum(4 * shape.size for shape in shapes)
    outs = pl.pallas_call(
        functools.partial(pack_kernel, plan),
        out_shape=shapes,
        in_specs=[SMEM] + [HBM] * len(rest),
        out_specs=[VMEM] * len(shapes),
        scratch_shapes=[pltpu.SemaphoreType.DMA((starts.shape[0],))],
        compiler_params=pltpu.CompilerParams(vmem_limit_bytes=16 * MIB),
        cost_estimate=pl.CostEstimate(flops=0, bytes_accessed=moved, transcendentals=0),
    )(starts, *[in_hbm(item[1]) for item in rest])
    for n, *_, groups in rest:
        result[n], outs = outs[: len(groups)], outs[len(groups) :]
    return [result[n] for n in range(len(items))], list(after)


def inner_kernel(pieces, share, scale, act_at, other_at, place, *refs):
    acts, cots = refs[:pieces], refs[pieces : 2 * pieces]
    own, other, give, keep, rows, total, done = refs[2 * pieces :]
    copies = []
    for i in range(PAIR):
        for n, (weight, at) in enumerate(((own, place[i] * share), (other, other_at + i * share))):
            source = weight.at[pl.ds(pl.multiple_of(at, share), share), :]
            copies.append(pltpu.make_async_copy(source, rows.at[n, i], done.at[n, i]))
    for copy in copies:
        copy.start()
    left = jnp.concatenate([a[:, act_at : act_at + PAIR * share] for a in acts], axis=0)
    right = jnp.concatenate([g[...] for g in cots], axis=0)
    total[...] = lax.dot_general(left, right, (((0,), (0,)), ((), ())), preferred_element_type=f32)
    for copy in copies:
        copy.wait()
    x = place[PAIR]

    def inner_new(i):
        grad = total[pl.ds(pl.multiple_of(i * share, share), share), :]
        return (rows[0, i].astype(f32) + rows[1, i].astype(f32)) - scale * grad

    give[...] = inner_new(1 - x).astype(bf16)
    keep[...] = inner_new(x)


def inner_block(place, acts, act_at, cots, own, other, other_at, share):
    pieces = len(acts)
    tok, kv = cots[0].shape
    if act_at % LANES or PAIR * share % LANES:
        acts, act_at = [a[:, act_at : act_at + PAIR * share] for a in acts], 0
    return pl.pallas_call(
        functools.partial(inner_kernel, pieces, share, inner_rate / (tok * pieces // CORES), act_at, other_at),
        out_shape=[jax.ShapeDtypeStruct((share, kv), bf16), jax.ShapeDtypeStruct((share, kv), f32)],
        in_specs=[SMEM] + [VMEM] * (2 * pieces) + [HBM] * 2,
        out_specs=[VMEM] * 2,
        scratch_shapes=[
            pltpu.VMEM((CORES, PAIR, share, kv), bf16),
            pltpu.VMEM((PAIR * share, kv), f32),
            pltpu.SemaphoreType.DMA((CORES, PAIR)),
        ],
        compiler_params=pltpu.CompilerParams(vmem_limit_bytes=24 * MIB),
        cost_estimate=pl.CostEstimate(flops=pieces * tok * share * kv, bytes_accessed=share * kv, transcendentals=0),
    )(place, *acts, *cots, in_hbm(own), other)


def keys_kernel(acts_count, at, *refs):
    acts, (*blocks, out) = refs[:acts_count], refs[acts_count:]
    if at:
        *blocks, before = blocks
    weight = jnp.concatenate([w[...] for w in blocks], axis=0)
    left = jnp.concatenate([a[:, at : at + weight.shape[0]] for a in acts], axis=0)
    product = jnp.dot(left, weight, preferred_element_type=f32)
    out[...] = before[...] + product if at else product


def keys_part(acts, blocks, at, before=()):
    rows, kv = len(acts) * acts[0].shape[0], blocks[0].shape[1]
    depth = sum(w.shape[0] for w in blocks)
    if at % LANES:
        acts = [a[:, at:] for a in acts]
        return before[0] + keys_part(acts, blocks, 0)
    return pl.pallas_call(
        functools.partial(keys_kernel, len(acts), at),
        out_shape=jax.ShapeDtypeStruct((rows, kv), f32),
        in_specs=[VMEM] * (len(acts) + len(blocks) + len(before)),
        out_specs=VMEM,
        compiler_params=pltpu.CompilerParams(vmem_limit_bytes=24 * MIB),
        cost_estimate=pl.CostEstimate(flops=2 * rows * depth * kv, bytes_accessed=rows * kv, transcendentals=0),
    )(*acts, *blocks, *before)


def core_sum_kernel(fsdp, tok, keep, came, to_x, stay_x, stay_f, *to_f):
    half = keep.shape[1] // 2
    total = keep[...] + came[...]
    rows = fsdp * tok
    stay_x[...] = total[:rows, :half]
    to_x[...] = total[rows:, :half].astype(bf16)
    for i in range(PAIR):
        here = slice(i * tok, (i + 1) * tok)
        stay_f[here, :] = total[i * rows : i * rows + tok, half:]
        for s in range(1, fsdp):
            to_f[s - 1][here, :] = total[i * rows + s * tok : i * rows + (s + 1) * tok, half:].astype(bf16)


def second_sum_kernel(fsdp, tok, *refs):
    stay_x, stay_f, from_x, *from_f = refs[: fsdp + 2]
    left, right, to_x, *to_f = refs[fsdp + 2 :]
    first = stay_x[...] + from_x[...].astype(f32)
    left[...] = first[:tok]
    for s in range(1, fsdp):
        to_f[s - 1][...] = first[s * tok : (s + 1) * tok].astype(bf16)
    second = stay_f[...]
    for came in from_f:
        second = second + came[...].astype(f32)
    right[...] = second[:tok]
    to_x[...] = second[tok:].astype(bf16)


def last_sum_kernel(left, right, from_x, *refs):
    *from_f, keys = refs
    half = left.shape[1]
    first = left[...]
    for came in from_f:
        first = first + came[...].astype(f32)
    keys[:, :half] = first.astype(bf16)
    keys[:, half:] = (right[...] + from_x[...].astype(f32)).astype(bf16)


def small_call(kernel, shapes, *args):
    size = sum(shape.size for shape in shapes)
    return pl.pallas_call(
        kernel,
        out_shape=shapes,
        in_specs=[VMEM] * len(args),
        out_specs=[VMEM] * len(shapes),
        compiler_params=pltpu.CompilerParams(vmem_limit_bytes=24 * MIB),
        cost_estimate=pl.CostEstimate(flops=size, bytes_accessed=8 * size, transcendentals=0),
    )(*args)


def join_kernel(starts, *refs):
    *parts, out, done = refs
    copies = []
    for n, part in enumerate(parts):
        width = part.shape[1]
        here = out.at[:, pl.ds(pl.multiple_of(starts[n], width), width)]
        copies.append(pltpu.make_async_copy(part.at[: out.shape[0], :], here, done.at[n]))
    for copy in copies:
        copy.start()
    for copy in copies:
        copy.wait()


def join(parts, starts):
    rows, width = parts[-1].shape
    return pl.pallas_call(
        join_kernel,
        out_shape=jax.ShapeDtypeStruct((rows, width * len(parts)), parts[0].dtype),
        in_specs=[SMEM] + [VMEM] * len(parts),
        out_specs=HBM,
        scratch_shapes=[pltpu.SemaphoreType.DMA((len(parts),))],
        compiler_params=pltpu.CompilerParams(vmem_limit_bytes=16 * MIB),
        cost_estimate=pl.CostEstimate(flops=0, bytes_accessed=4 * rows * width * len(parts), transcendentals=0),
    )(jnp.stack(starts).astype(jnp.int32), *parts)


def local(activations, cotangent, inner_weight, outer_weight, outer_momentum, next_activations):
    fsdp, nz = lax.axis_size("fsdp"), lax.axis_size("z")
    f, z, x, c = (lax.axis_index(a) for a in ("fsdp", "z", "x", "core"))
    tok, d = activations.shape
    kv = cotangent.shape[1]
    width = d // fsdp
    block = width // nz
    share = block // (PAIR * CORES)
    own_weight = inner_weight[0]
    swap = ring(CORES, 1)

    def column(b, i, k, s):
        return ((f + s) % fsdp) * width + b * block + i * CORES * share + ((c + k) % CORES) * share

    def pair_ring(k, s):
        at = lambda i, j: (i % CORES) * fsdp + j % fsdp
        return [(at(i, j), at(i + k, j + s)) for i in range(CORES) for j in range(fsdp)]

    shifts = [(k, s) for s in range(fsdp) for k in range(CORES)]
    stages = [[nz - 1], list(range(nz - 2, -1, -1))]

    cots = {(0, 0): cotangent}
    for s in range(1, fsdp):
        cots[0, s] = lax.ppermute(cotangent, "fsdp", ring(fsdp, s))
    columns = [[column(z ^ m, i, k, s) for m in ms for i in range(PAIR)] for ms in stages for k, s in shifts]
    rows = [[((z ^ m) * PAIR * CORES + i * CORES + 1 - c) * share for m in ms for i in range(PAIR)] for ms in stages]
    (mine, weights), _ = pack([(activations, 1, share, columns), (own_weight, 0, share, rows)])
    acts = []
    for stage in range(len(stages)):
        came = []
        for (k, s), part in zip(shifts, mine[stage * len(shifts) :]):
            came.append(part if (k, s) == (0, 0) else lax.ppermute(part, ("core", "fsdp"), pair_ring(k, s)))
        acts.append(came)
    other = [lax.ppermute(weight, "core", swap) for weight in weights]
    cots[1, 0] = lax.ppermute(cotangent, "core", swap)
    for s in range(1, fsdp):
        cots[1, s] = lax.ppermute(cots[0, s], "core", swap)

    far = [(i, k, s) for k in range(CORES) for i in range(PAIR) for s in range(fsdp)]
    index = lambda i, k, s: ((i % PAIR) * CORES + k % CORES) * fsdp + s % fsdp
    every = [(i, k, s) for i in range(PAIR) for k in range(CORES) for s in range(fsdp)]
    groups = [[column(z ^ m, (x + i) % PAIR, k, s) for m in range(nz)] for i, k, s in far]
    (mine,), _ = pack([(next_activations, 1, share, groups)])
    mine = dict(zip(far, mine))
    nexts = {}

    def send_next(i, k, s):
        pairs = [(index(*e), index(e[0] + i, e[1] + k, e[2] + s)) for e in every]
        nexts[i, k, s] = lax.ppermute(mine[i, k, s], ("x", "core", "fsdp"), pairs) if i or k or s else mine[i, k, s]

    near, away = [e for e in far if e[0] == 0], [e for e in far if e[0]]
    for e in near:
        send_next(*e)

    total = {}
    given = None
    for stage, ms in enumerate(stages):
        for n, m in enumerate(ms):
            place = jnp.stack([((z ^ m) * PAIR + i) * CORES + c for i in range(PAIR)] + [x]).astype(jnp.int32)
            at = n * PAIR * share
            ordered = [cots[k, s] for k, s in shifts]
            if m == 0:
                place, *came = lax.optimization_barrier((place, *[nexts[e] for e in near]))
                nexts.update(zip(near, came))
            if given is not None:
                place, _ = lax.optimization_barrier((place, given))
            given, keep = inner_block(place, acts[stage], at, ordered, own_weight, other[stage], at, share)
            held = keep + lax.ppermute(given, "x", ring(PAIR, 1)).astype(f32)
            total[m] = held if m not in total else held + total[m]
            if m:
                low = m & -m
                came = lax.ppermute(total[m].astype(bf16), "z", [(i, i ^ low) for i in range(nz)]).astype(f32)
                total[m ^ low] = came if m ^ low not in total else total[m ^ low] + came
    summed = total[0]

    given, *island_cots = lax.optimization_barrier((given, *[cots[0, s] for s in range(fsdp)]))
    grad_rows = lax.dot_general(
        jnp.concatenate(island_cots, axis=0), own_weight, (((1,), (1,)), ((), ())), preferred_element_type=f32
    ).astype(bf16)
    parts = [grad_rows]
    for s in range(1, fsdp):
        parts.append(lax.ppermute(grad_rows[s * tok : (s + 1) * tok], "fsdp", ring(fsdp, -s)))

    summed, *held = lax.optimization_barrier((summed, *[mine[e] for e in away]))
    mine.update(zip(away, held))

    pseudo_grad = outer_weight - summed / (nz * PAIR * CORES)
    new_momentum = nesterov * outer_momentum + pseudo_grad
    new_outer = outer_weight - outer_rate * (pseudo_grad + nesterov * new_momentum)

    rows = [new_outer.astype(bf16)]
    for m in range(1, nz):
        low = m & -m
        source = rows[m ^ low]
        if m == nz - 1:
            for e in away:
                send_next(*e)
            held = [source, *rows[1:], *[nexts[e] for e in away]]
            source, *held = lax.optimization_barrier(held)
            rows[1:], held = held[: m - 1], held[m - 1 :]
            nexts.update(zip(away, held))
            source, *parts = lax.optimization_barrier((source, *parts))
            input_grad = join(parts, [((f + s) % fsdp) * width for s in range(fsdp)])
        rows.append(lax.ppermute(source, "z", [(i, i ^ low) for i in range(nz)]))

    half = len(far) // CORES
    near, away = [nexts[e] for e in far[:half]], [nexts[e] for e in far[half:]]
    give, keep = keys_part(away, rows[:-1], 0), keys_part(near, rows[:-1], 0)
    give, keep, input_grad = lax.optimization_barrier((give, keep, input_grad))
    last = (nz - 1) * share
    give = keys_part(away, rows[-1:], last, [give])
    keep = keys_part(near, rows[-1:], last, [keep])
    came = lax.ppermute(give, "core", swap)
    shape = lambda n, kind: jax.ShapeDtypeStruct((n, kv // 2), kind)
    to_x, stay_x, stay_f, *to_f = small_call(
        functools.partial(core_sum_kernel, fsdp, tok),
        [shape(fsdp * tok, bf16), shape(fsdp * tok, f32), shape(PAIR * tok, f32)] + [shape(PAIR * tok, bf16)] * (fsdp - 1),
        keep,
        came,
    )

    def home(to_x, to_f):
        from_x = lax.ppermute(to_x, "x", ring(PAIR, 1))
        return [from_x] + [lax.ppermute(part, "fsdp", ring(fsdp, -s - 1)) for s, part in enumerate(to_f)]

    left, right, to_x, *to_f = small_call(
        functools.partial(second_sum_kernel, fsdp, tok),
        [shape(tok, f32)] * 2 + [shape(tok, bf16)] * fsdp,
        stay_x,
        stay_f,
        *home(to_x, to_f),
    )
    (keys,) = small_call(
        last_sum_kernel, [jax.ShapeDtypeStruct((tok, kv), bf16)], left, right, *home(to_x, to_f)
    )
    return (input_grad, keys, new_outer, new_momentum)


def solution(mesh):
    fsdp = mesh.shape["fsdp"]
    nz = mesh.shape["island"] // (PAIR * CORES)
    split = Mesh(mesh.devices.reshape(nz, PAIR, CORES, fsdp), ("z", "x", "core", "fsdp"))
    island = ("z", "x", "core")
    tokens = P(island + ("fsdp",), None)
    width = P(("fsdp",) + island, None)
    in_specs = (tokens, tokens, P(island, "fsdp", None), width, width, tokens)
    out_specs = (tokens, tokens, width, width)
    return jax.shard_map(local, mesh=split, in_specs=in_specs, out_specs=out_specs, check_vma=False)
```

```python
import functools

import jax
import jax.numpy as jnp
from jax import lax
from jax.experimental import pallas as pl
from jax.experimental.pallas import tpu as pltpu
from jax.sharding import Mesh, PartitionSpec as P

inner_rate = 1.2
outer_rate = 0.7
nesterov = 0.9
CORES = 2
PAIR = 2
LANES = 128

bf16, f32 = jnp.bfloat16, jnp.float32
VMEM, HBM = pl.BlockSpec(memory_space=pltpu.VMEM), pl.BlockSpec(memory_space=pltpu.HBM)
SMEM, ANY = pl.BlockSpec(memory_space=pltpu.SMEM), pl.BlockSpec(memory_space=pl.ANY)
MIB = 1024 * 1024


def ring(count, shift):
    return [(i, (i + shift) % count) for i in range(count)]


def strip(axis, start, size):
    return (pl.ds(start, size), slice(None)) if axis == 0 else (slice(None), pl.ds(start, size))


def in_hbm(array):
    return pltpu.with_memory_space_constraint(array, pltpu.HBM)


def pack_kernel(plan, starts, *refs):
    sources, outs, done = refs[: len(plan)], refs[len(plan) : -1], refs[-1]
    copies, o = [], 0
    for source, (axis, size, counts) in zip(sources, plan):
        for count in counts:
            for i in range(count):
                n = len(copies)
                part = source.at[strip(axis, pl.multiple_of(starts[n], size), size)]
                copies.append(pltpu.make_async_copy(part, outs[o].at[strip(axis, i * size, size)], done.at[n]))
            o += 1
    for copy in copies:
        copy.start()
    for copy in copies:
        copy.wait()


def pack(items, after=()):
    result, rest = {}, []
    for n, (array, axis, size, groups) in enumerate(items):
        if axis == 1 and size % LANES:
            strips = [[lax.dynamic_slice_in_dim(array, at, size, axis=axis) for at in group] for group in groups]
            result[n] = [jnp.concatenate(group, axis=axis) for group in strips]
        else:
            rest.append((n, array, axis, size, groups))
    if not rest:
        return [result[n] for n in range(len(items))], list(after)
    starts = jnp.stack([at for item in rest for group in item[4] for at in group]).astype(jnp.int32)
    if after:
        starts, *after = lax.optimization_barrier((starts, *after))
    plan, shapes = [], []
    for _, array, axis, size, groups in rest:
        counts = [len(group) for group in groups]
        plan.append((axis, size, counts))
        for n in counts:
            shape = (n * size, array.shape[1]) if axis == 0 else (array.shape[0], n * size)
            shapes.append(jax.ShapeDtypeStruct(shape, array.dtype))
    moved = sum(4 * shape.size for shape in shapes)
    outs = pl.pallas_call(
        functools.partial(pack_kernel, plan),
        out_shape=shapes,
        in_specs=[SMEM] + [HBM] * len(rest),
        out_specs=[pl.BlockSpec()] * len(shapes),
        scratch_shapes=[pltpu.SemaphoreType.DMA((starts.shape[0],))],
        compiler_params=pltpu.CompilerParams(vmem_limit_bytes=16 * MIB),
        cost_estimate=pl.CostEstimate(flops=0, bytes_accessed=moved, transcendentals=0),
    )(starts, *[in_hbm(item[1]) for item in rest])
    for n, *_, groups in rest:
        result[n], outs = outs[: len(groups)], outs[len(groups) :]
    return [result[n] for n in range(len(items))], list(after)


def inner_kernel(pieces, share, scale, act_at, place, *refs):
    acts, cots = refs[:pieces], refs[pieces : 2 * pieces]
    own, other, give, keep, left, right, rows, total, done = refs[2 * pieces :]
    tok = cots[0].shape[0]
    copies = []

    def fetch(source, target):
        copies.append(pltpu.make_async_copy(source, target, done.at[len(copies)]))

    for n, (act, cot) in enumerate(zip(acts, cots)):
        here = pl.ds(n * tok, tok)
        fetch(act.at[:, pl.ds(act_at, PAIR * share)], left.at[here, :])
        fetch(cot, right.at[here, :])
    for i in range(PAIR):
        strip = pl.ds(pl.multiple_of(place[i] * share, share), share)
        fetch(own.at[strip, :], rows.at[0, i])
        fetch(other.at[strip, :], rows.at[1, i])
    for copy in copies:
        copy.start()
    for copy in copies[: 2 * pieces]:
        copy.wait()
    total[...] = lax.dot_general(left[...], right[...], (((0,), (0,)), ((), ())), preferred_element_type=f32)
    for copy in copies[2 * pieces :]:
        copy.wait()
    x = place[PAIR]

    def inner_new(i):
        grad = total[pl.ds(pl.multiple_of(i * share, share), share), :]
        return (rows[0, i].astype(f32) + rows[1, i].astype(f32)) - scale * grad

    give[...] = inner_new(1 - x).astype(bf16)
    keep[...] = inner_new(x)


def inner_block(place, acts, act_at, cots, own, other, share):
    pieces = len(acts)
    tok, kv = cots[0].shape
    if act_at % LANES or PAIR * share % LANES:
        acts, act_at = [a[:, act_at : act_at + PAIR * share] for a in acts], 0
    return pl.pallas_call(
        functools.partial(inner_kernel, pieces, share, inner_rate / (tok * pieces // CORES), act_at),
        out_shape=[jax.ShapeDtypeStruct((share, kv), bf16), jax.ShapeDtypeStruct((share, kv), f32)],
        in_specs=[SMEM] + [ANY] * (2 * pieces) + [HBM, ANY],
        out_specs=[pl.BlockSpec()] * 2,
        scratch_shapes=[
            pltpu.VMEM((pieces * tok, PAIR * share), bf16),
            pltpu.VMEM((pieces * tok, kv), bf16),
            pltpu.VMEM((CORES, PAIR, share, kv), bf16),
            pltpu.VMEM((PAIR * share, kv), f32),
            pltpu.SemaphoreType.DMA((2 * pieces + CORES * PAIR,)),
        ],
        compiler_params=pltpu.CompilerParams(vmem_limit_bytes=32 * MIB),
        cost_estimate=pl.CostEstimate(flops=pieces * tok * share * kv, bytes_accessed=share * kv, transcendentals=0),
    )(place, *acts, *cots, in_hbm(own), other)


def keys_kernel(acts_count, at, *refs):
    acts, (*blocks, out) = refs[:acts_count], refs[acts_count:]
    if at:
        *blocks, before = blocks
    weight = jnp.concatenate([w[...] for w in blocks], axis=0)
    left = jnp.concatenate([a[:, at : at + weight.shape[0]] for a in acts], axis=0)
    product = jnp.dot(left, weight, preferred_element_type=f32)
    out[...] = before[...] + product if at else product


def keys_part(acts, blocks, at, before=()):
    rows, kv = len(acts) * acts[0].shape[0], blocks[0].shape[1]
    depth = sum(w.shape[0] for w in blocks)
    if at % LANES:
        acts = [a[:, at:] for a in acts]
        return before[0] + keys_part(acts, blocks, 0)
    return pl.pallas_call(
        functools.partial(keys_kernel, len(acts), at),
        out_shape=jax.ShapeDtypeStruct((rows, kv), f32),
        in_specs=[pl.BlockSpec()] * (len(acts) + len(blocks) + len(before)),
        out_specs=pl.BlockSpec(),
        compiler_params=pltpu.CompilerParams(vmem_limit_bytes=24 * MIB),
        cost_estimate=pl.CostEstimate(flops=2 * rows * depth * kv, bytes_accessed=rows * kv, transcendentals=0),
    )(*acts, *blocks, *before)


def core_sum_kernel(fsdp, tok, keep, came, to_x, stay_x, stay_f, *to_f):
    half = keep.shape[1] // 2
    total = keep[...] + came[...]
    rows = fsdp * tok
    stay_x[...] = total[:rows, :half]
    to_x[...] = total[rows:, :half].astype(bf16)
    for i in range(PAIR):
        here = slice(i * tok, (i + 1) * tok)
        stay_f[here, :] = total[i * rows : i * rows + tok, half:]
        for s in range(1, fsdp):
            to_f[s - 1][here, :] = total[i * rows + s * tok : i * rows + (s + 1) * tok, half:].astype(bf16)


def second_sum_kernel(fsdp, tok, *refs):
    stay_x, stay_f, from_x, *from_f = refs[: fsdp + 2]
    left, right, to_x, *to_f = refs[fsdp + 2 :]
    first = stay_x[...] + from_x[...].astype(f32)
    left[...] = first[:tok]
    for s in range(1, fsdp):
        to_f[s - 1][...] = first[s * tok : (s + 1) * tok].astype(bf16)
    second = stay_f[...]
    for came in from_f:
        second = second + came[...].astype(f32)
    right[...] = second[:tok]
    to_x[...] = second[tok:].astype(bf16)


def last_sum_kernel(left, right, from_x, *refs):
    *from_f, keys = refs
    half = left.shape[1]
    first = left[...]
    for came in from_f:
        first = first + came[...].astype(f32)
    keys[:, :half] = first.astype(bf16)
    keys[:, half:] = (right[...] + from_x[...].astype(f32)).astype(bf16)


def small_call(kernel, shapes, *args):
    size = sum(shape.size for shape in shapes)
    return pl.pallas_call(
        kernel,
        out_shape=shapes,
        in_specs=[VMEM] * len(args),
        out_specs=[VMEM] * len(shapes),
        compiler_params=pltpu.CompilerParams(vmem_limit_bytes=24 * MIB),
        cost_estimate=pl.CostEstimate(flops=size, bytes_accessed=8 * size, transcendentals=0),
    )(*args)


def join_kernel(starts, *refs):
    *parts, out, done = refs
    copies = []
    for n, part in enumerate(parts):
        width = part.shape[1]
        here = out.at[:, pl.ds(pl.multiple_of(starts[n], width), width)]
        copies.append(pltpu.make_async_copy(part.at[: out.shape[0], :], here, done.at[n]))
    for copy in copies:
        copy.start()
    for copy in copies:
        copy.wait()


def join(parts, starts):
    rows, width = parts[-1].shape
    return pl.pallas_call(
        join_kernel,
        out_shape=jax.ShapeDtypeStruct((rows, width * len(parts)), parts[0].dtype),
        in_specs=[SMEM] + [VMEM] * len(parts),
        out_specs=HBM,
        scratch_shapes=[pltpu.SemaphoreType.DMA((len(parts),))],
        compiler_params=pltpu.CompilerParams(vmem_limit_bytes=16 * MIB),
        cost_estimate=pl.CostEstimate(flops=0, bytes_accessed=4 * rows * width * len(parts), transcendentals=0),
    )(jnp.stack(starts).astype(jnp.int32), *parts)


def local(activations, cotangent, inner_weight, outer_weight, outer_momentum, next_activations):
    fsdp, nz = lax.axis_size("fsdp"), lax.axis_size("z")
    f, z, x, c = (lax.axis_index(a) for a in ("fsdp", "z", "x", "core"))
    tok, d = activations.shape
    kv = cotangent.shape[1]
    width = d // fsdp
    block = width // nz
    share = block // (PAIR * CORES)
    own_weight = inner_weight[0]
    swap = ring(CORES, 1)

    def column(b, i, k, s):
        return ((f + s) % fsdp) * width + b * block + i * CORES * share + ((c + k) % CORES) * share

    def pair_ring(k, s):
        at = lambda i, j: (i % CORES) * fsdp + j % fsdp
        return [(at(i, j), at(i + k, j + s)) for i in range(CORES) for j in range(fsdp)]

    shifts = [(k, s) for s in range(fsdp) for k in range(CORES)]
    order = list(range(nz - 1, -1, -1))
    stages = [order[: nz // 2], order[nz // 2 :]]

    cots = {(0, 0): cotangent}
    for s in range(1, fsdp):
        cots[0, s] = lax.ppermute(cotangent, "fsdp", ring(fsdp, s))
    columns = [[column(z ^ m, i, k, s) for m in ms for i in range(PAIR)] for ms in stages for k, s in shifts]
    (mine,), _ = pack([(activations, 1, share, columns)])
    acts = []
    for stage in range(len(stages)):
        came = []
        for (k, s), part in zip(shifts, mine[stage * len(shifts) :]):
            came.append(part if (k, s) == (0, 0) else lax.ppermute(part, ("core", "fsdp"), pair_ring(k, s)))
        acts.append(came)
    other_weight = lax.ppermute(own_weight, "core", swap)
    cots[1, 0] = lax.ppermute(cotangent, "core", swap)
    for s in range(1, fsdp):
        cots[1, s] = lax.ppermute(cots[0, s], "core", swap)

    far = [(i, k, s) for k in range(CORES) for i in range(PAIR) for s in range(fsdp)]
    index = lambda i, k, s: ((i % PAIR) * CORES + k % CORES) * fsdp + s % fsdp
    every = [(i, k, s) for i in range(PAIR) for k in range(CORES) for s in range(fsdp)]
    groups = [[column(z ^ m, (x + i) % PAIR, k, s) for m in range(nz)] for i, k, s in far]
    mine, nexts = {}, {}

    def send_next(i, k, s):
        pairs = [(index(*e), index(e[0] + i, e[1] + k, e[2] + s)) for e in every]
        nexts[i, k, s] = lax.ppermute(mine[i, k, s], ("x", "core", "fsdp"), pairs) if i or k or s else mine[i, k, s]

    near, away = [e for e in far if e[0] == 0], [e for e in far if e[0]]

    gives, keeps = {}, {}
    for stage, ms in enumerate(stages):
        for n, m in enumerate(ms):
            place = jnp.stack([((z ^ m) * PAIR + i) * CORES + c for i in range(PAIR)] + [x]).astype(jnp.int32)
            at = n * PAIR * share
            ordered = [cots[k, s] for k, s in shifts]
            if stage and n == 0:
                (parts,), (gives[m + 1],) = pack([(next_activations, 1, share, groups)], [gives[m + 1]])
                mine.update(zip(far, parts))
                for e in near:
                    send_next(*e)
            if m == 0:
                place, *came = lax.optimization_barrier((place, *[nexts[e] for e in near]))
                nexts.update(zip(near, came))
            if n:
                place, gives[m + 1] = lax.optimization_barrier((place, gives[m + 1]))
            gives[m], keeps[m] = inner_block(place, acts[stage], at, ordered, own_weight, other_weight, share)
    keeps[0], *island_cots = lax.optimization_barrier((keeps[0], *[cots[0, s] for s in range(fsdp)]))
    grad_rows = lax.dot_general(
        jnp.concatenate(island_cots, axis=0), own_weight, (((1,), (1,)), ((), ())), preferred_element_type=f32
    ).astype(bf16)
    parts = [grad_rows]
    for s in range(1, fsdp):
        parts.append(lax.ppermute(grad_rows[s * tok : (s + 1) * tok], "fsdp", ring(fsdp, -s)))

    total, over_x, over_z = {}, {}, {}
    for m in order:
        earlier = over_z if m % 2 else over_x
        if m + 2 in earlier:
            gives[m], earlier[m + 2] = lax.optimization_barrier((gives[m], earlier[m + 2]))
        over_x[m] = lax.ppermute(gives[m], "x", ring(PAIR, 1))
        if m % 2:
            keeps[m], gives[m - 1] = lax.optimization_barrier((keeps[m], gives[m - 1]))
            over_z[m] = lax.ppermute((keeps[m] + over_x[m].astype(f32)).astype(bf16), "z", [(i, i ^ 1) for i in range(nz)])
    for m in order:
        held = keeps[m] + over_x[m].astype(f32)
        total[m] = held if m not in total else held + total[m]
        if m:
            low = m & -m
            if m not in over_z:
                over_z[m] = lax.ppermute(total[m].astype(bf16), "z", [(i, i ^ low) for i in range(nz)])
            came = over_z[m].astype(f32)
            total[m ^ low] = came if m ^ low not in total else total[m ^ low] + came
    summed = total[0]

    summed, *held = lax.optimization_barrier((summed, *[mine[e] for e in away]))
    mine.update(zip(away, held))

    pseudo_grad = outer_weight - summed / (nz * PAIR * CORES)
    new_momentum = nesterov * outer_momentum + pseudo_grad
    new_outer = outer_weight - outer_rate * (pseudo_grad + nesterov * new_momentum)

    rows = [new_outer.astype(bf16)]
    for m in range(1, nz):
        low = m & -m
        source = rows[m ^ low]
        if m == nz - 1:
            for e in away:
                send_next(*e)
            held = [source, *rows[1:], *[nexts[e] for e in away]]
            source, *held = lax.optimization_barrier(held)
            rows[1:], held = held[: m - 1], held[m - 1 :]
            nexts.update(zip(away, held))
            source, *parts = lax.optimization_barrier((source, *parts))
            input_grad = join(parts, [((f + s) % fsdp) * width for s in range(fsdp)])
        rows.append(lax.ppermute(source, "z", [(i, i ^ low) for i in range(nz)]))

    half = len(far) // CORES
    near, away = [nexts[e] for e in far[:half]], [nexts[e] for e in far[half:]]
    give, keep = keys_part(away, rows[:-1], 0), keys_part(near, rows[:-1], 0)
    give, keep, input_grad = lax.optimization_barrier((give, keep, input_grad))
    last = (nz - 1) * share
    give = keys_part(away, rows[-1:], last, [give])
    keep = keys_part(near, rows[-1:], last, [keep])
    came = lax.ppermute(give, "core", swap)
    shape = lambda n, kind: jax.ShapeDtypeStruct((n, kv // 2), kind)
    to_x, stay_x, stay_f, *to_f = small_call(
        functools.partial(core_sum_kernel, fsdp, tok),
        [shape(fsdp * tok, bf16), shape(fsdp * tok, f32), shape(PAIR * tok, f32)] + [shape(PAIR * tok, bf16)] * (fsdp - 1),
        keep,
        came,
    )

    def home(to_x, to_f):
        from_x = lax.ppermute(to_x, "x", ring(PAIR, 1))
        return [from_x] + [lax.ppermute(part, "fsdp", ring(fsdp, -s - 1)) for s, part in enumerate(to_f)]

    left, right, to_x, *to_f = small_call(
        functools.partial(second_sum_kernel, fsdp, tok),
        [shape(tok, f32)] * 2 + [shape(tok, bf16)] * fsdp,
        stay_x,
        stay_f,
        *home(to_x, to_f),
    )
    (keys,) = small_call(
        last_sum_kernel, [jax.ShapeDtypeStruct((tok, kv), bf16)], left, right, *home(to_x, to_f)
    )
    return (input_grad, keys, new_outer, new_momentum)


def solution(mesh):
    fsdp = mesh.shape["fsdp"]
    nz = mesh.shape["island"] // (PAIR * CORES)
    split = Mesh(mesh.devices.reshape(nz, PAIR, CORES, fsdp), ("z", "x", "core", "fsdp"))
    island = ("z", "x", "core")
    tokens = P(island + ("fsdp",), None)
    width = P(("fsdp",) + island, None)
    in_specs = (tokens, tokens, P(island, "fsdp", None), width, width, tokens)
    out_specs = (tokens, tokens, width, width)
    return jax.shard_map(local, mesh=split, in_specs=in_specs, out_specs=out_specs, check_vma=False)
```

```python
import functools

import jax
import jax.numpy as jnp
from jax import lax
from jax.experimental import pallas as pl
from jax.experimental.pallas import tpu as pltpu
from jax.sharding import Mesh, PartitionSpec as P

inner_rate = 1.2
outer_rate = 0.7
nesterov = 0.9
CORES = 2
PAIR = 2
LANES = 128

bf16, f32 = jnp.bfloat16, jnp.float32
VMEM, HBM = pl.BlockSpec(memory_space=pltpu.VMEM), pl.BlockSpec(memory_space=pltpu.HBM)
SMEM, ANY = pl.BlockSpec(memory_space=pltpu.SMEM), pl.BlockSpec(memory_space=pl.ANY)
MIB = 1024 * 1024


def ring(count, shift):
    return [(i, (i + shift) % count) for i in range(count)]


def strip(axis, start, size):
    return (pl.ds(start, size), slice(None)) if axis == 0 else (slice(None), pl.ds(start, size))


def in_hbm(array):
    return pltpu.with_memory_space_constraint(array, pltpu.HBM)


def pack_kernel(plan, starts, *refs):
    sources, outs, done = refs[: len(plan)], refs[len(plan) : -1], refs[-1]
    copies, o = [], 0
    for source, (axis, size, counts) in zip(sources, plan):
        for count in counts:
            for i in range(count):
                n = len(copies)
                part = source.at[strip(axis, pl.multiple_of(starts[n], size), size)]
                copies.append(pltpu.make_async_copy(part, outs[o].at[strip(axis, i * size, size)], done.at[n]))
            o += 1
    for copy in copies:
        copy.start()
    for copy in copies:
        copy.wait()


def pack(items, after=(), target=jax.ShapeDtypeStruct):
    result, rest = {}, []
    for n, (array, axis, size, groups) in enumerate(items):
        if axis == 1 and size % LANES:
            strips = [[lax.dynamic_slice_in_dim(array, at, size, axis=axis) for at in group] for group in groups]
            result[n] = [jnp.concatenate(group, axis=axis) for group in strips]
        else:
            rest.append((n, array, axis, size, groups))
    if not rest:
        return [result[n] for n in range(len(items))], list(after)
    starts = jnp.stack([at for item in rest for group in item[4] for at in group]).astype(jnp.int32)
    if after:
        starts, *after = lax.optimization_barrier((starts, *after))
    plan, shapes = [], []
    for _, array, axis, size, groups in rest:
        counts = [len(group) for group in groups]
        plan.append((axis, size, counts))
        for n in counts:
            shape = (n * size, array.shape[1]) if axis == 0 else (array.shape[0], n * size)
            shapes.append(target(shape, array.dtype))
    moved = 4 * starts.shape[0] * 1024 * LANES
    outs = pl.pallas_call(
        functools.partial(pack_kernel, plan),
        out_shape=shapes,
        in_specs=[SMEM] + [HBM] * len(rest),
        out_specs=[pl.BlockSpec()] * len(shapes),
        scratch_shapes=[pltpu.SemaphoreType.DMA((starts.shape[0],))],
        compiler_params=pltpu.CompilerParams(vmem_limit_bytes=16 * MIB),
        cost_estimate=pl.CostEstimate(flops=0, bytes_accessed=moved, transcendentals=0),
    )(starts, *[in_hbm(item[1]) for item in rest])
    for n, *_, groups in rest:
        result[n], outs = outs[: len(groups)], outs[len(groups) :]
    return [result[n] for n in range(len(items))], list(after)


def inner_kernel(pieces, share, scale, act_at, place, *refs):
    acts, cots = refs[:pieces], refs[pieces : 2 * pieces]
    own, other, to_x, stay_x, to_z, stay_z, left, right, rows, total, done = refs[2 * pieces :]
    tok, kv = cots[0].shape
    strips = 2 * PAIR
    copies = []

    def fetch(source, target):
        copies.append(pltpu.make_async_copy(source, target, done.at[len(copies)]))

    for n, (act, cot) in enumerate(zip(acts, cots)):
        here = pl.ds(n * tok, tok)
        fetch(act.at[:, pl.ds(act_at, strips * share)], left.at[here, :])
        fetch(cot, right.at[here, :])
    for i in range(strips):
        strip_rows = pl.ds(pl.multiple_of(place[i] * share, share), share)
        here = pl.ds(i * share, share)
        fetch(own.at[strip_rows, :], rows.at[0, here, :])
        fetch(other.at[strip_rows, :], rows.at[1, here, :])
    for copy in copies:
        copy.start()
    for copy in copies[: 2 * pieces]:
        copy.wait()
    total[...] = lax.dot_general(left[...], right[...], (((0,), (0,)), ((), ())), preferred_element_type=f32)
    for copy in copies[2 * pieces :]:
        copy.wait()

    def inner_new(i, columns):
        here = slice(i * share, (i + 1) * share)
        return (rows[0, here, columns].astype(f32) + rows[1, here, columns].astype(f32)) - scale * total[here, columns]

    first, second = slice(0, kv // 2), slice(kv // 2, kv)
    for n in range(2):
        here = slice(n * share, (n + 1) * share)
        to_x[here, :] = inner_new(PAIR * n + 1, first).astype(bf16)
        to_z[here, :] = inner_new(n, second).astype(bf16)
    for n in range(2):
        here = slice(n * share, (n + 1) * share)
        stay_x[here, :] = inner_new(PAIR * n, first)
        stay_z[here, :] = inner_new(PAIR + n, second)


def inner_blocks(place, acts, act_at, cots, own, other, share):
    pieces = len(acts)
    tok, kv = cots[0].shape
    rows = 2 * PAIR * share
    if act_at % LANES or rows % LANES:
        acts, act_at = [a[:, act_at : act_at + rows] for a in acts], 0
    sent, kept = (jax.ShapeDtypeStruct((2 * share, kv // 2), kind) for kind in (bf16, f32))
    return pl.pallas_call(
        functools.partial(inner_kernel, pieces, share, inner_rate / (tok * pieces // CORES), act_at),
        out_shape=[sent, kept, sent, kept],
        in_specs=[SMEM] + [ANY] * (2 * pieces) + [HBM, ANY],
        out_specs=[pl.BlockSpec()] * 4,
        scratch_shapes=[
            pltpu.VMEM((pieces * tok, rows), bf16),
            pltpu.VMEM((pieces * tok, kv), bf16),
            pltpu.VMEM((CORES, rows, kv), bf16),
            pltpu.VMEM((rows, kv), f32),
            pltpu.SemaphoreType.DMA((2 * pieces + 2 * CORES * PAIR,)),
        ],
        compiler_params=pltpu.CompilerParams(vmem_limit_bytes=32 * MIB),
        cost_estimate=pl.CostEstimate(flops=pieces * tok * share * kv, bytes_accessed=share * kv, transcendentals=0),
    )(place, *acts, *cots, in_hbm(own), other)


def middle_kernel(share, stay_x, from_x, stay_z, from_z, to_z, keep_left, to_x, keep_right):
    over_x = stay_x[...] + from_x[...].astype(f32)
    over_z = stay_z[...] + from_z[...].astype(f32)
    to_z[...] = over_x[:share].astype(bf16)
    to_x[...] = over_z[share:].astype(bf16)
    keep_left[...] = over_x[share:]
    keep_right[...] = over_z[:share]


def block_sum(keep_left, from_z, keep_right, from_x, came):
    left = keep_left[...] + from_z[...].astype(f32)
    right = keep_right[...] + from_x[...].astype(f32)
    total = jnp.concatenate([left, right], axis=1)
    for other in came:
        total = total + other[...].astype(f32)
    return total


def gather_kernel(keep_left, keep_right, *refs):
    *came, left, right = refs
    total = jnp.concatenate([keep_left[...], keep_right[...]], axis=1)
    for other in came:
        total = total + other[...].astype(f32)
    left[...] = total[:, : left.shape[1]]
    right[...] = total[:, left.shape[1] :]


def block_kernel(*refs):
    *inputs, out = refs
    out[...] = block_sum(*inputs[:4], inputs[4:]).astype(bf16)


def update_kernel(replicas, *refs):
    *inputs, weight, momentum, share, new_outer, new_momentum = refs
    summed = block_sum(*inputs[:4], inputs[4:])
    pseudo_grad = weight[...] - summed / replicas
    moment = nesterov * momentum[...] + pseudo_grad
    outer = weight[...] - outer_rate * (pseudo_grad + nesterov * moment)
    share[...] = outer.astype(bf16)
    new_outer[...] = outer
    new_momentum[...] = moment


def keys_kernel(acts_count, counts, at, *refs):
    acts, (*pieces, out) = refs[:acts_count], refs[acts_count:]
    if at:
        *pieces, before = pieces
    blocks = []
    for count in counts:
        blocks.append(jnp.concatenate([w[...] for w in pieces[:count]], axis=1))
        pieces = pieces[count:]
    weight = jnp.concatenate(blocks, axis=0)
    left = jnp.concatenate([a[:, at : at + weight.shape[0]] for a in acts], axis=0)
    product = jnp.dot(left, weight, preferred_element_type=f32)
    out[...] = before[...] + product if at else product


def keys_part(acts, blocks, at, before=()):
    rows, kv = len(acts) * acts[0].shape[0], sum(w.shape[1] for w in blocks[0])
    depth = sum(block[0].shape[0] for block in blocks)
    if at % LANES:
        acts = [a[:, at:] for a in acts]
        return before[0] + keys_part(acts, blocks, 0)
    pieces = [w for block in blocks for w in block]
    return pl.pallas_call(
        functools.partial(keys_kernel, len(acts), [len(block) for block in blocks], at),
        out_shape=jax.ShapeDtypeStruct((rows, kv), f32),
        in_specs=[pl.BlockSpec()] * (len(acts) + len(pieces) + len(before)),
        out_specs=pl.BlockSpec(),
        compiler_params=pltpu.CompilerParams(vmem_limit_bytes=24 * MIB),
        cost_estimate=pl.CostEstimate(flops=2 * rows * depth * kv, bytes_accessed=rows * kv, transcendentals=0),
    )(*acts, *pieces, *before)


def core_sum_kernel(fsdp, tok, keep, came, to_x, stay_x, stay_f, *to_f):
    half = keep.shape[1] // 2
    total = keep[...] + came[...]
    rows = fsdp * tok
    stay_x[...] = total[:rows, :half]
    to_x[...] = total[rows:, :half].astype(bf16)
    for i in range(PAIR):
        here = slice(i * tok, (i + 1) * tok)
        stay_f[here, :] = total[i * rows : i * rows + tok, half:]
        for s in range(1, fsdp):
            to_f[s - 1][here, :] = total[i * rows + s * tok : i * rows + (s + 1) * tok, half:].astype(bf16)


def second_sum_kernel(fsdp, tok, *refs):
    stay_x, stay_f, from_x, *from_f = refs[: fsdp + 2]
    left, right, to_x, *to_f = refs[fsdp + 2 :]
    first = stay_x[...] + from_x[...].astype(f32)
    left[...] = first[:tok]
    for s in range(1, fsdp):
        to_f[s - 1][...] = first[s * tok : (s + 1) * tok].astype(bf16)
    second = stay_f[...]
    for came in from_f:
        second = second + came[...].astype(f32)
    right[...] = second[:tok]
    to_x[...] = second[tok:].astype(bf16)


def last_sum_kernel(left, right, from_x, *refs):
    *from_f, keys = refs
    half = left.shape[1]
    first = left[...]
    for came in from_f:
        first = first + came[...].astype(f32)
    keys[:, :half] = first.astype(bf16)
    keys[:, half:] = (right[...] + from_x[...].astype(f32)).astype(bf16)


def small_call(kernel, shapes, *args, spec=VMEM, weight=1):
    size = weight * sum(shape.size for shape in shapes)
    return pl.pallas_call(
        kernel,
        out_shape=shapes,
        in_specs=[spec] * len(args),
        out_specs=[spec] * len(shapes),
        compiler_params=pltpu.CompilerParams(vmem_limit_bytes=24 * MIB),
        cost_estimate=pl.CostEstimate(flops=size // 8, bytes_accessed=size // 8, transcendentals=0),
    )(*args)


def join_kernel(starts, *refs):
    *parts, out, done = refs
    copies = []
    for n, part in enumerate(parts):
        width = part.shape[1]
        here = out.at[:, pl.ds(pl.multiple_of(starts[n], width), width)]
        copies.append(pltpu.make_async_copy(part.at[: out.shape[0], :], here, done.at[n]))
    for copy in copies:
        copy.start()
    for copy in copies:
        copy.wait()


def join(parts, starts):
    rows, width = parts[-1].shape
    return pl.pallas_call(
        join_kernel,
        out_shape=jax.ShapeDtypeStruct((rows, width * len(parts)), parts[0].dtype),
        in_specs=[SMEM] + [VMEM] * len(parts),
        out_specs=HBM,
        scratch_shapes=[pltpu.SemaphoreType.DMA((len(parts),))],
        compiler_params=pltpu.CompilerParams(vmem_limit_bytes=16 * MIB),
        cost_estimate=pl.CostEstimate(flops=0, bytes_accessed=4 * rows * width * len(parts), transcendentals=0),
    )(jnp.stack(starts).astype(jnp.int32), *parts)


def local(activations, cotangent, inner_weight, outer_weight, outer_momentum, next_activations):
    fsdp, nz = lax.axis_size("fsdp"), lax.axis_size("z")
    f, z, x, c = (lax.axis_index(a) for a in ("fsdp", "z", "x", "core"))
    tok, d = activations.shape
    kv = cotangent.shape[1]
    width = d // fsdp
    block = width // nz
    share = block // (PAIR * CORES)
    own_weight = inner_weight[0]
    swap = ring(CORES, 1)

    def column(b, i, k, s):
        return ((f + s) % fsdp) * width + b * block + i * CORES * share + ((c + k) % CORES) * share

    def pair_ring(k, s):
        at = lambda i, j: (i % CORES) * fsdp + j % fsdp
        return [(at(i, j), at(i + k, j + s)) for i in range(CORES) for j in range(fsdp)]

    shifts = [(k, s) for s in range(fsdp) for k in range(CORES)]
    stages = [(m + 1, m) for m in range(nz - 2, -1, -2)]

    cots = {(0, 0): cotangent}
    for s in range(1, fsdp):
        cots[0, s] = lax.ppermute(cotangent, "fsdp", ring(fsdp, s))
    columns = [[column(z ^ m, (x + i) % PAIR, k, s) for m in ms for i in range(PAIR)] for ms in stages for k, s in shifts]
    (mine,), _ = pack([(activations, 1, share, columns)])
    acts = []
    for stage in range(len(stages)):
        came = []
        for (k, s), part in zip(shifts, mine[stage * len(shifts) :]):
            came.append(part if (k, s) == (0, 0) else lax.ppermute(part, ("core", "fsdp"), pair_ring(k, s)))
        acts.append(came)
    other_weight = lax.ppermute(own_weight, "core", swap)
    cots[1, 0] = lax.ppermute(cotangent, "core", swap)
    for s in range(1, fsdp):
        cots[1, s] = lax.ppermute(cots[0, s], "core", swap)

    far = [(i, k, s) for k in range(CORES) for i in range(PAIR) for s in range(fsdp)]
    near, away = [e for e in far if e[0] == 0], [e for e in far if e[0]]
    index = lambda i, k, s: ((i % PAIR) * CORES + k % CORES) * fsdp + s % fsdp
    every = [(i, k, s) for i in range(PAIR) for k in range(CORES) for s in range(fsdp)]
    groups = [[column(z ^ m, (x + i) % PAIR, k, s) for m in range(nz)] for i, k, s in far]
    wanted = [cots[0, s] for s in range(1, fsdp)]
    (parts,), wanted = pack([(next_activations, 1, share, groups)], wanted, pltpu.HBM)
    cots.update({(0, s): got for s, got in enumerate(wanted, 1)})
    mine, nexts = dict(zip(far, parts)), {}

    def send_next(i, k, s):
        pairs = [(index(*e), index(e[0] + i, e[1] + k, e[2] + s)) for e in every]
        nexts[i, k, s] = lax.ppermute(mine[i, k, s], ("x", "core", "fsdp"), pairs) if i or k or s else mine[i, k, s]

    ordered = [cots[k, s] for k, s in shifts]
    across_x, across_z = ring(PAIR, 1), [(i, i ^ 1) for i in range(nz)]
    over_z = {}

    def finish(m, to_z, to_x, keep_left, keep_right):
        from_z, from_x = lax.ppermute(to_z, "z", across_z), lax.ppermute(to_x, "x", across_x)
        return [keep_left, from_z, keep_right, from_x] + over_z.get(m, [])

    shape = lambda n, kind: jax.ShapeDtypeStruct((n * share, kv // 2), kind)
    for stage, ms in enumerate(stages):
        blocks = [((z ^ m) * PAIR + (x + i) % PAIR) * CORES + c for m in ms for i in range(PAIR)]
        place = jnp.stack(blocks).astype(jnp.int32)
        if not stage:
            place, *held = lax.optimization_barrier((place, *[mine[e] for e in far]))
            mine.update(zip(far, held))
            for e in near:
                send_next(*e)
        if stage:
            place, to_z, to_x = lax.optimization_barrier((place, to_z, to_x))
            m = stages[stage - 1][1]
            inputs = finish(m, to_z, to_x, keep_left, keep_right)
            (block_total,) = small_call(
                block_kernel, [jax.ShapeDtypeStruct((share, kv), bf16)], *inputs, spec=pl.BlockSpec()
            )
            low = m & -m
        to_x, stay_x, to_z, stay_z = inner_blocks(place, acts[stage], 0, ordered, own_weight, other_weight, share)
        if stage:
            to_x, to_z, block_total = lax.optimization_barrier((to_x, to_z, block_total))
            over_z.setdefault(m ^ low, []).append(lax.ppermute(block_total, "z", [(i, i ^ low) for i in range(nz)]))
        if not stage:
            stay_x, *island_cots = lax.optimization_barrier((stay_x, *[cots[0, s] for s in range(fsdp)]))
            grad_rows = lax.dot_general(
                jnp.concatenate(island_cots, axis=0), own_weight, (((1,), (1,)), ((), ())), preferred_element_type=f32
            ).astype(bf16)
            parts = [grad_rows] + [grad_rows[s * tok : (s + 1) * tok] for s in range(1, fsdp)]
            stay_x, *parts = lax.optimization_barrier((stay_x, *parts))
            for s in range(1, fsdp):
                parts[s] = lax.ppermute(parts[s], "fsdp", ring(fsdp, -s))
        from_x, from_z = lax.ppermute(to_x, "x", across_x), lax.ppermute(to_z, "z", across_z)
        to_z, keep_left, to_x, keep_right = small_call(
            functools.partial(middle_kernel, share),
            [shape(1, bf16), shape(1, f32)] * 2,
            stay_x,
            from_x,
            stay_z,
            from_z,
            spec=pl.BlockSpec(),
        )

    straight, diagonal = [e for e in away if e[2] == 0], [e for e in away if e[2]]
    held = (to_z, to_x, *[nexts[e] for e in near], *[mine[e] for e in straight])
    to_z, to_x, *held = lax.optimization_barrier(held)
    nexts.update(zip(near, held))
    mine.update(zip(straight, held[len(near) :]))
    inputs = finish(0, to_z, to_x, keep_left, keep_right)
    for e in straight:
        send_next(*e)
    inputs[0], inputs[2] = small_call(
        gather_kernel, [shape(1, f32)] * 2, keep_left, keep_right, *inputs[4:], spec=pl.BlockSpec(), weight=1 << 17
    )
    inputs[0], *held = lax.optimization_barrier((inputs[0], *[mine[e] for e in diagonal]))
    mine.update(zip(diagonal, held))
    for e in diagonal:
        send_next(*e)

    whole = jax.ShapeDtypeStruct((share, kv), f32)
    share_rows, new_outer, new_momentum = small_call(
        functools.partial(update_kernel, nz * PAIR * CORES),
        [jax.ShapeDtypeStruct((share, kv), bf16), whole, whole],
        *inputs[:4],
        outer_weight,
        outer_momentum,
        spec=pl.BlockSpec(),
    )

    rows = {}
    for m in sorted(range(1, nz), key=lambda m: (m & (m - 1)).bit_count() * nz - m):
        low = m & -m
        pieces = [share_rows] if m == low else list(rows[m ^ low])
        if m == 1:
            pieces[0], *held = lax.optimization_barrier((pieces[0], *[nexts[e] for e in straight]))
            nexts.update(zip(straight, held))
        if m == nz - 1:
            pieces[0], *parts = lax.optimization_barrier((pieces[0], *parts))
        rows[m] = [lax.ppermute(piece, "z", [(i, i ^ low) for i in range(nz)]) for piece in pieces]
    rows = [[share_rows]] + [rows[m] for m in range(1, nz)]
    input_grad = join(parts, [((f + s) % fsdp) * width for s in range(fsdp)])

    half = len(far) // CORES
    near, away = [nexts[e] for e in far[:half]], [nexts[e] for e in far[half:]]
    give, keep = keys_part(away, rows[:-1], 0), keys_part(near, rows[:-1], 0)
    give, keep, input_grad = lax.optimization_barrier((give, keep, input_grad))
    last = (nz - 1) * share
    give = keys_part(away, rows[-1:], last, [give])
    keep = keys_part(near, rows[-1:], last, [keep])
    came = lax.ppermute(give, "core", swap)
    shape = lambda n, kind: jax.ShapeDtypeStruct((n, kv // 2), kind)
    to_x, stay_x, stay_f, *to_f = small_call(
        functools.partial(core_sum_kernel, fsdp, tok),
        [shape(fsdp * tok, bf16), shape(fsdp * tok, f32), shape(PAIR * tok, f32)] + [shape(PAIR * tok, bf16)] * (fsdp - 1),
        keep,
        came,
    )

    def home(to_x, to_f):
        from_x = lax.ppermute(to_x, "x", ring(PAIR, 1))
        return [from_x] + [lax.ppermute(part, "fsdp", ring(fsdp, -s - 1)) for s, part in enumerate(to_f)]

    left, right, to_x, *to_f = small_call(
        functools.partial(second_sum_kernel, fsdp, tok),
        [shape(tok, f32)] * 2 + [shape(tok, bf16)] * fsdp,
        stay_x,
        stay_f,
        *home(to_x, to_f),
    )
    (keys,) = small_call(
        last_sum_kernel, [jax.ShapeDtypeStruct((tok, kv), bf16)], left, right, *home(to_x, to_f)
    )
    return (input_grad, keys, new_outer, new_momentum)


def solution(mesh):
    fsdp = mesh.shape["fsdp"]
    nz = mesh.shape["island"] // (PAIR * CORES)
    split = Mesh(mesh.devices.reshape(nz, PAIR, CORES, fsdp), ("z", "x", "core", "fsdp"))
    island = ("z", "x", "core")
    tokens = P(island + ("fsdp",), None)
    width = P(("fsdp",) + island, None)
    in_specs = (tokens, tokens, P(island, "fsdp", None), width, width, tokens)
    out_specs = (tokens, tokens, width, width)
    return jax.shard_map(local, mesh=split, in_specs=in_specs, out_specs=out_specs, check_vma=False)
```

```python
import functools

import jax
import jax.numpy as jnp
from jax import lax
from jax.experimental import pallas as pl
from jax.experimental.pallas import tpu as pltpu
from jax.sharding import Mesh, PartitionSpec as P

inner_rate = 1.2
outer_rate = 0.7
nesterov = 0.9
CORES = 2
PAIR = 2
LANES = 128

bf16, f32 = jnp.bfloat16, jnp.float32
VMEM, HBM = pl.BlockSpec(memory_space=pltpu.VMEM), pl.BlockSpec(memory_space=pltpu.HBM)
SMEM, ANY = pl.BlockSpec(memory_space=pltpu.SMEM), pl.BlockSpec(memory_space=pl.ANY)
MIB = 1024 * 1024


def ring(count, shift):
    return [(i, (i + shift) % count) for i in range(count)]


def strip(axis, start, size):
    return (pl.ds(start, size), slice(None)) if axis == 0 else (slice(None), pl.ds(start, size))


def in_hbm(array):
    return pltpu.with_memory_space_constraint(array, pltpu.HBM)


def pack_kernel(plan, starts, *refs):
    sources, outs, done = refs[: len(plan)], refs[len(plan) : -1], refs[-1]
    copies, o = [], 0
    for source, (axis, size, counts) in zip(sources, plan):
        for count in counts:
            for i in range(count):
                n = len(copies)
                part = source.at[strip(axis, pl.multiple_of(starts[n], size), size)]
                copies.append(pltpu.make_async_copy(part, outs[o].at[strip(axis, i * size, size)], done.at[n]))
            o += 1
    for copy in copies:
        copy.start()
    for copy in copies:
        copy.wait()


def pack(items, after=(), target=jax.ShapeDtypeStruct):
    result, rest = {}, []
    for n, (array, axis, size, groups) in enumerate(items):
        if axis == 1 and size % LANES:
            strips = [[lax.dynamic_slice_in_dim(array, at, size, axis=axis) for at in group] for group in groups]
            result[n] = [jnp.concatenate(group, axis=axis) for group in strips]
        else:
            rest.append((n, array, axis, size, groups))
    if not rest:
        return [result[n] for n in range(len(items))], list(after)
    starts = jnp.stack([at for item in rest for group in item[4] for at in group]).astype(jnp.int32)
    if after:
        starts, *after = lax.optimization_barrier((starts, *after))
    plan, shapes = [], []
    for _, array, axis, size, groups in rest:
        counts = [len(group) for group in groups]
        plan.append((axis, size, counts))
        for n in counts:
            shape = (n * size, array.shape[1]) if axis == 0 else (array.shape[0], n * size)
            shapes.append(target(shape, array.dtype))
    moved = 4 * starts.shape[0] * 1024 * LANES
    outs = pl.pallas_call(
        functools.partial(pack_kernel, plan),
        out_shape=shapes,
        in_specs=[SMEM] + [HBM] * len(rest),
        out_specs=[pl.BlockSpec()] * len(shapes),
        scratch_shapes=[pltpu.SemaphoreType.DMA((starts.shape[0],))],
        compiler_params=pltpu.CompilerParams(vmem_limit_bytes=16 * MIB),
        cost_estimate=pl.CostEstimate(flops=0, bytes_accessed=moved, transcendentals=0),
    )(starts, *[in_hbm(item[1]) for item in rest])
    for n, *_, groups in rest:
        result[n], outs = outs[: len(groups)], outs[len(groups) :]
    return [result[n] for n in range(len(items))], list(after)


def inner_kernel(pieces, share, scale, act_at, place, *refs):
    acts, cots = refs[:pieces], refs[pieces : 2 * pieces]
    own, other, to_x, stay_x, to_z, stay_z, left, right, rows, total, done = refs[2 * pieces :]
    tok, kv = cots[0].shape
    strips = 2 * PAIR
    copies = []

    def fetch(source, target):
        copies.append(pltpu.make_async_copy(source, target, done.at[len(copies)]))

    for n, (act, cot) in enumerate(zip(acts, cots)):
        here = pl.ds(n * tok, tok)
        fetch(act.at[:, pl.ds(act_at, strips * share)], left.at[here, :])
        fetch(cot, right.at[here, :])
    for i in range(strips):
        strip_rows = pl.ds(pl.multiple_of(place[i] * share, share), share)
        here = pl.ds(i * share, share)
        fetch(own.at[strip_rows, :], rows.at[0, here, :])
        fetch(other.at[strip_rows, :], rows.at[1, here, :])
    for copy in copies:
        copy.start()
    for copy in copies[: 2 * pieces]:
        copy.wait()
    total[...] = lax.dot_general(left[...], right[...], (((0,), (0,)), ((), ())), preferred_element_type=f32)
    for copy in copies[2 * pieces :]:
        copy.wait()

    def inner_new(i, columns):
        here = slice(i * share, (i + 1) * share)
        return (rows[0, here, columns].astype(f32) + rows[1, here, columns].astype(f32)) - scale * total[here, columns]

    first, second = slice(0, to_x.shape[1]), slice(to_x.shape[1], kv)
    for n in range(2):
        here = slice(n * share, (n + 1) * share)
        to_x[here, :] = inner_new(PAIR * n + 1, first).astype(bf16)
        to_z[here, :] = inner_new(n, second).astype(bf16)
    for n in range(2):
        here = slice(n * share, (n + 1) * share)
        stay_x[here, :] = inner_new(PAIR * n, first)
        stay_z[here, :] = inner_new(PAIR + n, second)


def inner_blocks(place, acts, act_at, cots, own, other, share, cut):
    pieces = len(acts)
    tok, kv = cots[0].shape
    rows = 2 * PAIR * share
    if act_at % LANES or rows % LANES:
        acts, act_at = [a[:, act_at : act_at + rows] for a in acts], 0
    shapes = [jax.ShapeDtypeStruct((2 * share, wide), kind) for wide in (cut, kv - cut) for kind in (bf16, f32)]
    return pl.pallas_call(
        functools.partial(inner_kernel, pieces, share, inner_rate / (tok * pieces // CORES), act_at),
        out_shape=shapes,
        in_specs=[SMEM] + [ANY] * (2 * pieces) + [HBM, ANY],
        out_specs=[pl.BlockSpec()] * 4,
        scratch_shapes=[
            pltpu.VMEM((pieces * tok, rows), bf16),
            pltpu.VMEM((pieces * tok, kv), bf16),
            pltpu.VMEM((CORES, rows, kv), bf16),
            pltpu.VMEM((rows, kv), f32),
            pltpu.SemaphoreType.DMA((2 * pieces + 2 * CORES * PAIR,)),
        ],
        compiler_params=pltpu.CompilerParams(vmem_limit_bytes=32 * MIB),
        cost_estimate=pl.CostEstimate(flops=pieces * tok * share * kv, bytes_accessed=share * kv, transcendentals=0),
    )(place, *acts, *cots, in_hbm(own), other)


def middle_kernel(share, stay_x, from_x, stay_z, from_z, to_z, keep_left, to_x, keep_right):
    over_x = stay_x[...] + from_x[...].astype(f32)
    over_z = stay_z[...] + from_z[...].astype(f32)
    to_z[...] = over_x[:share].astype(bf16)
    to_x[...] = over_z[share:].astype(bf16)
    keep_left[...] = over_x[share:]
    keep_right[...] = over_z[:share]


def block_sum(keep_left, from_z, keep_right, from_x, came):
    left = keep_left[...] + from_z[...].astype(f32)
    right = keep_right[...] + from_x[...].astype(f32)
    total = jnp.concatenate([left, right], axis=1)
    for other in came:
        total = total + other[...].astype(f32)
    return total


def gather_kernel(keep_left, keep_right, *refs):
    *came, left, right = refs
    total = jnp.concatenate([keep_left[...], keep_right[...]], axis=1)
    for other in came:
        total = total + other[...].astype(f32)
    left[...] = total[:, : left.shape[1]]
    right[...] = total[:, left.shape[1] :]


def block_kernel(*refs):
    *inputs, out = refs
    out[...] = block_sum(*inputs[:4], inputs[4:]).astype(bf16)


def update_kernel(replicas, *refs):
    *inputs, weight, momentum, share, new_outer, new_momentum = refs
    summed = block_sum(*inputs[:4], inputs[4:])
    pseudo_grad = weight[...] - summed / replicas
    moment = nesterov * momentum[...] + pseudo_grad
    outer = weight[...] - outer_rate * (pseudo_grad + nesterov * moment)
    share[...] = outer.astype(bf16)
    new_outer[...] = outer
    new_momentum[...] = moment


def keys_kernel(acts_count, counts, at, *refs):
    acts, (*pieces, out) = refs[:acts_count], refs[acts_count:]
    if at:
        *pieces, before = pieces
    blocks = []
    for count in counts:
        blocks.append(jnp.concatenate([w[...] for w in pieces[:count]], axis=1))
        pieces = pieces[count:]
    weight = jnp.concatenate(blocks, axis=0)
    left = jnp.concatenate([a[:, at : at + weight.shape[0]] for a in acts], axis=0)
    product = jnp.dot(left, weight, preferred_element_type=f32)
    out[...] = before[...] + product if at else product


def keys_part(acts, blocks, at, before=()):
    rows, kv = len(acts) * acts[0].shape[0], sum(w.shape[1] for w in blocks[0])
    depth = sum(block[0].shape[0] for block in blocks)
    if at % LANES:
        acts = [a[:, at:] for a in acts]
        return before[0] + keys_part(acts, blocks, 0)
    pieces = [w for block in blocks for w in block]
    return pl.pallas_call(
        functools.partial(keys_kernel, len(acts), [len(block) for block in blocks], at),
        out_shape=jax.ShapeDtypeStruct((rows, kv), f32),
        in_specs=[pl.BlockSpec()] * (len(acts) + len(pieces) + len(before)),
        out_specs=pl.BlockSpec(),
        compiler_params=pltpu.CompilerParams(vmem_limit_bytes=24 * MIB),
        cost_estimate=pl.CostEstimate(flops=2 * rows * depth * kv, bytes_accessed=rows * kv, transcendentals=0),
    )(*acts, *pieces, *before)


def core_sum_kernel(fsdp, tok, keep, came, to_x, stay_x, stay_f, *to_f):
    half = keep.shape[1] // 2
    total = keep[...] + came[...]
    rows = fsdp * tok
    stay_x[...] = total[:rows, :half]
    to_x[...] = total[rows:, :half].astype(bf16)
    for i in range(PAIR):
        here = slice(i * tok, (i + 1) * tok)
        stay_f[here, :] = total[i * rows : i * rows + tok, half:]
        for s in range(1, fsdp):
            to_f[s - 1][here, :] = total[i * rows + s * tok : i * rows + (s + 1) * tok, half:].astype(bf16)


def second_sum_kernel(fsdp, tok, *refs):
    stay_x, stay_f, from_x, *from_f = refs[: fsdp + 2]
    left, right, to_x, *to_f = refs[fsdp + 2 :]
    first = stay_x[...] + from_x[...].astype(f32)
    left[...] = first[:tok]
    for s in range(1, fsdp):
        to_f[s - 1][...] = first[s * tok : (s + 1) * tok].astype(bf16)
    second = stay_f[...]
    for came in from_f:
        second = second + came[...].astype(f32)
    right[...] = second[:tok]
    to_x[...] = second[tok:].astype(bf16)


def last_sum_kernel(left, right, from_x, *refs):
    *from_f, keys = refs
    half = left.shape[1]
    first = left[...]
    for came in from_f:
        first = first + came[...].astype(f32)
    keys[:, :half] = first.astype(bf16)
    keys[:, half:] = (right[...] + from_x[...].astype(f32)).astype(bf16)


def small_call(kernel, shapes, *args, spec=VMEM, weight=1):
    size = weight * sum(shape.size for shape in shapes)
    return pl.pallas_call(
        kernel,
        out_shape=shapes,
        in_specs=[spec] * len(args),
        out_specs=[spec] * len(shapes),
        compiler_params=pltpu.CompilerParams(vmem_limit_bytes=24 * MIB),
        cost_estimate=pl.CostEstimate(flops=size // 8, bytes_accessed=size // 8, transcendentals=0),
    )(*args)


def join_kernel(starts, *refs):
    *parts, out, done = refs
    copies = []
    for n, part in enumerate(parts):
        width = part.shape[1]
        here = out.at[:, pl.ds(pl.multiple_of(starts[n], width), width)]
        copies.append(pltpu.make_async_copy(part.at[: out.shape[0], :], here, done.at[n]))
    for copy in copies:
        copy.start()
    for copy in copies:
        copy.wait()


def join(parts, starts):
    rows, width = parts[-1].shape
    return pl.pallas_call(
        join_kernel,
        out_shape=jax.ShapeDtypeStruct((rows, width * len(parts)), parts[0].dtype),
        in_specs=[SMEM] + [VMEM] * len(parts),
        out_specs=HBM,
        scratch_shapes=[pltpu.SemaphoreType.DMA((len(parts),))],
        compiler_params=pltpu.CompilerParams(vmem_limit_bytes=16 * MIB),
        cost_estimate=pl.CostEstimate(flops=1 << 34, bytes_accessed=4 * rows * width * len(parts), transcendentals=0),
    )(jnp.stack(starts).astype(jnp.int32), *parts)


def local(activations, cotangent, inner_weight, outer_weight, outer_momentum, next_activations):
    fsdp, nz = lax.axis_size("fsdp"), lax.axis_size("z")
    f, z, x, c = (lax.axis_index(a) for a in ("fsdp", "z", "x", "core"))
    tok, d = activations.shape
    kv = cotangent.shape[1]
    width = d // fsdp
    block = width // nz
    share = block // (PAIR * CORES)
    own_weight = inner_weight[0]
    swap = ring(CORES, 1)

    def column(b, i, k, s):
        return ((f + s) % fsdp) * width + b * block + i * CORES * share + ((c + k) % CORES) * share

    def pair_ring(k, s):
        at = lambda i, j: (i % CORES) * fsdp + j % fsdp
        return [(at(i, j), at(i + k, j + s)) for i in range(CORES) for j in range(fsdp)]

    shifts = [(k, s) for s in range(fsdp) for k in range(CORES)]
    stages = [(m + 1, m) for m in range(nz - 2, -1, -2)]

    cots = {(0, 0): cotangent}
    for s in range(1, fsdp):
        cots[0, s] = lax.ppermute(cotangent, "fsdp", ring(fsdp, s))
    columns = [[column(z ^ m, (x + i) % PAIR, k, s) for m in ms for i in range(PAIR)] for ms in stages for k, s in shifts]
    (mine,), _ = pack([(activations, 1, share, columns)])
    acts = []
    for stage in range(len(stages)):
        came = []
        for (k, s), part in zip(shifts, mine[stage * len(shifts) :]):
            came.append(part if (k, s) == (0, 0) else lax.ppermute(part, ("core", "fsdp"), pair_ring(k, s)))
        acts.append(came)
    other_weight = lax.ppermute(own_weight, "core", swap)
    cots[1, 0] = lax.ppermute(cotangent, "core", swap)
    for s in range(1, fsdp):
        cots[1, s] = lax.ppermute(cots[0, s], "core", swap)

    far = [(i, k, s) for k in range(CORES) for i in range(PAIR) for s in range(fsdp)]
    near, away = [e for e in far if e[0] == 0], [e for e in far if e[0]]
    index = lambda i, k, s: ((i % PAIR) * CORES + k % CORES) * fsdp + s % fsdp
    every = [(i, k, s) for i in range(PAIR) for k in range(CORES) for s in range(fsdp)]
    groups = [[column(z ^ m, (x + i) % PAIR, k, s) for m in range(nz)] for i, k, s in far]
    wanted = [cots[0, s] for s in range(1, fsdp)]
    (parts,), wanted = pack([(next_activations, 1, share, groups)], wanted, pltpu.HBM)
    cots.update({(0, s): got for s, got in enumerate(wanted, 1)})
    mine, nexts = dict(zip(far, parts)), {}

    def send_next(i, k, s):
        pairs = [(index(*e), index(e[0] + i, e[1] + k, e[2] + s)) for e in every]
        nexts[i, k, s] = lax.ppermute(mine[i, k, s], ("x", "core", "fsdp"), pairs) if i or k or s else mine[i, k, s]

    ordered = [cots[k, s] for k, s in shifts]
    across_x, across_z = ring(PAIR, 1), [(i, i ^ 1) for i in range(nz)]
    over_z = {}

    def finish(m, to_z, to_x, keep_left, keep_right):
        from_z, from_x = lax.ppermute(to_z, "z", across_z), lax.ppermute(to_x, "x", across_x)
        return [keep_left, from_z, keep_right, from_x] + over_z.get(m, [])

    for stage, ms in enumerate(stages):
        cut = kv // 2 if ms[1] else 3 * kv // 4
        blocks = [((z ^ m) * PAIR + (x + i) % PAIR) * CORES + c for m in ms for i in range(PAIR)]
        place = jnp.stack(blocks).astype(jnp.int32)
        if not stage:
            place, *held = lax.optimization_barrier((place, *[mine[e] for e in far]))
            mine.update(zip(far, held))
            for e in near:
                send_next(*e)
        if stage:
            place, to_z, to_x = lax.optimization_barrier((place, to_z, to_x))
            m = stages[stage - 1][1]
            inputs = finish(m, to_z, to_x, keep_left, keep_right)
            low = m & -m
        to_x, stay_x, to_z, stay_z = inner_blocks(place, acts[stage], 0, ordered, own_weight, other_weight, share, cut)
        if stage:
            to_x, to_z, inputs[1], inputs[3] = lax.optimization_barrier((to_x, to_z, inputs[1], inputs[3]))
            (block_total,) = small_call(
                block_kernel, [jax.ShapeDtypeStruct((share, kv), bf16)], *inputs, spec=pl.BlockSpec()
            )
            over_z.setdefault(m ^ low, []).append(lax.ppermute(block_total, "z", [(i, i ^ low) for i in range(nz)]))
        if not stage:
            stay_x, *island_cots = lax.optimization_barrier((stay_x, *[cots[0, s] for s in range(fsdp)]))
            grad_rows = lax.dot_general(
                jnp.concatenate(island_cots, axis=0), own_weight, (((1,), (1,)), ((), ())), preferred_element_type=f32
            ).astype(bf16)
            parts = [grad_rows] + [grad_rows[s * tok : (s + 1) * tok] for s in range(1, fsdp)]
            stay_x, *parts = lax.optimization_barrier((stay_x, *parts))
            for s in range(1, fsdp):
                parts[s] = lax.ppermute(parts[s], "fsdp", ring(fsdp, -s))
        from_x, from_z = lax.ppermute(to_x, "x", across_x), lax.ppermute(to_z, "z", across_z)
        to_z, keep_left, to_x, keep_right = small_call(
            functools.partial(middle_kernel, share),
            [jax.ShapeDtypeStruct((share, wide), kind) for wide in (cut, kv - cut) for kind in (bf16, f32)],
            stay_x,
            from_x,
            stay_z,
            from_z,
            spec=pl.BlockSpec(),
        )

    straight, diagonal = [e for e in away if e[2] == 0], [e for e in away if e[2]]
    to_z, to_x, *held = lax.optimization_barrier((to_z, to_x, *[mine[e] for e in straight]))
    mine.update(zip(straight, held))
    inputs = finish(0, to_z, to_x, keep_left, keep_right)
    for e in straight:
        send_next(*e)
    inputs[0], inputs[2] = small_call(
        gather_kernel, [jax.ShapeDtypeStruct(part.shape, f32) for part in (keep_left, keep_right)], keep_left, keep_right, *inputs[4:], spec=pl.BlockSpec(), weight=200
    )
    inputs[0], *held = lax.optimization_barrier((inputs[0], *[mine[e] for e in diagonal]))
    mine.update(zip(diagonal, held))
    for e in diagonal:
        send_next(*e)

    whole = jax.ShapeDtypeStruct((share, kv), f32)
    share_rows, new_outer, new_momentum = small_call(
        functools.partial(update_kernel, nz * PAIR * CORES),
        [jax.ShapeDtypeStruct((share, kv), bf16), whole, whole],
        *inputs[:4],
        outer_weight,
        outer_momentum,
        spec=pl.BlockSpec(),
    )

    rows = {}
    for m in sorted(range(1, nz), key=lambda m: (m & (m - 1)).bit_count() * nz - m):
        low = m & -m
        pieces = [share_rows] if m == low else list(rows[m ^ low])
        if m == nz - 1:
            held = (share_rows, *parts, *[nexts[e] for e in far])
            share_rows, *held = lax.optimization_barrier(held)
            parts, held = held[: len(parts)], held[len(parts) :]
            nexts.update(zip(far, held))
            input_grad = join(parts, [((f + s) % fsdp) * width for s in range(fsdp)])
            pieces[0], input_grad = lax.optimization_barrier((pieces[0], input_grad))
        rows[m] = [lax.ppermute(piece, "z", [(i, i ^ low) for i in range(nz)]) for piece in pieces]
    rows = [[share_rows]] + [rows[m] for m in range(1, nz)]

    half = len(far) // CORES
    near, away = [nexts[e] for e in far[:half]], [nexts[e] for e in far[half:]]
    give, keep = keys_part(away, rows[:-1], 0), keys_part(near, rows[:-1], 0)
    give, keep, input_grad = lax.optimization_barrier((give, keep, input_grad))
    last = (nz - 1) * share
    give = keys_part(away, rows[-1:], last, [give])
    keep = keys_part(near, rows[-1:], last, [keep])
    came = lax.ppermute(give, "core", swap)
    shape = lambda n, kind: jax.ShapeDtypeStruct((n, kv // 2), kind)
    to_x, stay_x, stay_f, *to_f = small_call(
        functools.partial(core_sum_kernel, fsdp, tok),
        [shape(fsdp * tok, bf16), shape(fsdp * tok, f32), shape(PAIR * tok, f32)] + [shape(PAIR * tok, bf16)] * (fsdp - 1),
        keep,
        came,
    )

    def home(to_x, to_f):
        from_x = lax.ppermute(to_x, "x", ring(PAIR, 1))
        return [from_x] + [lax.ppermute(part, "fsdp", ring(fsdp, -s - 1)) for s, part in enumerate(to_f)]

    left, right, to_x, *to_f = small_call(
        functools.partial(second_sum_kernel, fsdp, tok),
        [shape(tok, f32)] * 2 + [shape(tok, bf16)] * fsdp,
        stay_x,
        stay_f,
        *home(to_x, to_f),
    )
    (keys,) = small_call(
        last_sum_kernel, [jax.ShapeDtypeStruct((tok, kv), bf16)], left, right, *home(to_x, to_f)
    )
    return (input_grad, keys, new_outer, new_momentum)


def solution(mesh):
    fsdp = mesh.shape["fsdp"]
    nz = mesh.shape["island"] // (PAIR * CORES)
    split = Mesh(mesh.devices.reshape(nz, PAIR, CORES, fsdp), ("z", "x", "core", "fsdp"))
    island = ("z", "x", "core")
    tokens = P(island + ("fsdp",), None)
    width = P(("fsdp",) + island, None)
    in_specs = (tokens, tokens, P(island, "fsdp", None), width, width, tokens)
    out_specs = (tokens, tokens, width, width)
    return jax.shard_map(local, mesh=split, in_specs=in_specs, out_specs=out_specs, check_vma=False)
```

```python
import functools

import jax
import jax.numpy as jnp
from jax import lax
from jax.experimental import pallas as pl
from jax.experimental.pallas import tpu as pltpu
from jax.sharding import Mesh, PartitionSpec as P

inner_rate = 1.2
outer_rate = 0.7
nesterov = 0.9
CORES = 2
PAIR = 2
LANES = 128

bf16, f32 = jnp.bfloat16, jnp.float32
VMEM, HBM = pl.BlockSpec(memory_space=pltpu.VMEM), pl.BlockSpec(memory_space=pltpu.HBM)
SMEM, ANY = pl.BlockSpec(memory_space=pltpu.SMEM), pl.BlockSpec(memory_space=pl.ANY)
MIB = 1024 * 1024


def ring(count, shift):
    return [(i, (i + shift) % count) for i in range(count)]


def strip(axis, start, size):
    return (pl.ds(start, size), slice(None)) if axis == 0 else (slice(None), pl.ds(start, size))


def in_hbm(array):
    return pltpu.with_memory_space_constraint(array, pltpu.HBM)


def pack_kernel(plan, starts, *refs):
    sources, outs, done = refs[: len(plan)], refs[len(plan) : -1], refs[-1]
    copies, o = [], 0
    for source, (axis, size, counts) in zip(sources, plan):
        for count in counts:
            for i in range(count):
                n = len(copies)
                part = source.at[strip(axis, pl.multiple_of(starts[n], size), size)]
                copies.append(pltpu.make_async_copy(part, outs[o].at[strip(axis, i * size, size)], done.at[n]))
            o += 1
    for copy in copies:
        copy.start()
    for copy in copies:
        copy.wait()


def pack(items, after=(), target=jax.ShapeDtypeStruct):
    result, rest = {}, []
    for n, (array, axis, size, groups) in enumerate(items):
        if axis == 1 and size % LANES:
            strips = [[lax.dynamic_slice_in_dim(array, at, size, axis=axis) for at in group] for group in groups]
            result[n] = [jnp.concatenate(group, axis=axis) for group in strips]
        else:
            rest.append((n, array, axis, size, groups))
    if not rest:
        return [result[n] for n in range(len(items))], list(after)
    starts = jnp.stack([at for item in rest for group in item[4] for at in group]).astype(jnp.int32)
    if after:
        starts, *after = lax.optimization_barrier((starts, *after))
    plan, shapes = [], []
    for _, array, axis, size, groups in rest:
        counts = [len(group) for group in groups]
        plan.append((axis, size, counts))
        for n in counts:
            shape = (n * size, array.shape[1]) if axis == 0 else (array.shape[0], n * size)
            shapes.append(target(shape, array.dtype))
    moved = 4 * starts.shape[0] * 1024 * LANES
    outs = pl.pallas_call(
        functools.partial(pack_kernel, plan),
        out_shape=shapes,
        in_specs=[SMEM] + [HBM] * len(rest),
        out_specs=[pl.BlockSpec()] * len(shapes),
        scratch_shapes=[pltpu.SemaphoreType.DMA((starts.shape[0],))],
        compiler_params=pltpu.CompilerParams(vmem_limit_bytes=16 * MIB),
        cost_estimate=pl.CostEstimate(flops=0, bytes_accessed=moved, transcendentals=0),
    )(starts, *[in_hbm(item[1]) for item in rest])
    for n, *_, groups in rest:
        result[n], outs = outs[: len(groups)], outs[len(groups) :]
    return [result[n] for n in range(len(items))], list(after)


def inner_kernel(pieces, share, scale, act_at, place, *refs):
    acts, cots = refs[:pieces], refs[pieces : 2 * pieces]
    own, other, to_x, stay_x, to_z, stay_z, left, right, rows, total, done = refs[2 * pieces :]
    tok, kv = cots[0].shape
    strips = 2 * PAIR
    copies = []

    def fetch(source, target):
        copies.append(pltpu.make_async_copy(source, target, done.at[len(copies)]))

    for n, (act, cot) in enumerate(zip(acts, cots)):
        here = pl.ds(n * tok, tok)
        fetch(act.at[:, pl.ds(act_at, strips * share)], left.at[here, :])
        fetch(cot, right.at[here, :])
    for i in range(strips):
        strip_rows = pl.ds(pl.multiple_of(place[i] * share, share), share)
        here = pl.ds(i * share, share)
        fetch(own.at[strip_rows, :], rows.at[0, here, :])
        fetch(other.at[strip_rows, :], rows.at[1, here, :])
    for copy in copies:
        copy.start()
    for copy in copies[: 2 * pieces]:
        copy.wait()
    total[...] = lax.dot_general(left[...], right[...], (((0,), (0,)), ((), ())), preferred_element_type=f32)
    for copy in copies[2 * pieces :]:
        copy.wait()

    def inner_new(i, columns):
        here = slice(i * share, (i + 1) * share)
        return (rows[0, here, columns].astype(f32) + rows[1, here, columns].astype(f32)) - scale * total[here, columns]

    first, second = slice(0, to_x.shape[1]), slice(to_x.shape[1], kv)
    for n in range(2):
        here = slice(n * share, (n + 1) * share)
        to_x[here, :] = inner_new(PAIR * n + 1, first).astype(bf16)
        to_z[here, :] = inner_new(n, second).astype(bf16)
    for n in range(2):
        here = slice(n * share, (n + 1) * share)
        stay_x[here, :] = inner_new(PAIR * n, first)
        stay_z[here, :] = inner_new(PAIR + n, second)


def inner_blocks(place, acts, act_at, cots, own, other, share, cut):
    pieces = len(acts)
    tok, kv = cots[0].shape
    rows = 2 * PAIR * share
    if act_at % LANES or rows % LANES:
        acts, act_at = [a[:, act_at : act_at + rows] for a in acts], 0
    shapes = [jax.ShapeDtypeStruct((2 * share, wide), kind) for wide in (cut, kv - cut) for kind in (bf16, f32)]
    return pl.pallas_call(
        functools.partial(inner_kernel, pieces, share, inner_rate / (tok * pieces // CORES), act_at),
        out_shape=shapes,
        in_specs=[SMEM] + [ANY] * (2 * pieces) + [HBM, ANY],
        out_specs=[pl.BlockSpec()] * 4,
        scratch_shapes=[
            pltpu.VMEM((pieces * tok, rows), bf16),
            pltpu.VMEM((pieces * tok, kv), bf16),
            pltpu.VMEM((CORES, rows, kv), bf16),
            pltpu.VMEM((rows, kv), f32),
            pltpu.SemaphoreType.DMA((2 * pieces + 2 * CORES * PAIR,)),
        ],
        compiler_params=pltpu.CompilerParams(vmem_limit_bytes=32 * MIB),
        cost_estimate=pl.CostEstimate(flops=pieces * tok * share * kv, bytes_accessed=share * kv, transcendentals=0),
    )(place, *acts, *cots, in_hbm(own), other)


def middle_kernel(share, stay_x, from_x, stay_z, from_z, to_z, keep_left, to_x, keep_right):
    over_x = stay_x[...] + from_x[...].astype(f32)
    over_z = stay_z[...] + from_z[...].astype(f32)
    to_z[...] = over_x[:share].astype(bf16)
    to_x[...] = over_z[share:].astype(bf16)
    keep_left[...] = over_x[share:]
    keep_right[...] = over_z[:share]


def block_sum(keep_left, from_z, keep_right, from_x, came):
    left = keep_left[...] + from_z[...].astype(f32)
    right = keep_right[...] + from_x[...].astype(f32)
    total = jnp.concatenate([left, right], axis=1)
    for other in came:
        total = total + other[...].astype(f32)
    return total


def gather_kernel(keep_left, keep_right, *refs):
    *came, left, right = refs
    total = jnp.concatenate([keep_left[...], keep_right[...]], axis=1)
    for other in came:
        total = total + other[...].astype(f32)
    left[...] = total[:, : left.shape[1]]
    right[...] = total[:, left.shape[1] :]


def block_kernel(*refs):
    *inputs, out = refs
    out[...] = block_sum(*inputs[:4], inputs[4:]).astype(bf16)


def update_kernel(replicas, *refs):
    *inputs, weight, momentum, share, new_outer, new_momentum = refs
    summed = block_sum(*inputs[:4], inputs[4:])
    pseudo_grad = weight[...] - summed / replicas
    moment = nesterov * momentum[...] + pseudo_grad
    outer = weight[...] - outer_rate * (pseudo_grad + nesterov * moment)
    share[...] = outer.astype(bf16)
    new_outer[...] = outer
    new_momentum[...] = moment


def keys_kernel(acts_count, counts, at, *refs):
    acts, refs = refs[:acts_count], refs[acts_count:]
    blocks = []
    for count in counts:
        blocks.append(jnp.concatenate([w[...] for w in refs[:count]], axis=1))
        refs = refs[count:]
    weight = jnp.concatenate(blocks, axis=0)
    before, outs = (refs[:1], refs[1:]) if at else ([], refs)
    each = acts_count // len(outs)
    for n, out in enumerate(outs):
        left = jnp.concatenate([a[:, at : at + weight.shape[0]] for a in acts[n * each : (n + 1) * each]], axis=0)
        product = jnp.dot(left, weight, preferred_element_type=f32)
        out[...] = before[0][...] + product if at else product


def keys_part(acts, blocks, at, before=(), outs=1):
    rows, kv = len(acts) * acts[0].shape[0] // outs, sum(w.shape[1] for w in blocks[0])
    depth = sum(block[0].shape[0] for block in blocks)
    if at % LANES:
        return [before[0] + keys_part([a[:, at:] for a in acts], blocks, 0)[0]]
    pieces = [w for block in blocks for w in block]
    flops = rows * depth * kv if at else 1 << 34
    return pl.pallas_call(
        functools.partial(keys_kernel, len(acts), [len(block) for block in blocks], at),
        out_shape=[jax.ShapeDtypeStruct((rows, kv), f32)] * outs,
        in_specs=[pl.BlockSpec()] * (len(acts) + len(pieces) + len(before)),
        out_specs=[pl.BlockSpec()] * outs,
        compiler_params=pltpu.CompilerParams(vmem_limit_bytes=32 * MIB),
        cost_estimate=pl.CostEstimate(flops=flops, bytes_accessed=rows * kv, transcendentals=0),
    )(*acts, *pieces, *before)


def core_sum_kernel(fsdp, tok, keep, came, to_x, stay_x, stay_f, *to_f):
    half = keep.shape[1] // 2
    total = keep[...] + came[...]
    rows = fsdp * tok
    stay_x[...] = total[:rows, :half]
    to_x[...] = total[rows:, :half].astype(bf16)
    for i in range(PAIR):
        here = slice(i * tok, (i + 1) * tok)
        stay_f[here, :] = total[i * rows : i * rows + tok, half:]
        for s in range(1, fsdp):
            to_f[s - 1][here, :] = total[i * rows + s * tok : i * rows + (s + 1) * tok, half:].astype(bf16)


def second_sum_kernel(fsdp, tok, *refs):
    stay_x, stay_f, from_x, *from_f = refs[: fsdp + 2]
    left, right, to_x, *to_f = refs[fsdp + 2 :]
    first = stay_x[...] + from_x[...].astype(f32)
    left[...] = first[:tok]
    for s in range(1, fsdp):
        to_f[s - 1][...] = first[s * tok : (s + 1) * tok].astype(bf16)
    second = stay_f[...]
    for came in from_f:
        second = second + came[...].astype(f32)
    right[...] = second[:tok]
    to_x[...] = second[tok:].astype(bf16)


def last_sum_kernel(left, right, from_x, *refs):
    *from_f, keys = refs
    half = left.shape[1]
    first = left[...]
    for came in from_f:
        first = first + came[...].astype(f32)
    keys[:, :half] = first.astype(bf16)
    keys[:, half:] = (right[...] + from_x[...].astype(f32)).astype(bf16)


def small_call(kernel, shapes, *args, spec=VMEM, weight=1):
    size = weight * sum(shape.size for shape in shapes)
    return pl.pallas_call(
        kernel,
        out_shape=shapes,
        in_specs=[spec] * len(args),
        out_specs=[spec] * len(shapes),
        compiler_params=pltpu.CompilerParams(vmem_limit_bytes=24 * MIB),
        cost_estimate=pl.CostEstimate(flops=size // 8, bytes_accessed=size // 8, transcendentals=0),
    )(*args)


def join_kernel(starts, *refs):
    *parts, out, done = refs
    copies = []
    for n, part in enumerate(parts):
        width = part.shape[1]
        here = out.at[:, pl.ds(pl.multiple_of(starts[n], width), width)]
        copies.append(pltpu.make_async_copy(part.at[: out.shape[0], :], here, done.at[n]))
    for copy in copies:
        copy.start()
    for copy in copies:
        copy.wait()


def join(parts, starts):
    rows, width = parts[-1].shape
    return pl.pallas_call(
        join_kernel,
        out_shape=jax.ShapeDtypeStruct((rows, width * len(parts)), parts[0].dtype),
        in_specs=[SMEM] + [VMEM] * len(parts),
        out_specs=HBM,
        scratch_shapes=[pltpu.SemaphoreType.DMA((len(parts),))],
        compiler_params=pltpu.CompilerParams(vmem_limit_bytes=16 * MIB),
        cost_estimate=pl.CostEstimate(flops=1 << 34, bytes_accessed=4 * rows * width * len(parts), transcendentals=0),
    )(jnp.stack(starts).astype(jnp.int32), *parts)


def local(activations, cotangent, inner_weight, outer_weight, outer_momentum, next_activations):
    fsdp, nz = lax.axis_size("fsdp"), lax.axis_size("z")
    f, z, x, c = (lax.axis_index(a) for a in ("fsdp", "z", "x", "core"))
    tok, d = activations.shape
    kv = cotangent.shape[1]
    width = d // fsdp
    block = width // nz
    share = block // (PAIR * CORES)
    own_weight = inner_weight[0]
    swap = ring(CORES, 1)

    def column(b, i, k, s):
        return ((f + s) % fsdp) * width + b * block + i * CORES * share + ((c + k) % CORES) * share

    def pair_ring(k, s):
        at = lambda i, j: (i % CORES) * fsdp + j % fsdp
        return [(at(i, j), at(i + k, j + s)) for i in range(CORES) for j in range(fsdp)]

    shifts = [(k, s) for s in range(fsdp) for k in range(CORES)]
    stages = [(m + 1, m) for m in range(nz - 2, -1, -2)]

    cots = {(0, 0): cotangent}
    for s in range(1, fsdp):
        cots[0, s] = lax.ppermute(cotangent, "fsdp", ring(fsdp, s))
    columns = [[column(z ^ m, (x + i) % PAIR, k, s) for m in ms for i in range(PAIR)] for ms in stages for k, s in shifts]
    (mine,), _ = pack([(activations, 1, share, columns)])
    acts = []
    for stage in range(len(stages)):
        came = []
        for (k, s), part in zip(shifts, mine[stage * len(shifts) :]):
            came.append(part if (k, s) == (0, 0) else lax.ppermute(part, ("core", "fsdp"), pair_ring(k, s)))
        acts.append(came)
    other_weight = lax.ppermute(own_weight, "core", swap)
    cots[1, 0] = lax.ppermute(cotangent, "core", swap)
    for s in range(1, fsdp):
        cots[1, s] = lax.ppermute(cots[0, s], "core", swap)

    far = [(i, k, s) for k in range(CORES) for i in range(PAIR) for s in range(fsdp)]
    index = lambda i, k, s: ((i % PAIR) * CORES + k % CORES) * fsdp + s % fsdp
    every = [(i, k, s) for i in range(PAIR) for k in range(CORES) for s in range(fsdp)]
    groups = [[column(z ^ m, (x + i) % PAIR, k, s) for m in range(nz)] for i, k, s in far]
    wanted = [cots[0, s] for s in range(1, fsdp)]
    (parts,), wanted = pack([(next_activations, 1, share, groups)], wanted, pltpu.HBM)
    cots.update({(0, s): got for s, got in enumerate(wanted, 1)})
    mine, nexts = dict(zip(far, parts)), {}

    def send_next(i, k, s):
        pairs = [(index(*e), index(e[0] + i, e[1] + k, e[2] + s)) for e in every]
        nexts[i, k, s] = lax.ppermute(mine[i, k, s], ("x", "core", "fsdp"), pairs) if i or k or s else mine[i, k, s]

    ordered = [cots[k, s] for k, s in shifts]
    across_x, across_z = ring(PAIR, 1), [(i, i ^ 1) for i in range(nz)]
    over_z = {}

    def finish(m, to_z, to_x, keep_left, keep_right):
        from_z, from_x = lax.ppermute(to_z, "z", across_z), lax.ppermute(to_x, "x", across_x)
        return [keep_left, from_z, keep_right, from_x] + over_z.get(m, [])

    for stage, ms in enumerate(stages):
        cut = kv // 2 if ms[1] else 3 * kv // 4
        blocks = [((z ^ m) * PAIR + (x + i) % PAIR) * CORES + c for m in ms for i in range(PAIR)]
        place = jnp.stack(blocks).astype(jnp.int32)
        if not stage:
            place, *held = lax.optimization_barrier((place, *[mine[e] for e in far]))
            mine.update(zip(far, held))
        if stage:
            place, to_z, to_x = lax.optimization_barrier((place, to_z, to_x))
            m = stages[stage - 1][1]
            inputs = finish(m, to_z, to_x, keep_left, keep_right)
            low = m & -m
        to_x, stay_x, to_z, stay_z = inner_blocks(place, acts[stage], 0, ordered, own_weight, other_weight, share, cut)
        if stage:
            to_x, to_z, inputs[1], inputs[3] = lax.optimization_barrier((to_x, to_z, inputs[1], inputs[3]))
            (block_total,) = small_call(
                block_kernel, [jax.ShapeDtypeStruct((share, kv), bf16)], *inputs, spec=pl.BlockSpec()
            )
            over_z.setdefault(m ^ low, []).append(lax.ppermute(block_total, "z", [(i, i ^ low) for i in range(nz)]))
        if not stage:
            stay_x, *island_cots = lax.optimization_barrier((stay_x, *[cots[0, s] for s in range(fsdp)]))
            grad_rows = lax.dot_general(
                jnp.concatenate(island_cots, axis=0), own_weight, (((1,), (1,)), ((), ())), preferred_element_type=f32
            ).astype(bf16)
            parts = [grad_rows] + [grad_rows[s * tok : (s + 1) * tok] for s in range(1, fsdp)]
            stay_x, *parts = lax.optimization_barrier((stay_x, *parts))
            for s in range(1, fsdp):
                parts[s] = lax.ppermute(parts[s], "fsdp", ring(fsdp, -s))
        from_x, from_z = lax.ppermute(to_x, "x", across_x), lax.ppermute(to_z, "z", across_z)
        to_z, keep_left, to_x, keep_right = small_call(
            functools.partial(middle_kernel, share),
            [jax.ShapeDtypeStruct((share, wide), kind) for wide in (cut, kv - cut) for kind in (bf16, f32)],
            stay_x,
            from_x,
            stay_z,
            from_z,
            spec=pl.BlockSpec(),
        )

    inputs = finish(0, to_z, to_x, keep_left, keep_right)
    inputs[0], inputs[2] = small_call(
        gather_kernel, [jax.ShapeDtypeStruct(part.shape, f32) for part in (keep_left, keep_right)], keep_left, keep_right, *inputs[4:], spec=pl.BlockSpec(), weight=200
    )
    whole = jax.ShapeDtypeStruct((share, kv), f32)
    share_rows, new_outer, new_momentum = small_call(
        functools.partial(update_kernel, nz * PAIR * CORES),
        [jax.ShapeDtypeStruct((share, kv), bf16), whole, whole],
        *inputs[:4],
        outer_weight,
        outer_momentum,
        spec=pl.BlockSpec(),
    )

    share_rows, *held = lax.optimization_barrier((share_rows, *[mine[e] for e in far]))
    mine.update(zip(far, held))
    for e in far:
        send_next(*e)

    rows = {}
    for m in sorted(range(1, nz), key=lambda m: (m & (m - 1)).bit_count() * nz - m):
        low = m & -m
        pieces = [share_rows] if m == low else list(rows[m ^ low])
        if m == nz - 1:
            share_rows, *parts = lax.optimization_barrier((share_rows, *parts))
            input_grad = join(parts, [((f + s) % fsdp) * width for s in range(fsdp)])
            pieces[0], input_grad = lax.optimization_barrier((pieces[0], input_grad))
        rows[m] = [lax.ppermute(piece, "z", [(i, i ^ low) for i in range(nz)]) for piece in pieces]
    rows = [[share_rows]] + [rows[m] for m in range(1, nz)]

    half = len(far) // CORES
    near, away = [nexts[e] for e in far[:half]], [nexts[e] for e in far[half:]]
    give, keep = keys_part(away + near, rows[:-1], 0, outs=2)
    give, keep, input_grad = lax.optimization_barrier((give, keep, input_grad))
    last = (nz - 1) * share
    (give,) = keys_part(away, rows[-1:], last, [give])
    (keep,) = keys_part(near, rows[-1:], last, [keep])
    came = lax.ppermute(give, "core", swap)
    shape = lambda n, kind: jax.ShapeDtypeStruct((n, kv // 2), kind)
    to_x, stay_x, stay_f, *to_f = small_call(
        functools.partial(core_sum_kernel, fsdp, tok),
        [shape(fsdp * tok, bf16), shape(fsdp * tok, f32), shape(PAIR * tok, f32)] + [shape(PAIR * tok, bf16)] * (fsdp - 1),
        keep,
        came,
    )

    def home(to_x, to_f):
        from_x = lax.ppermute(to_x, "x", ring(PAIR, 1))
        return [from_x] + [lax.ppermute(part, "fsdp", ring(fsdp, -s - 1)) for s, part in enumerate(to_f)]

    left, right, to_x, *to_f = small_call(
        functools.partial(second_sum_kernel, fsdp, tok),
        [shape(tok, f32)] * 2 + [shape(tok, bf16)] * fsdp,
        stay_x,
        stay_f,
        *home(to_x, to_f),
    )
    (keys,) = small_call(
        last_sum_kernel, [jax.ShapeDtypeStruct((tok, kv), bf16)], left, right, *home(to_x, to_f)
    )
    return (input_grad, keys, new_outer, new_momentum)


def solution(mesh):
    fsdp = mesh.shape["fsdp"]
    nz = mesh.shape["island"] // (PAIR * CORES)
    split = Mesh(mesh.devices.reshape(nz, PAIR, CORES, fsdp), ("z", "x", "core", "fsdp"))
    island = ("z", "x", "core")
    tokens = P(island + ("fsdp",), None)
    width = P(("fsdp",) + island, None)
    in_specs = (tokens, tokens, P(island, "fsdp", None), width, width, tokens)
    out_specs = (tokens, tokens, width, width)
    return jax.shard_map(local, mesh=split, in_specs=in_specs, out_specs=out_specs, check_vma=False)
```

```python
import functools

import jax
import jax.numpy as jnp
from jax import lax
from jax.experimental import pallas as pl
from jax.experimental.pallas import tpu as pltpu
from jax.sharding import Mesh, PartitionSpec as P

inner_rate = 1.2
outer_rate = 0.7
nesterov = 0.9
CORES = 2
PAIR = 2
LANES = 128

bf16, f32 = jnp.bfloat16, jnp.float32
VMEM, HBM = pl.BlockSpec(memory_space=pltpu.VMEM), pl.BlockSpec(memory_space=pltpu.HBM)
SMEM, ANY = pl.BlockSpec(memory_space=pltpu.SMEM), pl.BlockSpec(memory_space=pl.ANY)
MIB = 1024 * 1024


def ring(count, shift):
    return [(i, (i + shift) % count) for i in range(count)]


def strip(axis, start, size):
    return (pl.ds(start, size), slice(None)) if axis == 0 else (slice(None), pl.ds(start, size))


def in_hbm(array):
    return pltpu.with_memory_space_constraint(array, pltpu.HBM)


def pack_kernel(plan, starts, *refs):
    sources, outs, done = refs[: len(plan)], refs[len(plan) : -1], refs[-1]
    copies, o = [], 0
    for source, (axis, size, counts) in zip(sources, plan):
        for count in counts:
            for i in range(count):
                n = len(copies)
                part = source.at[strip(axis, pl.multiple_of(starts[n], size), size)]
                copies.append(pltpu.make_async_copy(part, outs[o].at[strip(axis, i * size, size)], done.at[n]))
            o += 1
    for copy in copies:
        copy.start()
    for copy in copies:
        copy.wait()


def pack(items, after=(), target=jax.ShapeDtypeStruct):
    result, rest = {}, []
    for n, (array, axis, size, groups) in enumerate(items):
        if axis == 1 and size % LANES:
            strips = [[lax.dynamic_slice_in_dim(array, at, size, axis=axis) for at in group] for group in groups]
            result[n] = [jnp.concatenate(group, axis=axis) for group in strips]
        else:
            rest.append((n, array, axis, size, groups))
    if not rest:
        return [result[n] for n in range(len(items))], list(after)
    starts = jnp.stack([at for item in rest for group in item[4] for at in group]).astype(jnp.int32)
    if after:
        starts, *after = lax.optimization_barrier((starts, *after))
    plan, shapes = [], []
    for _, array, axis, size, groups in rest:
        counts = [len(group) for group in groups]
        plan.append((axis, size, counts))
        for n in counts:
            shape = (n * size, array.shape[1]) if axis == 0 else (array.shape[0], n * size)
            shapes.append(target(shape, array.dtype))
    moved = 4 * starts.shape[0] * 1024 * LANES
    outs = pl.pallas_call(
        functools.partial(pack_kernel, plan),
        out_shape=shapes,
        in_specs=[SMEM] + [HBM] * len(rest),
        out_specs=[pl.BlockSpec()] * len(shapes),
        scratch_shapes=[pltpu.SemaphoreType.DMA((starts.shape[0],))],
        compiler_params=pltpu.CompilerParams(vmem_limit_bytes=16 * MIB),
        cost_estimate=pl.CostEstimate(flops=0, bytes_accessed=moved, transcendentals=0),
    )(starts, *[in_hbm(item[1]) for item in rest])
    for n, *_, groups in rest:
        result[n], outs = outs[: len(groups)], outs[len(groups) :]
    return [result[n] for n in range(len(items))], list(after)


def inner_kernel(pieces, share, scale, act_at, place, *refs):
    acts, cots = refs[:pieces], refs[pieces : 2 * pieces]
    own, other, to_x, stay_x, to_z, stay_z, left, right, rows, total, done = refs[2 * pieces :]
    tok, kv = cots[0].shape
    strips = 2 * PAIR
    copies = []

    def fetch(source, target):
        copies.append(pltpu.make_async_copy(source, target, done.at[len(copies)]))

    for n, (act, cot) in enumerate(zip(acts, cots)):
        here = pl.ds(n * tok, tok)
        fetch(act.at[:, pl.ds(act_at, strips * share)], left.at[here, :])
        fetch(cot, right.at[here, :])
    for i in range(strips):
        strip_rows = pl.ds(pl.multiple_of(place[i] * share, share), share)
        here = pl.ds(i * share, share)
        fetch(own.at[strip_rows, :], rows.at[0, here, :])
        fetch(other.at[strip_rows, :], rows.at[1, here, :])
    for copy in copies:
        copy.start()
    for copy in copies[: 2 * pieces]:
        copy.wait()
    total[...] = lax.dot_general(left[...], right[...], (((0,), (0,)), ((), ())), preferred_element_type=f32)
    for copy in copies[2 * pieces :]:
        copy.wait()

    def inner_new(i, columns):
        here = slice(i * share, (i + 1) * share)
        return (rows[0, here, columns].astype(f32) + rows[1, here, columns].astype(f32)) - scale * total[here, columns]

    first, second = slice(0, to_x.shape[1]), slice(to_x.shape[1], kv)
    for n in range(2):
        here = slice(n * share, (n + 1) * share)
        to_x[here, :] = inner_new(PAIR * n + 1, first).astype(bf16)
        to_z[here, :] = inner_new(n, second).astype(bf16)
    for n in range(2):
        here = slice(n * share, (n + 1) * share)
        stay_x[here, :] = inner_new(PAIR * n, first)
        stay_z[here, :] = inner_new(PAIR + n, second)


def inner_blocks(place, acts, act_at, cots, own, other, share, cut):
    pieces = len(acts)
    tok, kv = cots[0].shape
    rows = 2 * PAIR * share
    if act_at % LANES or rows % LANES:
        acts, act_at = [a[:, act_at : act_at + rows] for a in acts], 0
    shapes = [jax.ShapeDtypeStruct((2 * share, wide), kind) for wide in (cut, kv - cut) for kind in (bf16, f32)]
    return pl.pallas_call(
        functools.partial(inner_kernel, pieces, share, inner_rate / (tok * pieces // CORES), act_at),
        out_shape=shapes,
        in_specs=[SMEM] + [ANY] * (2 * pieces) + [HBM, ANY],
        out_specs=[pl.BlockSpec()] * 4,
        scratch_shapes=[
            pltpu.VMEM((pieces * tok, rows), bf16),
            pltpu.VMEM((pieces * tok, kv), bf16),
            pltpu.VMEM((CORES, rows, kv), bf16),
            pltpu.VMEM((rows, kv), f32),
            pltpu.SemaphoreType.DMA((2 * pieces + 2 * CORES * PAIR,)),
        ],
        compiler_params=pltpu.CompilerParams(vmem_limit_bytes=32 * MIB),
        cost_estimate=pl.CostEstimate(flops=pieces * tok * share * kv, bytes_accessed=share * kv, transcendentals=0),
    )(place, *acts, *cots, in_hbm(own), other)


def middle_kernel(share, stay_x, from_x, stay_z, from_z, to_z, keep_left, to_x, keep_right):
    over_x = stay_x[...] + from_x[...].astype(f32)
    over_z = stay_z[...] + from_z[...].astype(f32)
    to_z[...] = over_x[:share].astype(bf16)
    to_x[...] = over_z[share:].astype(bf16)
    keep_left[...] = over_x[share:]
    keep_right[...] = over_z[:share]


def block_sum(keep_left, from_z, keep_right, from_x, came):
    left = keep_left[...] + from_z[...].astype(f32)
    right = keep_right[...] + from_x[...].astype(f32)
    total = jnp.concatenate([left, right], axis=1)
    for other in came:
        total = total + other[...].astype(f32)
    return total


def gather_kernel(keep_left, keep_right, *refs):
    *came, left, right = refs
    total = jnp.concatenate([keep_left[...], keep_right[...]], axis=1)
    for other in came:
        total = total + other[...].astype(f32)
    left[...] = total[:, : left.shape[1]]
    right[...] = total[:, left.shape[1] :]


def block_kernel(*refs):
    *inputs, out = refs
    out[...] = block_sum(*inputs[:4], inputs[4:]).astype(bf16)


def outer_step(replicas, inputs, weight, momentum):
    pseudo_grad = weight[...] - block_sum(*inputs[:4], inputs[4:]) / replicas
    moment = nesterov * momentum[...] + pseudo_grad
    return weight[...] - outer_rate * (pseudo_grad + nesterov * moment), moment


def share_kernel(replicas, *refs):
    *inputs, weight, momentum, share = refs
    share[...] = outer_step(replicas, inputs, weight, momentum)[0].astype(bf16)


def state_kernel(replicas, *refs):
    *inputs, weight, momentum, new_outer, new_momentum = refs
    new_outer[...], new_momentum[...] = outer_step(replicas, inputs, weight, momentum)


def keys_kernel(acts_count, counts, at, *refs):
    acts, refs = refs[:acts_count], refs[acts_count:]
    blocks = []
    for count in counts:
        blocks.append(jnp.concatenate([w[...] for w in refs[:count]], axis=1))
        refs = refs[count:]
    weight = jnp.concatenate(blocks, axis=0)
    before, outs = (refs[:1], refs[1:]) if at else ([], refs)
    each = acts_count // len(outs)
    for n, out in enumerate(outs):
        left = jnp.concatenate([a[:, at : at + weight.shape[0]] for a in acts[n * each : (n + 1) * each]], axis=0)
        product = jnp.dot(left, weight, preferred_element_type=f32)
        out[...] = before[0][...] + product if at else product


def keys_part(acts, blocks, at, before=(), outs=1):
    rows, kv = len(acts) * acts[0].shape[0] // outs, sum(w.shape[1] for w in blocks[0])
    depth = sum(block[0].shape[0] for block in blocks)
    if at % LANES:
        return [before[0] + keys_part([a[:, at:] for a in acts], blocks, 0)[0]]
    pieces = [w for block in blocks for w in block]
    flops = rows * depth * kv if at else 1 << 34
    return pl.pallas_call(
        functools.partial(keys_kernel, len(acts), [len(block) for block in blocks], at),
        out_shape=[jax.ShapeDtypeStruct((rows, kv), f32)] * outs,
        in_specs=[pl.BlockSpec()] * (len(acts) + len(pieces) + len(before)),
        out_specs=[pl.BlockSpec()] * outs,
        compiler_params=pltpu.CompilerParams(vmem_limit_bytes=32 * MIB),
        cost_estimate=pl.CostEstimate(flops=flops, bytes_accessed=rows * kv, transcendentals=0),
    )(*acts, *pieces, *before)


def core_sum_kernel(fsdp, tok, keep, came, to_x, stay_x, stay_f, *to_f):
    half = keep.shape[1] // 2
    total = keep[...] + came[...]
    rows = fsdp * tok
    stay_x[...] = total[:rows, :half]
    to_x[...] = total[rows:, :half].astype(bf16)
    for i in range(PAIR):
        here = slice(i * tok, (i + 1) * tok)
        stay_f[here, :] = total[i * rows : i * rows + tok, half:]
        for s in range(1, fsdp):
            to_f[s - 1][here, :] = total[i * rows + s * tok : i * rows + (s + 1) * tok, half:].astype(bf16)


def second_sum_kernel(fsdp, tok, *refs):
    stay_x, stay_f, from_x, *from_f = refs[: fsdp + 2]
    left, right, to_x, *to_f = refs[fsdp + 2 :]
    first = stay_x[...] + from_x[...].astype(f32)
    left[...] = first[:tok]
    for s in range(1, fsdp):
        to_f[s - 1][...] = first[s * tok : (s + 1) * tok].astype(bf16)
    second = stay_f[...]
    for came in from_f:
        second = second + came[...].astype(f32)
    right[...] = second[:tok]
    to_x[...] = second[tok:].astype(bf16)


def last_sum_kernel(left, right, from_x, *refs):
    *from_f, keys = refs
    half = left.shape[1]
    first = left[...]
    for came in from_f:
        first = first + came[...].astype(f32)
    keys[:, :half] = first.astype(bf16)
    keys[:, half:] = (right[...] + from_x[...].astype(f32)).astype(bf16)


def small_call(kernel, shapes, *args, spec=VMEM, weight=1):
    size = weight * sum(shape.size for shape in shapes)
    return pl.pallas_call(
        kernel,
        out_shape=shapes,
        in_specs=[spec] * len(args),
        out_specs=[spec] * len(shapes),
        compiler_params=pltpu.CompilerParams(vmem_limit_bytes=24 * MIB),
        cost_estimate=pl.CostEstimate(flops=size // 8, bytes_accessed=size // 8, transcendentals=0),
    )(*args)


def join_kernel(starts, *refs):
    *parts, out, done = refs
    copies = []
    for n, part in enumerate(parts):
        width = part.shape[1]
        here = out.at[:, pl.ds(pl.multiple_of(starts[n], width), width)]
        copies.append(pltpu.make_async_copy(part.at[: out.shape[0], :], here, done.at[n]))
    for copy in copies:
        copy.start()
    for copy in copies:
        copy.wait()


def join(parts, starts):
    rows, width = parts[-1].shape
    return pl.pallas_call(
        join_kernel,
        out_shape=jax.ShapeDtypeStruct((rows, width * len(parts)), parts[0].dtype),
        in_specs=[SMEM] + [VMEM] * len(parts),
        out_specs=HBM,
        scratch_shapes=[pltpu.SemaphoreType.DMA((len(parts),))],
        compiler_params=pltpu.CompilerParams(vmem_limit_bytes=16 * MIB),
        cost_estimate=pl.CostEstimate(flops=0, bytes_accessed=4 * rows * width * len(parts), transcendentals=0),
    )(jnp.stack(starts).astype(jnp.int32), *parts)


def local(activations, cotangent, inner_weight, outer_weight, outer_momentum, next_activations):
    fsdp, nz = lax.axis_size("fsdp"), lax.axis_size("z")
    f, z, x, c = (lax.axis_index(a) for a in ("fsdp", "z", "x", "core"))
    tok, d = activations.shape
    kv = cotangent.shape[1]
    width = d // fsdp
    block = width // nz
    share = block // (PAIR * CORES)
    own_weight = inner_weight[0]
    swap = ring(CORES, 1)

    def column(b, i, k, s):
        return ((f + s) % fsdp) * width + b * block + i * CORES * share + ((c + k) % CORES) * share

    def pair_ring(k, s):
        at = lambda i, j: (i % CORES) * fsdp + j % fsdp
        return [(at(i, j), at(i + k, j + s)) for i in range(CORES) for j in range(fsdp)]

    shifts = [(k, s) for s in range(fsdp) for k in range(CORES)]
    stages = [(m + 1, m) for m in range(nz - 2, -1, -2)]

    far = [(i, k, s) for k in range(CORES) for i in range(PAIR) for s in range(fsdp)]
    early = [(0, 1, 0), (1, 0, 0)]
    late = [e for e in far if e not in early]
    index = lambda i, k, s: ((i % PAIR) * CORES + k % CORES) * fsdp + s % fsdp
    every = [(i, k, s) for i in range(PAIR) for k in range(CORES) for s in range(fsdp)]
    mine, nexts = {}, {}

    def next_groups(places):
        return [[column(z ^ m, (x + i) % PAIR, k, s) for m in range(nz)] for i, k, s in places]

    def send_next(i, k, s):
        pairs = [(index(*e), index(e[0] + i, e[1] + k, e[2] + s)) for e in every]
        nexts[i, k, s] = lax.ppermute(mine[i, k, s], ("x", "core", "fsdp"), pairs) if i or k or s else mine[i, k, s]

    cots = {(0, 0): cotangent}
    for s in range(1, fsdp):
        cots[0, s] = lax.ppermute(cotangent, "fsdp", ring(fsdp, s))
    columns = [[column(z ^ m, (x + i) % PAIR, k, s) for m in ms for i in range(PAIR)] for ms in stages for k, s in shifts]
    items = [(activations, 1, share, columns), (next_activations, 1, share, next_groups(early))]
    (packed, parts), _ = pack(items)
    mine.update(zip(early, parts))
    for e in early:
        send_next(*e)
    acts = []
    for stage in range(len(stages)):
        came = []
        for (k, s), part in zip(shifts, packed[stage * len(shifts) :]):
            came.append(part if (k, s) == (0, 0) else lax.ppermute(part, ("core", "fsdp"), pair_ring(k, s)))
        acts.append(came)
    other_weight = lax.ppermute(own_weight, "core", swap)
    cots[1, 0] = lax.ppermute(cotangent, "core", swap)
    for s in range(1, fsdp):
        cots[1, s] = lax.ppermute(cots[0, s], "core", swap)

    wanted = [cots[0, s] for s in range(1, fsdp)]
    (parts,), wanted = pack([(next_activations, 1, share, next_groups(late))], wanted, pltpu.HBM)
    cots.update({(0, s): got for s, got in enumerate(wanted, 1)})
    mine.update(zip(late, parts))

    ordered = [cots[k, s] for k, s in shifts]
    across_x, across_z = ring(PAIR, 1), [(i, i ^ 1) for i in range(nz)]
    over_z = {}

    def finish(m, to_z, to_x, keep_left, keep_right):
        from_z, from_x = lax.ppermute(to_z, "z", across_z), lax.ppermute(to_x, "x", across_x)
        return [keep_left, from_z, keep_right, from_x] + over_z.get(m, [])

    for stage, ms in enumerate(stages):
        cut = kv // 2 if ms[1] else 3 * kv // 4
        blocks = [((z ^ m) * PAIR + (x + i) % PAIR) * CORES + c for m in ms for i in range(PAIR)]
        place = jnp.stack(blocks).astype(jnp.int32)
        if not stage:
            held = (place, *[mine[e] for e in late], *[nexts[e] for e in early])
            place, *held = lax.optimization_barrier(held)
            mine.update(zip(late, held))
            nexts.update(zip(early, held[len(late) :]))
        if stage:
            place, to_z, to_x = lax.optimization_barrier((place, to_z, to_x))
            m = stages[stage - 1][1]
            inputs = finish(m, to_z, to_x, keep_left, keep_right)
            low = m & -m
        to_x, stay_x, to_z, stay_z = inner_blocks(place, acts[stage], 0, ordered, own_weight, other_weight, share, cut)
        if stage:
            to_x, to_z, inputs[1], inputs[3] = lax.optimization_barrier((to_x, to_z, inputs[1], inputs[3]))
            (block_total,) = small_call(
                block_kernel, [jax.ShapeDtypeStruct((share, kv), bf16)], *inputs, spec=pl.BlockSpec()
            )
            over_z.setdefault(m ^ low, []).append(lax.ppermute(block_total, "z", [(i, i ^ low) for i in range(nz)]))
        if not stage:
            stay_x, *island_cots = lax.optimization_barrier((stay_x, *[cots[0, s] for s in range(fsdp)]))
            grad_rows = lax.dot_general(
                jnp.concatenate(island_cots, axis=0), own_weight, (((1,), (1,)), ((), ())), preferred_element_type=f32
            ).astype(bf16)
            parts = [grad_rows] + [grad_rows[s * tok : (s + 1) * tok] for s in range(1, fsdp)]
            stay_x, *parts = lax.optimization_barrier((stay_x, *parts))
            for s in range(1, fsdp):
                parts[s] = lax.ppermute(parts[s], "fsdp", ring(fsdp, -s))
        from_x, from_z = lax.ppermute(to_x, "x", across_x), lax.ppermute(to_z, "z", across_z)
        to_z, keep_left, to_x, keep_right = small_call(
            functools.partial(middle_kernel, share),
            [jax.ShapeDtypeStruct((share, wide), kind) for wide in (cut, kv - cut) for kind in (bf16, f32)],
            stay_x,
            from_x,
            stay_z,
            from_z,
            spec=pl.BlockSpec(),
        )

    inputs = finish(0, to_z, to_x, keep_left, keep_right)
    inputs[0], inputs[2] = small_call(
        gather_kernel, [jax.ShapeDtypeStruct(part.shape, f32) for part in (keep_left, keep_right)], keep_left, keep_right, *inputs[4:], spec=pl.BlockSpec(), weight=200
    )
    replicas = nz * PAIR * CORES
    inputs = [*inputs[:4], outer_weight, outer_momentum]
    (share_rows,) = small_call(
        functools.partial(share_kernel, replicas),
        [jax.ShapeDtypeStruct((share, kv), bf16)],
        *inputs,
        spec=pl.BlockSpec(),
    )
    share_rows, *inputs = lax.optimization_barrier((share_rows, *inputs))
    new_outer, new_momentum = small_call(
        functools.partial(state_kernel, replicas),
        [jax.ShapeDtypeStruct((share, kv), f32)] * 2,
        *inputs,
        spec=pl.BlockSpec(),
        weight=1 << 17,
    )
    share_rows, *held = lax.optimization_barrier((share_rows, *[mine[e] for e in late]))
    mine.update(zip(late, held))
    for e in late:
        send_next(*e)

    rows = {}
    for m in sorted(range(1, nz), key=lambda m: (m & (m - 1)).bit_count() * nz - m):
        low = m & -m
        pieces = [share_rows] if m == low else list(rows[m ^ low])
        if m == nz - 1:
            pieces[0], new_outer = lax.optimization_barrier((pieces[0], new_outer))
        rows[m] = [lax.ppermute(piece, "z", [(i, i ^ low) for i in range(nz)]) for piece in pieces]
    rows = [[share_rows]] + [rows[m] for m in range(1, nz)]
    input_grad = join(parts, [((f + s) % fsdp) * width for s in range(fsdp)])

    half = len(far) // CORES
    near, away = [nexts[e] for e in far[:half]], [nexts[e] for e in far[half:]]
    give, keep = keys_part(away + near, rows[:-1], 0, outs=2)
    give, keep, input_grad = lax.optimization_barrier((give, keep, input_grad))
    last = (nz - 1) * share
    (give,) = keys_part(away, rows[-1:], last, [give])
    (keep,) = keys_part(near, rows[-1:], last, [keep])
    came = lax.ppermute(give, "core", swap)
    shape = lambda n, kind: jax.ShapeDtypeStruct((n, kv // 2), kind)
    to_x, stay_x, stay_f, *to_f = small_call(
        functools.partial(core_sum_kernel, fsdp, tok),
        [shape(fsdp * tok, bf16), shape(fsdp * tok, f32), shape(PAIR * tok, f32)] + [shape(PAIR * tok, bf16)] * (fsdp - 1),
        keep,
        came,
    )

    def home(to_x, to_f):
        from_x = lax.ppermute(to_x, "x", ring(PAIR, 1))
        return [from_x] + [lax.ppermute(part, "fsdp", ring(fsdp, -s - 1)) for s, part in enumerate(to_f)]

    left, right, to_x, *to_f = small_call(
        functools.partial(second_sum_kernel, fsdp, tok),
        [shape(tok, f32)] * 2 + [shape(tok, bf16)] * fsdp,
        stay_x,
        stay_f,
        *home(to_x, to_f),
    )
    (keys,) = small_call(
        last_sum_kernel, [jax.ShapeDtypeStruct((tok, kv), bf16)], left, right, *home(to_x, to_f)
    )
    return (input_grad, keys, new_outer, new_momentum)


def solution(mesh):
    fsdp = mesh.shape["fsdp"]
    nz = mesh.shape["island"] // (PAIR * CORES)
    split = Mesh(mesh.devices.reshape(nz, PAIR, CORES, fsdp), ("z", "x", "core", "fsdp"))
    island = ("z", "x", "core")
    tokens = P(island + ("fsdp",), None)
    width = P(("fsdp",) + island, None)
    in_specs = (tokens, tokens, P(island, "fsdp", None), width, width, tokens)
    out_specs = (tokens, tokens, width, width)
    return jax.shard_map(local, mesh=split, in_specs=in_specs, out_specs=out_specs, check_vma=False)
```

```python
import functools

import jax
import jax.numpy as jnp
from jax import lax
from jax.experimental import pallas as pl
from jax.experimental.pallas import tpu as pltpu
from jax.sharding import Mesh, PartitionSpec as P

inner_rate = 1.2
outer_rate = 0.7
nesterov = 0.9
CORES = 2
PAIR = 2
LANES = 128

bf16, f32 = jnp.bfloat16, jnp.float32
VMEM, HBM = pl.BlockSpec(memory_space=pltpu.VMEM), pl.BlockSpec(memory_space=pltpu.HBM)
SMEM, ANY = pl.BlockSpec(memory_space=pltpu.SMEM), pl.BlockSpec(memory_space=pl.ANY)
MIB = 1024 * 1024


def ring(count, shift):
    return [(i, (i + shift) % count) for i in range(count)]


def strip(axis, start, size):
    return (pl.ds(start, size), slice(None)) if axis == 0 else (slice(None), pl.ds(start, size))


def in_hbm(array):
    return pltpu.with_memory_space_constraint(array, pltpu.HBM)


def pack_kernel(plan, starts, *refs):
    sources, outs, done = refs[: len(plan)], refs[len(plan) : -1], refs[-1]
    copies, o = [], 0
    for source, (axis, size, counts) in zip(sources, plan):
        for count in counts:
            for i in range(count):
                n = len(copies)
                part = source.at[strip(axis, pl.multiple_of(starts[n], size), size)]
                copies.append(pltpu.make_async_copy(part, outs[o].at[strip(axis, i * size, size)], done.at[n]))
            o += 1
    for copy in copies:
        copy.start()
    for copy in copies:
        copy.wait()


def pack(items, after=(), target=jax.ShapeDtypeStruct):
    result, rest = {}, []
    for n, (array, axis, size, groups) in enumerate(items):
        if axis == 1 and size % LANES:
            strips = [[lax.dynamic_slice_in_dim(array, at, size, axis=axis) for at in group] for group in groups]
            result[n] = [jnp.concatenate(group, axis=axis) for group in strips]
        else:
            rest.append((n, array, axis, size, groups))
    if not rest:
        return [result[n] for n in range(len(items))], list(after)
    starts = jnp.stack([at for item in rest for group in item[4] for at in group]).astype(jnp.int32)
    if after:
        starts, *after = lax.optimization_barrier((starts, *after))
    plan, shapes = [], []
    for _, array, axis, size, groups in rest:
        counts = [len(group) for group in groups]
        plan.append((axis, size, counts))
        for n in counts:
            shape = (n * size, array.shape[1]) if axis == 0 else (array.shape[0], n * size)
            shapes.append(target(shape, array.dtype))
    moved = 4 * starts.shape[0] * 1024 * LANES
    outs = pl.pallas_call(
        functools.partial(pack_kernel, plan),
        out_shape=shapes,
        in_specs=[SMEM] + [HBM] * len(rest),
        out_specs=[pl.BlockSpec()] * len(shapes),
        scratch_shapes=[pltpu.SemaphoreType.DMA((starts.shape[0],))],
        compiler_params=pltpu.CompilerParams(vmem_limit_bytes=16 * MIB),
        cost_estimate=pl.CostEstimate(flops=0, bytes_accessed=moved, transcendentals=0),
    )(starts, *[in_hbm(item[1]) for item in rest])
    for n, *_, groups in rest:
        result[n], outs = outs[: len(groups)], outs[len(groups) :]
    return [result[n] for n in range(len(items))], list(after)


def inner_kernel(pieces, share, scale, act_at, place, *refs):
    acts, cots = refs[:pieces], refs[pieces : 2 * pieces]
    own, other, to_x, stay_x, to_z, stay_z, left, right, rows, total, done = refs[2 * pieces :]
    tok, kv = cots[0].shape
    strips = 2 * PAIR
    copies = []

    def fetch(source, target):
        copies.append(pltpu.make_async_copy(source, target, done.at[len(copies)]))

    for n, (act, cot) in enumerate(zip(acts, cots)):
        here = pl.ds(n * tok, tok)
        fetch(act.at[:, pl.ds(act_at, strips * share)], left.at[here, :])
        fetch(cot, right.at[here, :])
    for i in range(strips):
        strip_rows = pl.ds(pl.multiple_of(place[i] * share, share), share)
        here = pl.ds(i * share, share)
        fetch(own.at[strip_rows, :], rows.at[0, here, :])
        fetch(other.at[strip_rows, :], rows.at[1, here, :])
    for copy in copies:
        copy.start()
    for copy in copies[: 2 * pieces]:
        copy.wait()
    total[...] = lax.dot_general(left[...], right[...], (((0,), (0,)), ((), ())), preferred_element_type=f32)
    for copy in copies[2 * pieces :]:
        copy.wait()

    def inner_new(i, columns):
        here = slice(i * share, (i + 1) * share)
        return (rows[0, here, columns].astype(f32) + rows[1, here, columns].astype(f32)) - scale * total[here, columns]

    first, second = slice(0, to_x.shape[1]), slice(to_x.shape[1], kv)
    for n in range(2):
        here = slice(n * share, (n + 1) * share)
        to_x[here, :] = inner_new(PAIR * n + 1, first).astype(bf16)
        to_z[here, :] = inner_new(n, second).astype(bf16)
    for n in range(2):
        here = slice(n * share, (n + 1) * share)
        stay_x[here, :] = inner_new(PAIR * n, first)
        stay_z[here, :] = inner_new(PAIR + n, second)


def inner_blocks(place, acts, act_at, cots, own, other, share, cut):
    pieces = len(acts)
    tok, kv = cots[0].shape
    rows = 2 * PAIR * share
    if act_at % LANES or rows % LANES:
        acts, act_at = [a[:, act_at : act_at + rows] for a in acts], 0
    shapes = [jax.ShapeDtypeStruct((2 * share, wide), kind) for wide in (cut, kv - cut) for kind in (bf16, f32)]
    return pl.pallas_call(
        functools.partial(inner_kernel, pieces, share, inner_rate / (tok * pieces // CORES), act_at),
        out_shape=shapes,
        in_specs=[SMEM] + [ANY] * (2 * pieces) + [HBM, ANY],
        out_specs=[pl.BlockSpec()] * 4,
        scratch_shapes=[
            pltpu.VMEM((pieces * tok, rows), bf16),
            pltpu.VMEM((pieces * tok, kv), bf16),
            pltpu.VMEM((CORES, rows, kv), bf16),
            pltpu.VMEM((rows, kv), f32),
            pltpu.SemaphoreType.DMA((2 * pieces + 2 * CORES * PAIR,)),
        ],
        compiler_params=pltpu.CompilerParams(vmem_limit_bytes=32 * MIB),
        cost_estimate=pl.CostEstimate(flops=pieces * tok * share * kv, bytes_accessed=share * kv, transcendentals=0),
    )(place, *acts, *cots, in_hbm(own), other)


def middle_kernel(share, stay_x, from_x, stay_z, from_z, to_z, keep_left, to_x, keep_right):
    over_x = stay_x[...] + from_x[...].astype(f32)
    over_z = stay_z[...] + from_z[...].astype(f32)
    to_z[...] = over_x[:share].astype(bf16)
    to_x[...] = over_z[share:].astype(bf16)
    keep_left[...] = over_x[share:]
    keep_right[...] = over_z[:share]


def block_sum(keep_left, from_z, keep_right, from_x, came):
    left = keep_left[...] + from_z[...].astype(f32)
    right = keep_right[...] + from_x[...].astype(f32)
    total = jnp.concatenate([left, right], axis=1)
    for other in came:
        total = total + other[...].astype(f32)
    return total


def gather_kernel(keep_left, keep_right, *refs):
    *came, left, right = refs
    total = jnp.concatenate([keep_left[...], keep_right[...]], axis=1)
    for other in came:
        total = total + other[...].astype(f32)
    left[...] = total[:, : left.shape[1]]
    right[...] = total[:, left.shape[1] :]


def block_kernel(*refs):
    *inputs, out = refs
    out[...] = block_sum(*inputs[:4], inputs[4:]).astype(bf16)


def outer_step(replicas, inputs, weight, momentum):
    pseudo_grad = weight[...] - block_sum(*inputs[:4], inputs[4:]) / replicas
    moment = nesterov * momentum[...] + pseudo_grad
    return weight[...] - outer_rate * (pseudo_grad + nesterov * moment), moment


def share_kernel(replicas, *refs):
    *inputs, weight, momentum, share = refs
    share[...] = outer_step(replicas, inputs, weight, momentum)[0].astype(bf16)


def state_kernel(replicas, *refs):
    *inputs, weight, momentum, new_outer, new_momentum = refs
    new_outer[...], new_momentum[...] = outer_step(replicas, inputs, weight, momentum)


def keys_kernel(acts_count, counts, at, *refs):
    acts, refs = refs[:acts_count], refs[acts_count:]
    blocks = []
    for count in counts:
        blocks.append(jnp.concatenate([w[...] for w in refs[:count]], axis=1))
        refs = refs[count:]
    weight = jnp.concatenate(blocks, axis=0)
    before, outs = (refs[:1], refs[1:]) if at else ([], refs)
    each = acts_count // len(outs)
    for n, out in enumerate(outs):
        left = jnp.concatenate([a[:, at : at + weight.shape[0]] for a in acts[n * each : (n + 1) * each]], axis=0)
        product = jnp.dot(left, weight, preferred_element_type=f32)
        out[...] = (before[0][...] + product if at else product).astype(out.dtype)


def keys_part(acts, blocks, at, before=(), outs=1, kind=f32):
    rows, kv = len(acts) * acts[0].shape[0] // outs, sum(w.shape[1] for w in blocks[0])
    depth = sum(block[0].shape[0] for block in blocks)
    if at % LANES:
        return [(before[0] + keys_part([a[:, at:] for a in acts], blocks, 0)[0]).astype(kind)]
    pieces = [w for block in blocks for w in block]
    flops = rows * depth * kv if at else 1 << 34
    return pl.pallas_call(
        functools.partial(keys_kernel, len(acts), [len(block) for block in blocks], at),
        out_shape=[jax.ShapeDtypeStruct((rows, kv), kind)] * outs,
        in_specs=[pl.BlockSpec()] * (len(acts) + len(pieces) + len(before)),
        out_specs=[pl.BlockSpec()] * outs,
        compiler_params=pltpu.CompilerParams(vmem_limit_bytes=32 * MIB),
        cost_estimate=pl.CostEstimate(flops=flops, bytes_accessed=rows * kv, transcendentals=0),
    )(*acts, *pieces, *before)


def core_sum_kernel(fsdp, tok, keep, came, to_x, stay_x, stay_f, *to_f):
    half = keep.shape[1] // 2
    total = keep[...] + came[...].astype(f32)
    rows = fsdp * tok
    stay_x[...] = total[:rows, :half]
    to_x[...] = total[rows:, :half].astype(bf16)
    for i in range(PAIR):
        here = slice(i * tok, (i + 1) * tok)
        stay_f[here, :] = total[i * rows : i * rows + tok, half:]
        for s in range(1, fsdp):
            to_f[s - 1][here, :] = total[i * rows + s * tok : i * rows + (s + 1) * tok, half:].astype(bf16)


def second_sum_kernel(fsdp, tok, *refs):
    stay_x, stay_f, from_x, *from_f = refs[: fsdp + 2]
    left, right, to_x, *to_f = refs[fsdp + 2 :]
    first = stay_x[...] + from_x[...].astype(f32)
    left[...] = first[:tok]
    for s in range(1, fsdp):
        to_f[s - 1][...] = first[s * tok : (s + 1) * tok].astype(bf16)
    second = stay_f[...]
    for came in from_f:
        second = second + came[...].astype(f32)
    right[...] = second[:tok]
    to_x[...] = second[tok:].astype(bf16)


def last_sum_kernel(left, right, from_x, *refs):
    *from_f, keys = refs
    half = left.shape[1]
    first = left[...]
    for came in from_f:
        first = first + came[...].astype(f32)
    keys[:, :half] = first.astype(bf16)
    keys[:, half:] = (right[...] + from_x[...].astype(f32)).astype(bf16)


def small_call(kernel, shapes, *args, spec=VMEM, weight=1):
    size = weight * sum(shape.size for shape in shapes)
    return pl.pallas_call(
        kernel,
        out_shape=shapes,
        in_specs=[spec] * len(args),
        out_specs=[spec] * len(shapes),
        compiler_params=pltpu.CompilerParams(vmem_limit_bytes=24 * MIB),
        cost_estimate=pl.CostEstimate(flops=size // 8, bytes_accessed=size // 8, transcendentals=0),
    )(*args)


def join_kernel(starts, *refs):
    *parts, out, done = refs
    copies = []
    for n, part in enumerate(parts):
        width = part.shape[1]
        here = out.at[:, pl.ds(pl.multiple_of(starts[n], width), width)]
        copies.append(pltpu.make_async_copy(part.at[: out.shape[0], :], here, done.at[n]))
    for copy in copies:
        copy.start()
    for copy in copies:
        copy.wait()


def join(parts, starts):
    rows, width = parts[-1].shape
    return pl.pallas_call(
        join_kernel,
        out_shape=jax.ShapeDtypeStruct((rows, width * len(parts)), parts[0].dtype),
        in_specs=[SMEM] + [VMEM] * len(parts),
        out_specs=HBM,
        scratch_shapes=[pltpu.SemaphoreType.DMA((len(parts),))],
        compiler_params=pltpu.CompilerParams(vmem_limit_bytes=16 * MIB),
        cost_estimate=pl.CostEstimate(flops=0, bytes_accessed=4 * rows * width * len(parts), transcendentals=0),
    )(jnp.stack(starts).astype(jnp.int32), *parts)


def local(activations, cotangent, inner_weight, outer_weight, outer_momentum, next_activations):
    fsdp, nz = lax.axis_size("fsdp"), lax.axis_size("z")
    f, z, x, c = (lax.axis_index(a) for a in ("fsdp", "z", "x", "core"))
    tok, d = activations.shape
    kv = cotangent.shape[1]
    width = d // fsdp
    block = width // nz
    share = block // (PAIR * CORES)
    own_weight = inner_weight[0]
    swap = ring(CORES, 1)

    def column(b, i, k, s):
        return ((f + s) % fsdp) * width + b * block + i * CORES * share + ((c + k) % CORES) * share

    def pair_ring(k, s):
        at = lambda i, j: (i % CORES) * fsdp + j % fsdp
        return [(at(i, j), at(i + k, j + s)) for i in range(CORES) for j in range(fsdp)]

    shifts = [(k, s) for s in range(fsdp) for k in range(CORES)]
    stages = [(m + 1, m) for m in range(nz - 2, -1, -2)]

    far = [(i, k, s) for k in range(CORES) for i in range(PAIR) for s in range(fsdp)]
    early = [(0, 1, 0)]
    late = [e for e in far if e not in early]
    index = lambda i, k, s: ((i % PAIR) * CORES + k % CORES) * fsdp + s % fsdp
    every = [(i, k, s) for i in range(PAIR) for k in range(CORES) for s in range(fsdp)]
    mine, nexts = {}, {}

    def next_groups(places):
        return [[column(z ^ m, (x + i) % PAIR, k, s) for m in range(nz)] for i, k, s in places]

    def send_next(i, k, s):
        pairs = [(index(*e), index(e[0] + i, e[1] + k, e[2] + s)) for e in every]
        nexts[i, k, s] = lax.ppermute(mine[i, k, s], ("x", "core", "fsdp"), pairs) if i or k or s else mine[i, k, s]

    cots = {(0, 0): cotangent}
    for s in range(1, fsdp):
        cots[0, s] = lax.ppermute(cotangent, "fsdp", ring(fsdp, s))
    columns = [[column(z ^ m, (x + i) % PAIR, k, s) for m in ms for i in range(PAIR)] for ms in stages for k, s in shifts]
    (packed,), _ = pack([(activations, 1, share, columns)])
    acts = []
    for stage in range(len(stages)):
        came = []
        for (k, s), part in zip(shifts, packed[stage * len(shifts) :]):
            came.append(part if (k, s) == (0, 0) else lax.ppermute(part, ("core", "fsdp"), pair_ring(k, s)))
        acts.append(came)
    other_weight = lax.ppermute(own_weight, "core", swap)
    cots[1, 0] = lax.ppermute(cotangent, "core", swap)
    for s in range(1, fsdp):
        cots[1, s] = lax.ppermute(cots[0, s], "core", swap)

    wanted = [cots[0, s] for s in range(1, fsdp)]
    (parts,), wanted = pack([(next_activations, 1, share, next_groups(far))], wanted, pltpu.HBM)
    cots.update({(0, s): got for s, got in enumerate(wanted, 1)})
    mine.update(zip(far, parts))

    ordered = [cots[k, s] for k, s in shifts]
    across_x, across_z = ring(PAIR, 1), [(i, i ^ 1) for i in range(nz)]
    over_z = {}

    def finish(m, to_z, to_x, keep_left, keep_right):
        from_z, from_x = lax.ppermute(to_z, "z", across_z), lax.ppermute(to_x, "x", across_x)
        return [keep_left, from_z, keep_right, from_x] + over_z.get(m, [])

    for stage, ms in enumerate(stages):
        cut = kv // 2 if ms[1] else 3 * kv // 4
        blocks = [((z ^ m) * PAIR + (x + i) % PAIR) * CORES + c for m in ms for i in range(PAIR)]
        place = jnp.stack(blocks).astype(jnp.int32)
        if not stage:
            place, *held = lax.optimization_barrier((place, *[mine[e] for e in far]))
            mine.update(zip(far, held))
            for e in early:
                send_next(*e)
        if stage:
            place, to_z, to_x = lax.optimization_barrier((place, to_z, to_x))
            m = stages[stage - 1][1]
            inputs = finish(m, to_z, to_x, keep_left, keep_right)
            low = m & -m
        to_x, stay_x, to_z, stay_z = inner_blocks(place, acts[stage], 0, ordered, own_weight, other_weight, share, cut)
        if stage:
            to_x, to_z, inputs[1], inputs[3] = lax.optimization_barrier((to_x, to_z, inputs[1], inputs[3]))
            (block_total,) = small_call(
                block_kernel, [jax.ShapeDtypeStruct((share, kv), bf16)], *inputs, spec=pl.BlockSpec()
            )
            over_z.setdefault(m ^ low, []).append(lax.ppermute(block_total, "z", [(i, i ^ low) for i in range(nz)]))
        if not stage:
            stay_x, *island_cots = lax.optimization_barrier((stay_x, *[cots[0, s] for s in range(fsdp)]))
            grad_rows = lax.dot_general(
                jnp.concatenate(island_cots, axis=0), own_weight, (((1,), (1,)), ((), ())), preferred_element_type=f32
            ).astype(bf16)
            parts = [grad_rows] + [grad_rows[s * tok : (s + 1) * tok] for s in range(1, fsdp)]
            stay_x, *parts = lax.optimization_barrier((stay_x, *parts))
            for s in range(1, fsdp):
                parts[s] = lax.ppermute(parts[s], "fsdp", ring(fsdp, -s))
        from_x, from_z = lax.ppermute(to_x, "x", across_x), lax.ppermute(to_z, "z", across_z)
        to_z, keep_left, to_x, keep_right = small_call(
            functools.partial(middle_kernel, share),
            [jax.ShapeDtypeStruct((share, wide), kind) for wide in (cut, kv - cut) for kind in (bf16, f32)],
            stay_x,
            from_x,
            stay_z,
            from_z,
            spec=pl.BlockSpec(),
        )

    inputs = finish(0, to_z, to_x, keep_left, keep_right)
    inputs[0], inputs[2] = small_call(
        gather_kernel, [jax.ShapeDtypeStruct(part.shape, f32) for part in (keep_left, keep_right)], keep_left, keep_right, *inputs[4:], spec=pl.BlockSpec(), weight=200
    )
    inputs[0], *held = lax.optimization_barrier((inputs[0], *[nexts[e] for e in early]))
    nexts.update(zip(early, held))
    replicas = nz * PAIR * CORES
    inputs = [*inputs[:4], outer_weight, outer_momentum]
    (share_rows,) = small_call(
        functools.partial(share_kernel, replicas),
        [jax.ShapeDtypeStruct((share, kv), bf16)],
        *inputs,
        spec=pl.BlockSpec(),
    )
    share_rows, *inputs = lax.optimization_barrier((share_rows, *inputs))
    new_outer, new_momentum = small_call(
        functools.partial(state_kernel, replicas),
        [jax.ShapeDtypeStruct((share, kv), f32)] * 2,
        *inputs,
        spec=pl.BlockSpec(),
        weight=1 << 17,
    )
    share_rows, *held = lax.optimization_barrier((share_rows, *[mine[e] for e in late]))
    mine.update(zip(late, held))
    for e in late:
        send_next(*e)

    rows = {}
    for m in sorted(range(1, nz), key=lambda m: (m & (m - 1)).bit_count() * nz - m):
        low = m & -m
        pieces = [share_rows] if m == low else list(rows[m ^ low])
        if m == nz - 1:
            pieces[0], new_outer = lax.optimization_barrier((pieces[0], new_outer))
        rows[m] = [lax.ppermute(piece, "z", [(i, i ^ low) for i in range(nz)]) for piece in pieces]
    rows = [[share_rows]] + [rows[m] for m in range(1, nz)]
    input_grad = join(parts, [((f + s) % fsdp) * width for s in range(fsdp)])

    half = len(far) // CORES
    near, away = [nexts[e] for e in far[:half]], [nexts[e] for e in far[half:]]
    give, keep = keys_part(away + near, rows[:-1], 0, outs=2)
    give, keep, input_grad = lax.optimization_barrier((give, keep, input_grad))
    last = (nz - 1) * share
    (give,) = keys_part(away, rows[-1:], last, [give], kind=bf16)
    (keep,) = keys_part(near, rows[-1:], last, [keep])
    came = lax.ppermute(give, "core", swap)
    shape = lambda n, kind: jax.ShapeDtypeStruct((n, kv // 2), kind)
    to_x, stay_x, stay_f, *to_f = small_call(
        functools.partial(core_sum_kernel, fsdp, tok),
        [shape(fsdp * tok, bf16), shape(fsdp * tok, f32), shape(PAIR * tok, f32)] + [shape(PAIR * tok, bf16)] * (fsdp - 1),
        keep,
        came,
    )

    def home(to_x, to_f):
        from_x = lax.ppermute(to_x, "x", ring(PAIR, 1))
        return [from_x] + [lax.ppermute(part, "fsdp", ring(fsdp, -s - 1)) for s, part in enumerate(to_f)]

    left, right, to_x, *to_f = small_call(
        functools.partial(second_sum_kernel, fsdp, tok),
        [shape(tok, f32)] * 2 + [shape(tok, bf16)] * fsdp,
        stay_x,
        stay_f,
        *home(to_x, to_f),
    )
    (keys,) = small_call(
        last_sum_kernel, [jax.ShapeDtypeStruct((tok, kv), bf16)], left, right, *home(to_x, to_f)
    )
    return (input_grad, keys, new_outer, new_momentum)


def solution(mesh):
    fsdp = mesh.shape["fsdp"]
    nz = mesh.shape["island"] // (PAIR * CORES)
    split = Mesh(mesh.devices.reshape(nz, PAIR, CORES, fsdp), ("z", "x", "core", "fsdp"))
    island = ("z", "x", "core")
    tokens = P(island + ("fsdp",), None)
    width = P(("fsdp",) + island, None)
    in_specs = (tokens, tokens, P(island, "fsdp", None), width, width, tokens)
    out_specs = (tokens, tokens, width, width)
    return jax.shard_map(local, mesh=split, in_specs=in_specs, out_specs=out_specs, check_vma=False)
```

```python
import functools

import jax
import jax.numpy as jnp
from jax import lax
from jax.experimental import pallas as pl
from jax.experimental.pallas import tpu as pltpu
from jax.sharding import Mesh, PartitionSpec as P

inner_rate = 1.2
outer_rate = 0.7
nesterov = 0.9
CORES = 2
PAIR = 2
LANES = 128

bf16, f32 = jnp.bfloat16, jnp.float32
VMEM, HBM = pl.BlockSpec(memory_space=pltpu.VMEM), pl.BlockSpec(memory_space=pltpu.HBM)
SMEM, ANY = pl.BlockSpec(memory_space=pltpu.SMEM), pl.BlockSpec(memory_space=pl.ANY)
MIB = 1024 * 1024


def ring(count, shift):
    return [(i, (i + shift) % count) for i in range(count)]


def strip(axis, start, size):
    return (pl.ds(start, size), slice(None)) if axis == 0 else (slice(None), pl.ds(start, size))


def in_hbm(array):
    return pltpu.with_memory_space_constraint(array, pltpu.HBM)


def pack_kernel(plan, starts, *refs):
    sources, outs, done = refs[: len(plan)], refs[len(plan) : -1], refs[-1]
    copies, o = [], 0
    for source, (axis, size, counts) in zip(sources, plan):
        for count in counts:
            for i in range(count):
                n = len(copies)
                part = source.at[strip(axis, pl.multiple_of(starts[n], size), size)]
                copies.append(pltpu.make_async_copy(part, outs[o].at[strip(axis, i * size, size)], done.at[n]))
            o += 1
    for copy in copies:
        copy.start()
    for copy in copies:
        copy.wait()


def pack(items, after=(), target=jax.ShapeDtypeStruct):
    result, rest = {}, []
    for n, (array, axis, size, groups) in enumerate(items):
        if axis == 1 and size % LANES:
            strips = [[lax.dynamic_slice_in_dim(array, at, size, axis=axis) for at in group] for group in groups]
            result[n] = [jnp.concatenate(group, axis=axis) for group in strips]
        else:
            rest.append((n, array, axis, size, groups))
    if not rest:
        return [result[n] for n in range(len(items))], list(after)
    starts = jnp.stack([at for item in rest for group in item[4] for at in group]).astype(jnp.int32)
    if after:
        starts, *after = lax.optimization_barrier((starts, *after))
    plan, shapes = [], []
    for _, array, axis, size, groups in rest:
        counts = [len(group) for group in groups]
        plan.append((axis, size, counts))
        for n in counts:
            shape = (n * size, array.shape[1]) if axis == 0 else (array.shape[0], n * size)
            shapes.append(target(shape, array.dtype))
    moved = 4 * starts.shape[0] * 1024 * LANES
    outs = pl.pallas_call(
        functools.partial(pack_kernel, plan),
        out_shape=shapes,
        in_specs=[SMEM] + [HBM] * len(rest),
        out_specs=[pl.BlockSpec()] * len(shapes),
        scratch_shapes=[pltpu.SemaphoreType.DMA((starts.shape[0],))],
        compiler_params=pltpu.CompilerParams(vmem_limit_bytes=16 * MIB),
        cost_estimate=pl.CostEstimate(flops=0, bytes_accessed=moved, transcendentals=0),
    )(starts, *[in_hbm(item[1]) for item in rest])
    for n, *_, groups in rest:
        result[n], outs = outs[: len(groups)], outs[len(groups) :]
    return [result[n] for n in range(len(items))], list(after)


def inner_kernel(pieces, share, scale, act_at, place, *refs):
    acts, cots = refs[:pieces], refs[pieces : 2 * pieces]
    own, other, to_x, stay_x, to_z, stay_z, left, right, rows, total, done = refs[2 * pieces :]
    tok, kv = cots[0].shape
    strips = 2 * PAIR
    copies = []

    def fetch(source, target):
        copies.append(pltpu.make_async_copy(source, target, done.at[len(copies)]))

    for n, (act, cot) in enumerate(zip(acts, cots)):
        here = pl.ds(n * tok, tok)
        fetch(act.at[:, pl.ds(act_at, strips * share)], left.at[here, :])
        fetch(cot, right.at[here, :])
    for i in range(strips):
        strip_rows = pl.ds(pl.multiple_of(place[i] * share, share), share)
        here = pl.ds(i * share, share)
        fetch(own.at[strip_rows, :], rows.at[0, here, :])
        fetch(other.at[strip_rows, :], rows.at[1, here, :])
    for copy in copies:
        copy.start()
    for copy in copies[: 2 * pieces]:
        copy.wait()
    total[...] = lax.dot_general(left[...], right[...], (((0,), (0,)), ((), ())), preferred_element_type=f32)
    for copy in copies[2 * pieces :]:
        copy.wait()

    def inner_new(i, columns):
        here = slice(i * share, (i + 1) * share)
        return (rows[0, here, columns].astype(f32) + rows[1, here, columns].astype(f32)) - scale * total[here, columns]

    first, second = slice(0, to_x.shape[1]), slice(to_x.shape[1], kv)
    for n in range(2):
        here = slice(n * share, (n + 1) * share)
        to_x[here, :] = inner_new(PAIR * n + 1, first).astype(bf16)
        to_z[here, :] = inner_new(n, second).astype(bf16)
    for n in range(2):
        here = slice(n * share, (n + 1) * share)
        stay_x[here, :] = inner_new(PAIR * n, first)
        stay_z[here, :] = inner_new(PAIR + n, second)


def inner_blocks(place, acts, act_at, cots, own, other, share, cut):
    pieces = len(acts)
    tok, kv = cots[0].shape
    rows = 2 * PAIR * share
    if act_at % LANES or rows % LANES:
        acts, act_at = [a[:, act_at : act_at + rows] for a in acts], 0
    shapes = [jax.ShapeDtypeStruct((2 * share, wide), kind) for wide in (cut, kv - cut) for kind in (bf16, f32)]
    return pl.pallas_call(
        functools.partial(inner_kernel, pieces, share, inner_rate / (tok * pieces // CORES), act_at),
        out_shape=shapes,
        in_specs=[SMEM] + [ANY] * (2 * pieces) + [HBM, ANY],
        out_specs=[pl.BlockSpec()] * 4,
        scratch_shapes=[
            pltpu.VMEM((pieces * tok, rows), bf16),
            pltpu.VMEM((pieces * tok, kv), bf16),
            pltpu.VMEM((CORES, rows, kv), bf16),
            pltpu.VMEM((rows, kv), f32),
            pltpu.SemaphoreType.DMA((2 * pieces + 2 * CORES * PAIR,)),
        ],
        compiler_params=pltpu.CompilerParams(vmem_limit_bytes=32 * MIB),
        cost_estimate=pl.CostEstimate(flops=pieces * tok * share * kv, bytes_accessed=share * kv, transcendentals=0),
    )(place, *acts, *cots, in_hbm(own), other)


def middle_kernel(share, stay_x, from_x, stay_z, from_z, to_z, keep_left, to_x, keep_right):
    over_x = stay_x[...] + from_x[...].astype(f32)
    over_z = stay_z[...] + from_z[...].astype(f32)
    to_z[...] = over_x[:share].astype(bf16)
    to_x[...] = over_z[share:].astype(bf16)
    keep_left[...] = over_x[share:]
    keep_right[...] = over_z[:share]


def block_sum(keep_left, from_z, keep_right, from_x, came):
    left = keep_left[...] + from_z[...].astype(f32)
    right = keep_right[...] + from_x[...].astype(f32)
    total = jnp.concatenate([left, right], axis=1)
    for other in came:
        total = total + other[...].astype(f32)
    return total


def gather_kernel(keep_left, keep_right, *refs):
    *came, left, right = refs
    total = jnp.concatenate([keep_left[...], keep_right[...]], axis=1)
    for other in came:
        total = total + other[...].astype(f32)
    left[...] = total[:, : left.shape[1]]
    right[...] = total[:, left.shape[1] :]


def block_kernel(*refs):
    *inputs, out = refs
    out[...] = block_sum(*inputs[:4], inputs[4:]).astype(bf16)


def outer_step(replicas, inputs, weight, momentum):
    pseudo_grad = weight[...] - block_sum(*inputs[:4], inputs[4:]) / replicas
    moment = nesterov * momentum[...] + pseudo_grad
    return weight[...] - outer_rate * (pseudo_grad + nesterov * moment), moment


def share_kernel(replicas, *refs):
    *inputs, weight, momentum, share = refs
    share[...] = outer_step(replicas, inputs, weight, momentum)[0].astype(bf16)


def state_kernel(replicas, *refs):
    *inputs, weight, momentum, new_outer, new_momentum = refs
    new_outer[...], new_momentum[...] = outer_step(replicas, inputs, weight, momentum)


def keys_kernel(orders, counts, at, *refs):
    acts_count = sum(len(order) for order in orders)
    acts, refs = refs[:acts_count], refs[acts_count:]
    blocks = []
    for count in counts:
        blocks.append(jnp.concatenate([w[...] for w in refs[:count]], axis=1))
        refs = refs[count:]
    weight = jnp.concatenate(blocks, axis=0)
    before, outs = (refs[:1], refs[1:]) if at else ([], refs)
    for order, out in zip(orders, outs):
        left = jnp.concatenate([acts[n][:, at : at + weight.shape[0]] for n in order], axis=0)
        product = jnp.dot(left, weight, preferred_element_type=f32)
        out[...] = (before[0][...] + product if at else product).astype(out.dtype)


def keys_part(acts, blocks, at, before=(), orders=None, kind=f32):
    orders = orders or [list(range(len(acts)))]
    outs = len(orders)
    rows, kv = len(acts) * acts[0].shape[0] // outs, sum(w.shape[1] for w in blocks[0])
    depth = sum(block[0].shape[0] for block in blocks)
    if at % LANES:
        return [(before[0] + keys_part([a[:, at:] for a in acts], blocks, 0)[0]).astype(kind)]
    pieces = [w for block in blocks for w in block]
    flops = rows * depth * kv if at else 1 << 34
    return pl.pallas_call(
        functools.partial(keys_kernel, orders, [len(block) for block in blocks], at),
        out_shape=[jax.ShapeDtypeStruct((rows, kv), kind)] * outs,
        in_specs=[pl.BlockSpec()] * (len(acts) + len(pieces) + len(before)),
        out_specs=[pl.BlockSpec()] * outs,
        compiler_params=pltpu.CompilerParams(vmem_limit_bytes=32 * MIB),
        cost_estimate=pl.CostEstimate(flops=flops, bytes_accessed=rows * kv, transcendentals=0),
    )(*acts, *pieces, *before)


def core_sum_kernel(fsdp, tok, keep, came, to_x, stay_x, stay_f, *to_f):
    half = keep.shape[1] // 2
    total = keep[...] + came[...].astype(f32)
    rows = fsdp * tok
    stay_x[...] = total[:rows, :half]
    to_x[...] = total[rows:, :half].astype(bf16)
    for i in range(PAIR):
        here = slice(i * tok, (i + 1) * tok)
        stay_f[here, :] = total[i * rows : i * rows + tok, half:]
        for s in range(1, fsdp):
            to_f[s - 1][here, :] = total[i * rows + s * tok : i * rows + (s + 1) * tok, half:].astype(bf16)


def second_sum_kernel(fsdp, tok, *refs):
    stay_x, stay_f, from_x, *from_f = refs[: fsdp + 2]
    left, right, to_x, *to_f = refs[fsdp + 2 :]
    first = stay_x[...] + from_x[...].astype(f32)
    left[...] = first[:tok]
    for s in range(1, fsdp):
        to_f[s - 1][...] = first[s * tok : (s + 1) * tok].astype(bf16)
    second = stay_f[...]
    for came in from_f:
        second = second + came[...].astype(f32)
    right[...] = second[:tok]
    to_x[...] = second[tok:].astype(bf16)


def last_sum_kernel(left, right, from_x, *refs):
    *from_f, keys = refs
    half = left.shape[1]
    first = left[...]
    for came in from_f:
        first = first + came[...].astype(f32)
    keys[:, :half] = first.astype(bf16)
    keys[:, half:] = (right[...] + from_x[...].astype(f32)).astype(bf16)


def small_call(kernel, shapes, *args, spec=VMEM, weight=1):
    size = weight * sum(shape.size for shape in shapes)
    return pl.pallas_call(
        kernel,
        out_shape=shapes,
        in_specs=[spec] * len(args),
        out_specs=[spec] * len(shapes),
        compiler_params=pltpu.CompilerParams(vmem_limit_bytes=24 * MIB),
        cost_estimate=pl.CostEstimate(flops=size // 8, bytes_accessed=size // 8, transcendentals=0),
    )(*args)


def join_kernel(starts, *refs):
    *parts, out, done = refs
    copies = []
    for n, part in enumerate(parts):
        width = part.shape[1]
        here = out.at[:, pl.ds(pl.multiple_of(starts[n], width), width)]
        copies.append(pltpu.make_async_copy(part.at[: out.shape[0], :], here, done.at[n]))
    for copy in copies:
        copy.start()
    for copy in copies:
        copy.wait()


def join(parts, starts):
    rows, width = parts[-1].shape
    return pl.pallas_call(
        join_kernel,
        out_shape=jax.ShapeDtypeStruct((rows, width * len(parts)), parts[0].dtype),
        in_specs=[SMEM] + [VMEM] * len(parts),
        out_specs=HBM,
        scratch_shapes=[pltpu.SemaphoreType.DMA((len(parts),))],
        compiler_params=pltpu.CompilerParams(vmem_limit_bytes=16 * MIB),
        cost_estimate=pl.CostEstimate(flops=0, bytes_accessed=4 * rows * width * len(parts), transcendentals=0),
    )(jnp.stack(starts).astype(jnp.int32), *parts)


def local(activations, cotangent, inner_weight, outer_weight, outer_momentum, next_activations):
    fsdp, nz = lax.axis_size("fsdp"), lax.axis_size("z")
    f, z, x, c = (lax.axis_index(a) for a in ("fsdp", "z", "x", "core"))
    tok, d = activations.shape
    kv = cotangent.shape[1]
    width = d // fsdp
    block = width // nz
    share = block // (PAIR * CORES)
    own_weight = inner_weight[0]
    swap = ring(CORES, 1)

    def column(b, i, k, s):
        return ((f + s) % fsdp) * width + b * block + i * CORES * share + ((c + k) % CORES) * share

    def pair_ring(k, s):
        at = lambda i, j: (i % CORES) * fsdp + j % fsdp
        return [(at(i, j), at(i + k, j + s)) for i in range(CORES) for j in range(fsdp)]

    shifts = [(k, s) for s in range(fsdp) for k in range(CORES)]
    stages = [(m + 1, m) for m in range(nz - 2, -1, -2)]

    far = [(i, k, s) for k in range(CORES) for i in range(PAIR) for s in range(fsdp)]
    index = lambda i, k, s: ((i % PAIR) * CORES + k % CORES) * fsdp + s % fsdp
    every = [(i, k, s) for i in range(PAIR) for k in range(CORES) for s in range(fsdp)]
    mine, nexts = {}, {}

    def next_groups(places):
        return [[column(z ^ m, (x + i) % PAIR, k, s) for m in range(nz)] for i, k, s in places]

    def send_next(i, k, s):
        pairs = [(index(*e), index(e[0] + i, e[1] + k, e[2] + s)) for e in every]
        nexts[i, k, s] = lax.ppermute(mine[i, k, s], ("x", "core", "fsdp"), pairs) if i or k or s else mine[i, k, s]

    cots = {(0, 0): cotangent}
    for s in range(1, fsdp):
        cots[0, s] = lax.ppermute(cotangent, "fsdp", ring(fsdp, s))
    columns = [[column(z ^ m, (x + i) % PAIR, k, s) for m in ms for i in range(PAIR)] for ms in stages for k, s in shifts]
    (packed,), _ = pack([(activations, 1, share, columns)])
    acts = []
    for stage in range(len(stages)):
        came = []
        for (k, s), part in zip(shifts, packed[stage * len(shifts) :]):
            came.append(part if (k, s) == (0, 0) else lax.ppermute(part, ("core", "fsdp"), pair_ring(k, s)))
        acts.append(came)
    other_weight = lax.ppermute(own_weight, "core", swap)
    cots[1, 0] = lax.ppermute(cotangent, "core", swap)
    for s in range(1, fsdp):
        cots[1, s] = lax.ppermute(cots[0, s], "core", swap)

    wanted = [cots[0, s] for s in range(1, fsdp)]
    (parts,), wanted = pack([(next_activations, 1, share, next_groups(far))], wanted, pltpu.HBM)
    cots.update({(0, s): got for s, got in enumerate(wanted, 1)})
    mine.update(zip(far, parts))

    ordered = [cots[k, s] for k, s in shifts]
    across_x, across_z = ring(PAIR, 1), [(i, i ^ 1) for i in range(nz)]
    over_z = {}

    def finish(m, to_z, to_x, keep_left, keep_right):
        from_z, from_x = lax.ppermute(to_z, "z", across_z), lax.ppermute(to_x, "x", across_x)
        return [keep_left, from_z, keep_right, from_x] + over_z.get(m, [])

    for stage, ms in enumerate(stages):
        cut = kv // 2 if ms[1] else 3 * kv // 4
        blocks = [((z ^ m) * PAIR + (x + i) % PAIR) * CORES + c for m in ms for i in range(PAIR)]
        place = jnp.stack(blocks).astype(jnp.int32)
        if not stage:
            place, *held = lax.optimization_barrier((place, *[mine[e] for e in far]))
            mine.update(zip(far, held))
        if stage:
            place, to_z, to_x = lax.optimization_barrier((place, to_z, to_x))
            m = stages[stage - 1][1]
            inputs = finish(m, to_z, to_x, keep_left, keep_right)
            low = m & -m
        to_x, stay_x, to_z, stay_z = inner_blocks(place, acts[stage], 0, ordered, own_weight, other_weight, share, cut)
        if stage:
            to_x, to_z, inputs[1], inputs[3] = lax.optimization_barrier((to_x, to_z, inputs[1], inputs[3]))
            (block_total,) = small_call(
                block_kernel, [jax.ShapeDtypeStruct((share, kv), bf16)], *inputs, spec=pl.BlockSpec()
            )
            over_z.setdefault(m ^ low, []).append(lax.ppermute(block_total, "z", [(i, i ^ low) for i in range(nz)]))
        if not stage:
            stay_x, *island_cots = lax.optimization_barrier((stay_x, *[cots[0, s] for s in range(fsdp)]))
            grad_rows = lax.dot_general(
                jnp.concatenate(island_cots, axis=0), own_weight, (((1,), (1,)), ((), ())), preferred_element_type=f32
            ).astype(bf16)
            parts = [grad_rows] + [grad_rows[s * tok : (s + 1) * tok] for s in range(1, fsdp)]
            stay_x, *parts = lax.optimization_barrier((stay_x, *parts))
            for s in range(1, fsdp):
                parts[s] = lax.ppermute(parts[s], "fsdp", ring(fsdp, -s))
        from_x, from_z = lax.ppermute(to_x, "x", across_x), lax.ppermute(to_z, "z", across_z)
        to_z, keep_left, to_x, keep_right = small_call(
            functools.partial(middle_kernel, share),
            [jax.ShapeDtypeStruct((share, wide), kind) for wide in (cut, kv - cut) for kind in (bf16, f32)],
            stay_x,
            from_x,
            stay_z,
            from_z,
            spec=pl.BlockSpec(),
        )

    inputs = finish(0, to_z, to_x, keep_left, keep_right)
    inputs[0], inputs[2] = small_call(
        gather_kernel, [jax.ShapeDtypeStruct(part.shape, f32) for part in (keep_left, keep_right)], keep_left, keep_right, *inputs[4:], spec=pl.BlockSpec(), weight=200
    )
    replicas = nz * PAIR * CORES
    inputs = [*inputs[:4], outer_weight, outer_momentum]
    (share_rows,) = small_call(
        functools.partial(share_kernel, replicas),
        [jax.ShapeDtypeStruct((share, kv), bf16)],
        *inputs,
        spec=pl.BlockSpec(),
    )
    share_rows, *inputs = lax.optimization_barrier((share_rows, *inputs))
    new_outer, new_momentum = small_call(
        functools.partial(state_kernel, replicas),
        [jax.ShapeDtypeStruct((share, kv), f32)] * 2,
        *inputs,
        spec=pl.BlockSpec(),
        weight=1 << 17,
    )
    share_rows, *held = lax.optimization_barrier((share_rows, *[mine[e] for e in far]))
    mine.update(zip(far, held))
    for e in far:
        send_next(*e)

    rows = {}
    for m in sorted(range(1, nz), key=lambda m: (m & (m - 1)).bit_count() * nz - m):
        low = m & -m
        pieces = [share_rows] if m == low else list(rows[m ^ low])
        if m == nz - 1:
            pieces[0], new_outer = lax.optimization_barrier((pieces[0], new_outer))
        rows[m] = [lax.ppermute(piece, "z", [(i, i ^ low) for i in range(nz)]) for piece in pieces]
    rows = [[share_rows]] + [rows[m] for m in range(1, nz)]
    input_grad = join(parts, [((f + s) % fsdp) * width for s in range(fsdp)])

    half = len(far) // CORES
    near, away = [nexts[e] for e in far[:half]], [nexts[e] for e in far[half:]]
    orders = [list(range(half)), [2 * half - 1] + list(range(half, 2 * half - 1))]
    keep, give = keys_part(near + away[1:] + away[:1], rows[:-1], 0, orders=orders)
    give, keep, input_grad = lax.optimization_barrier((give, keep, input_grad))
    last = (nz - 1) * share
    (give,) = keys_part(away, rows[-1:], last, [give], kind=bf16)
    (keep,) = keys_part(near, rows[-1:], last, [keep])
    came = lax.ppermute(give, "core", swap)
    shape = lambda n, kind: jax.ShapeDtypeStruct((n, kv // 2), kind)
    to_x, stay_x, stay_f, *to_f = small_call(
        functools.partial(core_sum_kernel, fsdp, tok),
        [shape(fsdp * tok, bf16), shape(fsdp * tok, f32), shape(PAIR * tok, f32)] + [shape(PAIR * tok, bf16)] * (fsdp - 1),
        keep,
        came,
    )

    def home(to_x, to_f):
        from_x = lax.ppermute(to_x, "x", ring(PAIR, 1))
        return [from_x] + [lax.ppermute(part, "fsdp", ring(fsdp, -s - 1)) for s, part in enumerate(to_f)]

    left, right, to_x, *to_f = small_call(
        functools.partial(second_sum_kernel, fsdp, tok),
        [shape(tok, f32)] * 2 + [shape(tok, bf16)] * fsdp,
        stay_x,
        stay_f,
        *home(to_x, to_f),
    )
    (keys,) = small_call(
        last_sum_kernel, [jax.ShapeDtypeStruct((tok, kv), bf16)], left, right, *home(to_x, to_f)
    )
    return (input_grad, keys, new_outer, new_momentum)


def solution(mesh):
    fsdp = mesh.shape["fsdp"]
    nz = mesh.shape["island"] // (PAIR * CORES)
    split = Mesh(mesh.devices.reshape(nz, PAIR, CORES, fsdp), ("z", "x", "core", "fsdp"))
    island = ("z", "x", "core")
    tokens = P(island + ("fsdp",), None)
    width = P(("fsdp",) + island, None)
    in_specs = (tokens, tokens, P(island, "fsdp", None), width, width, tokens)
    out_specs = (tokens, tokens, width, width)
    return jax.shard_map(local, mesh=split, in_specs=in_specs, out_specs=out_specs, check_vma=False)
```

```python
import functools

import jax
import jax.numpy as jnp
from jax import lax
from jax.experimental import pallas as pl
from jax.experimental.pallas import tpu as pltpu
from jax.sharding import Mesh, PartitionSpec as P

inner_rate = 1.2
outer_rate = 0.7
nesterov = 0.9
CORES = 2
PAIR = 2
LANES = 128

bf16, f32 = jnp.bfloat16, jnp.float32
VMEM, HBM = pl.BlockSpec(memory_space=pltpu.VMEM), pl.BlockSpec(memory_space=pltpu.HBM)
SMEM, ANY = pl.BlockSpec(memory_space=pltpu.SMEM), pl.BlockSpec(memory_space=pl.ANY)
MIB = 1024 * 1024


def ring(count, shift):
    return [(i, (i + shift) % count) for i in range(count)]


def strip(axis, start, size):
    return (pl.ds(start, size), slice(None)) if axis == 0 else (slice(None), pl.ds(start, size))


def in_hbm(array):
    return pltpu.with_memory_space_constraint(array, pltpu.HBM)


def pack_kernel(plan, starts, *refs):
    sources, outs, done = refs[: len(plan)], refs[len(plan) : -1], refs[-1]
    copies, o = [], 0
    for source, (axis, size, counts) in zip(sources, plan):
        for count in counts:
            for i in range(count):
                n = len(copies)
                part = source.at[strip(axis, pl.multiple_of(starts[n], size), size)]
                copies.append(pltpu.make_async_copy(part, outs[o].at[strip(axis, i * size, size)], done.at[n]))
            o += 1
    for copy in copies:
        copy.start()
    for copy in copies:
        copy.wait()


def pack(items, after=(), target=jax.ShapeDtypeStruct):
    result, rest = {}, []
    for n, (array, axis, size, groups) in enumerate(items):
        if axis == 1 and size % LANES:
            strips = [[lax.dynamic_slice_in_dim(array, at, size, axis=axis) for at in group] for group in groups]
            result[n] = [jnp.concatenate(group, axis=axis) for group in strips]
        else:
            rest.append((n, array, axis, size, groups))
    if not rest:
        return [result[n] for n in range(len(items))], list(after)
    starts = jnp.stack([at for item in rest for group in item[4] for at in group]).astype(jnp.int32)
    if after:
        starts, *after = lax.optimization_barrier((starts, *after))
    plan, shapes = [], []
    for _, array, axis, size, groups in rest:
        counts = [len(group) for group in groups]
        plan.append((axis, size, counts))
        for n in counts:
            shape = (n * size, array.shape[1]) if axis == 0 else (array.shape[0], n * size)
            shapes.append(target(shape, array.dtype))
    moved = 4 * starts.shape[0] * 1024 * LANES
    outs = pl.pallas_call(
        functools.partial(pack_kernel, plan),
        out_shape=shapes,
        in_specs=[SMEM] + [HBM] * len(rest),
        out_specs=[pl.BlockSpec()] * len(shapes),
        scratch_shapes=[pltpu.SemaphoreType.DMA((starts.shape[0],))],
        compiler_params=pltpu.CompilerParams(vmem_limit_bytes=16 * MIB),
        cost_estimate=pl.CostEstimate(flops=0, bytes_accessed=moved, transcendentals=0),
    )(starts, *[in_hbm(item[1]) for item in rest])
    for n, *_, groups in rest:
        result[n], outs = outs[: len(groups)], outs[len(groups) :]
    return [result[n] for n in range(len(items))], list(after)


def inner_kernel(pieces, share, scale, act_at, place, *refs):
    acts, cots = refs[:pieces], refs[pieces : 2 * pieces]
    own, other, to_x, stay_x, to_z, stay_z, left, right, rows, total, done = refs[2 * pieces :]
    tok, kv = cots[0].shape
    strips = 2 * PAIR
    copies = []

    def fetch(source, target):
        copies.append(pltpu.make_async_copy(source, target, done.at[len(copies)]))

    for n, (act, cot) in enumerate(zip(acts, cots)):
        here = pl.ds(n * tok, tok)
        fetch(act.at[:, pl.ds(act_at, strips * share)], left.at[here, :])
        fetch(cot, right.at[here, :])
    for i in range(strips):
        strip_rows = pl.ds(pl.multiple_of(place[i] * share, share), share)
        here = pl.ds(i * share, share)
        fetch(own.at[strip_rows, :], rows.at[0, here, :])
        fetch(other.at[strip_rows, :], rows.at[1, here, :])
    for copy in copies:
        copy.start()
    for copy in copies[: 2 * pieces]:
        copy.wait()
    total[...] = lax.dot_general(left[...], right[...], (((0,), (0,)), ((), ())), preferred_element_type=f32)
    for copy in copies[2 * pieces :]:
        copy.wait()

    def inner_new(i, columns):
        here = slice(i * share, (i + 1) * share)
        return (rows[0, here, columns].astype(f32) + rows[1, here, columns].astype(f32)) - scale * total[here, columns]

    first, second = slice(0, to_x.shape[1]), slice(to_x.shape[1], kv)
    for n in range(2):
        here = slice(n * share, (n + 1) * share)
        to_x[here, :] = inner_new(PAIR * n + 1, first).astype(bf16)
        to_z[here, :] = inner_new(n, second).astype(bf16)
    for n in range(2):
        here = slice(n * share, (n + 1) * share)
        stay_x[here, :] = inner_new(PAIR * n, first)
        stay_z[here, :] = inner_new(PAIR + n, second)


def inner_blocks(place, acts, act_at, cots, own, other, share, cut):
    pieces = len(acts)
    tok, kv = cots[0].shape
    rows = 2 * PAIR * share
    if act_at % LANES or rows % LANES:
        acts, act_at = [a[:, act_at : act_at + rows] for a in acts], 0
    shapes = [jax.ShapeDtypeStruct((2 * share, wide), kind) for wide in (cut, kv - cut) for kind in (bf16, f32)]
    return pl.pallas_call(
        functools.partial(inner_kernel, pieces, share, inner_rate / (tok * pieces // CORES), act_at),
        out_shape=shapes,
        in_specs=[SMEM] + [ANY] * (2 * pieces) + [HBM, ANY],
        out_specs=[pl.BlockSpec()] * 4,
        scratch_shapes=[
            pltpu.VMEM((pieces * tok, rows), bf16),
            pltpu.VMEM((pieces * tok, kv), bf16),
            pltpu.VMEM((CORES, rows, kv), bf16),
            pltpu.VMEM((rows, kv), f32),
            pltpu.SemaphoreType.DMA((2 * pieces + 2 * CORES * PAIR,)),
        ],
        compiler_params=pltpu.CompilerParams(vmem_limit_bytes=32 * MIB),
        cost_estimate=pl.CostEstimate(flops=pieces * tok * share * kv, bytes_accessed=share * kv, transcendentals=0),
    )(place, *acts, *cots, in_hbm(own), other)


def middle_kernel(share, stay_x, from_x, stay_z, from_z, to_z, keep_left, to_x, keep_right):
    over_x = stay_x[...] + from_x[...].astype(f32)
    over_z = stay_z[...] + from_z[...].astype(f32)
    to_z[...] = over_x[:share].astype(bf16)
    to_x[...] = over_z[share:].astype(bf16)
    keep_left[...] = over_x[share:]
    keep_right[...] = over_z[:share]


def block_sum(keep_left, from_z, keep_right, from_x, came):
    left = keep_left[...] + from_z[...].astype(f32)
    right = keep_right[...] + from_x[...].astype(f32)
    total = jnp.concatenate([left, right], axis=1)
    for other in came:
        total = total + other[...].astype(f32)
    return total


def gather_kernel(keep_left, keep_right, *refs):
    *came, left, right = refs
    total = jnp.concatenate([keep_left[...], keep_right[...]], axis=1)
    for other in came:
        total = total + other[...].astype(f32)
    left[...] = total[:, : left.shape[1]]
    right[...] = total[:, left.shape[1] :]


def block_kernel(*refs):
    *inputs, out = refs
    out[...] = block_sum(*inputs[:4], inputs[4:]).astype(bf16)


def outer_step(replicas, inputs, weight, momentum):
    pseudo_grad = weight[...] - block_sum(*inputs[:4], inputs[4:]) / replicas
    moment = nesterov * momentum[...] + pseudo_grad
    return weight[...] - outer_rate * (pseudo_grad + nesterov * moment), moment


def share_kernel(replicas, *refs):
    *inputs, weight, momentum, share = refs
    share[...] = outer_step(replicas, inputs, weight, momentum)[0].astype(bf16)


def state_kernel(replicas, *refs):
    *inputs, weight, momentum, new_outer, new_momentum = refs
    new_outer[...], new_momentum[...] = outer_step(replicas, inputs, weight, momentum)


def keys_kernel(orders, counts, at, *refs):
    acts_count = sum(len(order) for order in orders)
    acts, refs = refs[:acts_count], refs[acts_count:]
    blocks = []
    for count in counts:
        blocks.append(jnp.concatenate([w[...] for w in refs[:count]], axis=1))
        refs = refs[count:]
    weight = jnp.concatenate(blocks, axis=0)
    before, outs = (refs[:1], refs[1:]) if at else ([], refs)
    for order, out in zip(orders, outs):
        left = jnp.concatenate([acts[n][:, at : at + weight.shape[0]] for n in order], axis=0)
        product = jnp.dot(left, weight, preferred_element_type=f32)
        out[...] = (before[0][...] + product if at else product).astype(out.dtype)


def keys_part(acts, blocks, at, before=(), orders=None, kind=f32):
    orders = orders or [list(range(len(acts)))]
    outs = len(orders)
    rows, kv = len(acts) * acts[0].shape[0] // outs, sum(w.shape[1] for w in blocks[0])
    depth = sum(block[0].shape[0] for block in blocks)
    if at % LANES:
        return [(before[0] + keys_part([a[:, at:] for a in acts], blocks, 0)[0]).astype(kind)]
    pieces = [w for block in blocks for w in block]
    flops = rows * depth * kv if at else 1 << 34
    return pl.pallas_call(
        functools.partial(keys_kernel, orders, [len(block) for block in blocks], at),
        out_shape=[jax.ShapeDtypeStruct((rows, kv), kind)] * outs,
        in_specs=[pl.BlockSpec()] * (len(acts) + len(pieces) + len(before)),
        out_specs=[pl.BlockSpec()] * outs,
        compiler_params=pltpu.CompilerParams(vmem_limit_bytes=32 * MIB),
        cost_estimate=pl.CostEstimate(flops=flops, bytes_accessed=rows * kv, transcendentals=0),
    )(*acts, *pieces, *before)


def core_sum_kernel(fsdp, tok, keep, came, to_x, stay_x, stay_f, *to_f):
    half = keep.shape[1] // 2
    total = keep[...] + came[...].astype(f32)
    rows = fsdp * tok
    stay_x[...] = total[:rows, :half]
    to_x[...] = total[rows:, :half].astype(bf16)
    for i in range(PAIR):
        here = slice(i * tok, (i + 1) * tok)
        stay_f[here, :] = total[i * rows : i * rows + tok, half:]
        for s in range(1, fsdp):
            to_f[s - 1][here, :] = total[i * rows + s * tok : i * rows + (s + 1) * tok, half:].astype(bf16)


def second_sum_kernel(fsdp, tok, *refs):
    stay_x, stay_f, from_x, *from_f = refs[: fsdp + 2]
    left, right, to_x, *to_f = refs[fsdp + 2 :]
    first = stay_x[...] + from_x[...].astype(f32)
    left[...] = first[:tok]
    for s in range(1, fsdp):
        to_f[s - 1][...] = first[s * tok : (s + 1) * tok].astype(bf16)
    second = stay_f[...]
    for came in from_f:
        second = second + came[...].astype(f32)
    right[...] = second[:tok]
    to_x[...] = second[tok:].astype(bf16)


def last_sum_kernel(left, right, from_x, *refs):
    *from_f, keys = refs
    half = left.shape[1]
    first = left[...]
    for came in from_f:
        first = first + came[...].astype(f32)
    keys[:, :half] = first.astype(bf16)
    keys[:, half:] = (right[...] + from_x[...].astype(f32)).astype(bf16)


def small_call(kernel, shapes, *args, spec=VMEM, weight=1):
    size = weight * sum(shape.size for shape in shapes)
    return pl.pallas_call(
        kernel,
        out_shape=shapes,
        in_specs=[spec] * len(args),
        out_specs=[spec] * len(shapes),
        compiler_params=pltpu.CompilerParams(vmem_limit_bytes=24 * MIB),
        cost_estimate=pl.CostEstimate(flops=size // 8, bytes_accessed=size // 8, transcendentals=0),
    )(*args)


def join_kernel(starts, *refs):
    *parts, out, done = refs
    copies = []
    for n, part in enumerate(parts):
        width = part.shape[1]
        here = out.at[:, pl.ds(pl.multiple_of(starts[n], width), width)]
        copies.append(pltpu.make_async_copy(part.at[: out.shape[0], :], here, done.at[n]))
    for copy in copies:
        copy.start()
    for copy in copies:
        copy.wait()


def join(parts, starts):
    rows, width = parts[-1].shape
    return pl.pallas_call(
        join_kernel,
        out_shape=jax.ShapeDtypeStruct((rows, width * len(parts)), parts[0].dtype),
        in_specs=[SMEM] + [VMEM] * len(parts),
        out_specs=HBM,
        scratch_shapes=[pltpu.SemaphoreType.DMA((len(parts),))],
        compiler_params=pltpu.CompilerParams(vmem_limit_bytes=16 * MIB),
        cost_estimate=pl.CostEstimate(flops=0, bytes_accessed=4 * rows * width * len(parts), transcendentals=0),
    )(jnp.stack(starts).astype(jnp.int32), *parts)


def local(activations, cotangent, inner_weight, outer_weight, outer_momentum, next_activations):
    fsdp, nz = lax.axis_size("fsdp"), lax.axis_size("z")
    f, z, x, c = (lax.axis_index(a) for a in ("fsdp", "z", "x", "core"))
    tok, d = activations.shape
    kv = cotangent.shape[1]
    width = d // fsdp
    block = width // nz
    share = block // (PAIR * CORES)
    own_weight = inner_weight[0]
    swap = ring(CORES, 1)

    def column(b, i, k, s):
        return ((f + s) % fsdp) * width + b * block + i * CORES * share + ((c + k) % CORES) * share

    def pair_ring(k, s):
        at = lambda i, j: (i % CORES) * fsdp + j % fsdp
        return [(at(i, j), at(i + k, j + s)) for i in range(CORES) for j in range(fsdp)]

    shifts = [(k, s) for s in range(fsdp) for k in range(CORES)]
    stages = [(m + 1, m) for m in range(nz - 2, -1, -2)]

    far = [(i, k, s) for k in range(CORES) for i in range(PAIR) for s in range(fsdp)]
    index = lambda i, k, s: ((i % PAIR) * CORES + k % CORES) * fsdp + s % fsdp
    every = [(i, k, s) for i in range(PAIR) for k in range(CORES) for s in range(fsdp)]
    mine, nexts = {}, {}

    def next_groups(places):
        return [[column(z ^ m, (x + i) % PAIR, k, s) for m in range(nz)] for i, k, s in places]

    def send_next(i, k, s):
        pairs = [(index(*e), index(e[0] + i, e[1] + k, e[2] + s)) for e in every]
        nexts[i, k, s] = lax.ppermute(mine[i, k, s], ("x", "core", "fsdp"), pairs) if i or k or s else mine[i, k, s]

    cots = {(0, 0): cotangent}
    for s in range(1, fsdp):
        cots[0, s] = lax.ppermute(cotangent, "fsdp", ring(fsdp, s))
    columns = [[column(z ^ m, (x + i) % PAIR, k, s) for m in ms for i in range(PAIR)] for ms in stages for k, s in shifts]
    (packed,), _ = pack([(activations, 1, share, columns)])
    acts = []
    for stage in range(len(stages)):
        came = []
        for (k, s), part in zip(shifts, packed[stage * len(shifts) :]):
            came.append(part if (k, s) == (0, 0) else lax.ppermute(part, ("core", "fsdp"), pair_ring(k, s)))
        acts.append(came)
    other_weight = lax.ppermute(own_weight, "core", swap)
    cots[1, 0] = lax.ppermute(cotangent, "core", swap)
    for s in range(1, fsdp):
        cots[1, s] = lax.ppermute(cots[0, s], "core", swap)

    wanted = [cots[0, s] for s in range(1, fsdp)]
    (parts,), wanted = pack([(next_activations, 1, share, next_groups(far))], wanted, pltpu.HBM)
    cots.update({(0, s): got for s, got in enumerate(wanted, 1)})
    mine.update(zip(far, parts))

    ordered = [cots[k, s] for k, s in shifts]
    across_x, across_z = ring(PAIR, 1), [(i, i ^ 1) for i in range(nz)]
    over_z = {}

    def finish(m, to_z, to_x, keep_left, keep_right):
        from_z, from_x = lax.ppermute(to_z, "z", across_z), lax.ppermute(to_x, "x", across_x)
        return [keep_left, from_z, keep_right, from_x] + over_z.get(m, [])

    for stage, ms in enumerate(stages):
        cut = kv // 2 if ms[1] else 3 * kv // 4
        blocks = [((z ^ m) * PAIR + (x + i) % PAIR) * CORES + c for m in ms for i in range(PAIR)]
        place = jnp.stack(blocks).astype(jnp.int32)
        if not stage:
            place, *held = lax.optimization_barrier((place, *[mine[e] for e in far]))
            mine.update(zip(far, held))
        if stage:
            place, to_z, to_x = lax.optimization_barrier((place, to_z, to_x))
            m = stages[stage - 1][1]
            inputs = finish(m, to_z, to_x, keep_left, keep_right)
            low = m & -m
        to_x, stay_x, to_z, stay_z = inner_blocks(place, acts[stage], 0, ordered, own_weight, other_weight, share, cut)
        if stage:
            to_x, to_z, inputs[1], inputs[3] = lax.optimization_barrier((to_x, to_z, inputs[1], inputs[3]))
            (block_total,) = small_call(
                block_kernel, [jax.ShapeDtypeStruct((share, kv), bf16)], *inputs, spec=pl.BlockSpec()
            )
            over_z.setdefault(m ^ low, []).append(lax.ppermute(block_total, "z", [(i, i ^ low) for i in range(nz)]))
        if not stage:
            stay_x, *island_cots = lax.optimization_barrier((stay_x, *[cots[0, s] for s in range(fsdp)]))
            grad_rows = lax.dot_general(
                jnp.concatenate(island_cots, axis=0), own_weight, (((1,), (1,)), ((), ())), preferred_element_type=f32
            ).astype(bf16)
            parts = [grad_rows] + [grad_rows[s * tok : (s + 1) * tok] for s in range(1, fsdp)]
            stay_x, *parts = lax.optimization_barrier((stay_x, *parts))
            for s in range(1, fsdp):
                parts[s] = lax.ppermute(parts[s], "fsdp", ring(fsdp, -s))
        from_x, from_z = lax.ppermute(to_x, "x", across_x), lax.ppermute(to_z, "z", across_z)
        to_z, keep_left, to_x, keep_right = small_call(
            functools.partial(middle_kernel, share),
            [jax.ShapeDtypeStruct((share, wide), kind) for wide in (cut, kv - cut) for kind in (bf16, f32)],
            stay_x,
            from_x,
            stay_z,
            from_z,
            spec=pl.BlockSpec(),
        )

    inputs = finish(0, to_z, to_x, keep_left, keep_right)
    inputs[0], inputs[2] = small_call(
        gather_kernel, [jax.ShapeDtypeStruct(part.shape, f32) for part in (keep_left, keep_right)], keep_left, keep_right, *inputs[4:], spec=pl.BlockSpec(), weight=200
    )
    replicas = nz * PAIR * CORES
    inputs = [*inputs[:4], outer_weight, outer_momentum]
    (share_rows,) = small_call(
        functools.partial(share_kernel, replicas),
        [jax.ShapeDtypeStruct((share, kv), bf16)],
        *inputs,
        spec=pl.BlockSpec(),
    )
    share_rows, *held = lax.optimization_barrier((share_rows, *[mine[e] for e in far]))
    mine.update(zip(far, held))
    for e in far:
        send_next(*e)

    rows = {}
    for m in sorted(range(1, nz), key=lambda m: (m & (m - 1)).bit_count() * nz - m):
        low = m & -m
        pieces = [share_rows] if m == low else list(rows[m ^ low])
        if m == nz - 1:
            ready = rows[1] if m > 1 else [share_rows]
            inputs[0], *ready = lax.optimization_barrier((inputs[0], *ready))
            if m > 1:
                rows[1] = ready
            new_outer, new_momentum = small_call(
                functools.partial(state_kernel, replicas),
                [jax.ShapeDtypeStruct((share, kv), f32)] * 2,
                *inputs,
                spec=pl.BlockSpec(),
                weight=1 << 17,
            )
            pieces[0], new_outer = lax.optimization_barrier((pieces[0], new_outer))
        rows[m] = [lax.ppermute(piece, "z", [(i, i ^ low) for i in range(nz)]) for piece in pieces]
    rows = [[share_rows]] + [rows[m] for m in range(1, nz)]
    input_grad = join(parts, [((f + s) % fsdp) * width for s in range(fsdp)])

    half = len(far) // CORES
    near, away = [nexts[e] for e in far[:half]], [nexts[e] for e in far[half:]]
    orders = [list(range(half)), [2 * half - 1] + list(range(half, 2 * half - 1))]
    keep, give = keys_part(near + away[1:] + away[:1], rows[:-1], 0, orders=orders)
    give, keep, input_grad = lax.optimization_barrier((give, keep, input_grad))
    last = (nz - 1) * share
    (give,) = keys_part(away, rows[-1:], last, [give], kind=bf16)
    (keep,) = keys_part(near, rows[-1:], last, [keep])
    came = lax.ppermute(give, "core", swap)
    shape = lambda n, kind: jax.ShapeDtypeStruct((n, kv // 2), kind)
    to_x, stay_x, stay_f, *to_f = small_call(
        functools.partial(core_sum_kernel, fsdp, tok),
        [shape(fsdp * tok, bf16), shape(fsdp * tok, f32), shape(PAIR * tok, f32)] + [shape(PAIR * tok, bf16)] * (fsdp - 1),
        keep,
        came,
    )

    def home(to_x, to_f):
        from_x = lax.ppermute(to_x, "x", ring(PAIR, 1))
        return [from_x] + [lax.ppermute(part, "fsdp", ring(fsdp, -s - 1)) for s, part in enumerate(to_f)]

    left, right, to_x, *to_f = small_call(
        functools.partial(second_sum_kernel, fsdp, tok),
        [shape(tok, f32)] * 2 + [shape(tok, bf16)] * fsdp,
        stay_x,
        stay_f,
        *home(to_x, to_f),
    )
    (keys,) = small_call(
        last_sum_kernel, [jax.ShapeDtypeStruct((tok, kv), bf16)], left, right, *home(to_x, to_f)
    )
    return (input_grad, keys, new_outer, new_momentum)


def solution(mesh):
    fsdp = mesh.shape["fsdp"]
    nz = mesh.shape["island"] // (PAIR * CORES)
    split = Mesh(mesh.devices.reshape(nz, PAIR, CORES, fsdp), ("z", "x", "core", "fsdp"))
    island = ("z", "x", "core")
    tokens = P(island + ("fsdp",), None)
    width = P(("fsdp",) + island, None)
    in_specs = (tokens, tokens, P(island, "fsdp", None), width, width, tokens)
    out_specs = (tokens, tokens, width, width)
    return jax.shard_map(local, mesh=split, in_specs=in_specs, out_specs=out_specs, check_vma=False)
```

```python
import functools

import jax
import jax.numpy as jnp
from jax import lax
from jax.experimental import pallas as pl
from jax.experimental.pallas import tpu as pltpu
from jax.sharding import Mesh, PartitionSpec as P

inner_rate = 1.2
outer_rate = 0.7
nesterov = 0.9
CORES = 2
PAIR = 2
LANES = 128

bf16, f32 = jnp.bfloat16, jnp.float32
VMEM, HBM = pl.BlockSpec(memory_space=pltpu.VMEM), pl.BlockSpec(memory_space=pltpu.HBM)
SMEM, ANY = pl.BlockSpec(memory_space=pltpu.SMEM), pl.BlockSpec(memory_space=pl.ANY)
MIB = 1024 * 1024


def ring(count, shift):
    return [(i, (i + shift) % count) for i in range(count)]


def strip(axis, start, size):
    return (pl.ds(start, size), slice(None)) if axis == 0 else (slice(None), pl.ds(start, size))


def in_hbm(array):
    return pltpu.with_memory_space_constraint(array, pltpu.HBM)


def pack_kernel(plan, starts, *refs):
    sources, outs, done = refs[: len(plan)], refs[len(plan) : -1], refs[-1]
    copies, o = [], 0
    for source, (axis, size, counts) in zip(sources, plan):
        for count in counts:
            for i in range(count):
                n = len(copies)
                part = source.at[strip(axis, pl.multiple_of(starts[n], size), size)]
                copies.append(pltpu.make_async_copy(part, outs[o].at[strip(axis, i * size, size)], done.at[n]))
            o += 1
    for copy in copies:
        copy.start()
    for copy in copies:
        copy.wait()


def pack(items, after=(), target=jax.ShapeDtypeStruct):
    result, rest = {}, []
    for n, (array, axis, size, groups) in enumerate(items):
        if axis == 1 and size % LANES:
            strips = [[lax.dynamic_slice_in_dim(array, at, size, axis=axis) for at in group] for group in groups]
            result[n] = [jnp.concatenate(group, axis=axis) for group in strips]
        else:
            rest.append((n, array, axis, size, groups))
    if not rest:
        return [result[n] for n in range(len(items))], list(after)
    starts = jnp.stack([at for item in rest for group in item[4] for at in group]).astype(jnp.int32)
    if after:
        starts, *after = lax.optimization_barrier((starts, *after))
    plan, shapes = [], []
    for _, array, axis, size, groups in rest:
        counts = [len(group) for group in groups]
        plan.append((axis, size, counts))
        for n in counts:
            shape = (n * size, array.shape[1]) if axis == 0 else (array.shape[0], n * size)
            shapes.append(target(shape, array.dtype))
    moved = 4 * starts.shape[0] * 1024 * LANES
    outs = pl.pallas_call(
        functools.partial(pack_kernel, plan),
        out_shape=shapes,
        in_specs=[SMEM] + [HBM] * len(rest),
        out_specs=[pl.BlockSpec()] * len(shapes),
        scratch_shapes=[pltpu.SemaphoreType.DMA((starts.shape[0],))],
        compiler_params=pltpu.CompilerParams(vmem_limit_bytes=16 * MIB),
        cost_estimate=pl.CostEstimate(flops=0, bytes_accessed=moved, transcendentals=0),
    )(starts, *[in_hbm(item[1]) for item in rest])
    for n, *_, groups in rest:
        result[n], outs = outs[: len(groups)], outs[len(groups) :]
    return [result[n] for n in range(len(items))], list(after)


def inner_kernel(pieces, share, scale, act_at, place, *refs):
    acts, cots = refs[:pieces], refs[pieces : 2 * pieces]
    own, other, to_x, stay_x, to_z, stay_z, left, right, rows, total, done = refs[2 * pieces :]
    tok, kv = cots[0].shape
    strips = 2 * PAIR
    copies = []

    def fetch(source, target):
        copies.append(pltpu.make_async_copy(source, target, done.at[len(copies)]))

    for n, (act, cot) in enumerate(zip(acts, cots)):
        here = pl.ds(n * tok, tok)
        fetch(act.at[:, pl.ds(act_at, strips * share)], left.at[here, :])
        fetch(cot, right.at[here, :])
    for i in range(strips):
        strip_rows = pl.ds(pl.multiple_of(place[i] * share, share), share)
        here = pl.ds(i * share, share)
        fetch(own.at[strip_rows, :], rows.at[0, here, :])
        fetch(other.at[strip_rows, :], rows.at[1, here, :])
    for copy in copies:
        copy.start()
    for copy in copies[: 2 * pieces]:
        copy.wait()
    total[...] = lax.dot_general(left[...], right[...], (((0,), (0,)), ((), ())), preferred_element_type=f32)
    for copy in copies[2 * pieces :]:
        copy.wait()

    def inner_new(i, columns):
        here = slice(i * share, (i + 1) * share)
        return (rows[0, here, columns].astype(f32) + rows[1, here, columns].astype(f32)) - scale * total[here, columns]

    first, second = slice(0, to_x.shape[1]), slice(to_x.shape[1], kv)
    for n in range(2):
        here = slice(n * share, (n + 1) * share)
        to_x[here, :] = inner_new(PAIR * n + 1, first).astype(bf16)
        to_z[here, :] = inner_new(n, second).astype(bf16)
    for n in range(2):
        here = slice(n * share, (n + 1) * share)
        stay_x[here, :] = inner_new(PAIR * n, first)
        stay_z[here, :] = inner_new(PAIR + n, second)


def inner_blocks(place, acts, act_at, cots, own, other, share, cut):
    pieces = len(acts)
    tok, kv = cots[0].shape
    rows = 2 * PAIR * share
    if act_at % LANES or rows % LANES:
        acts, act_at = [a[:, act_at : act_at + rows] for a in acts], 0
    shapes = [jax.ShapeDtypeStruct((2 * share, wide), kind) for wide in (cut, kv - cut) for kind in (bf16, f32)]
    return pl.pallas_call(
        functools.partial(inner_kernel, pieces, share, inner_rate / (tok * pieces // CORES), act_at),
        out_shape=shapes,
        in_specs=[SMEM] + [ANY] * (2 * pieces) + [HBM, ANY],
        out_specs=[pl.BlockSpec()] * 4,
        scratch_shapes=[
            pltpu.VMEM((pieces * tok, rows), bf16),
            pltpu.VMEM((pieces * tok, kv), bf16),
            pltpu.VMEM((CORES, rows, kv), bf16),
            pltpu.VMEM((rows, kv), f32),
            pltpu.SemaphoreType.DMA((2 * pieces + 2 * CORES * PAIR,)),
        ],
        compiler_params=pltpu.CompilerParams(vmem_limit_bytes=32 * MIB),
        cost_estimate=pl.CostEstimate(flops=pieces * tok * share * kv, bytes_accessed=share * kv, transcendentals=0),
    )(place, *acts, *cots, in_hbm(own), other)


def middle_kernel(share, stay_x, from_x, stay_z, from_z, to_z, keep_left, to_x, keep_right):
    over_x = stay_x[...] + from_x[...].astype(f32)
    over_z = stay_z[...] + from_z[...].astype(f32)
    to_z[...] = over_x[:share].astype(bf16)
    to_x[...] = over_z[share:].astype(bf16)
    keep_left[...] = over_x[share:]
    keep_right[...] = over_z[:share]


def block_sum(keep_left, from_z, keep_right, from_x, came):
    left = keep_left[...] + from_z[...].astype(f32)
    right = keep_right[...] + from_x[...].astype(f32)
    total = jnp.concatenate([left, right], axis=1)
    for other in came:
        total = total + other[...].astype(f32)
    return total


def gather_kernel(keep_left, keep_right, *refs):
    *came, left, right = refs
    total = jnp.concatenate([keep_left[...], keep_right[...]], axis=1)
    for other in came:
        total = total + other[...].astype(f32)
    left[...] = total[:, : left.shape[1]]
    right[...] = total[:, left.shape[1] :]


def block_kernel(*refs):
    *inputs, out = refs
    out[...] = block_sum(*inputs[:4], inputs[4:]).astype(bf16)


def outer_step(replicas, inputs, weight, momentum):
    pseudo_grad = weight[...] - block_sum(*inputs[:4], inputs[4:]) / replicas
    moment = nesterov * momentum[...] + pseudo_grad
    return weight[...] - outer_rate * (pseudo_grad + nesterov * moment), moment


def share_kernel(replicas, *refs):
    *inputs, weight, momentum, share = refs
    share[...] = outer_step(replicas, inputs, weight, momentum)[0].astype(bf16)


def state_kernel(replicas, *refs):
    *inputs, weight, momentum, new_outer, new_momentum = refs
    new_outer[...], new_momentum[...] = outer_step(replicas, inputs, weight, momentum)


def keys_kernel(acts_count, counts, at, *refs):
    acts, refs = refs[:acts_count], refs[acts_count:]
    blocks = []
    for count in counts:
        blocks.append(jnp.concatenate([w[...] for w in refs[:count]], axis=1))
        refs = refs[count:]
    weight = jnp.concatenate(blocks, axis=0)
    before, outs = (refs[:1], refs[1:]) if at else ([], refs)
    each = acts_count // len(outs)
    for n, out in enumerate(outs):
        left = jnp.concatenate([a[:, at : at + weight.shape[0]] for a in acts[n * each : (n + 1) * each]], axis=0)
        product = jnp.dot(left, weight, preferred_element_type=f32)
        out[...] = (before[0][...] + product if at else product).astype(out.dtype)


def keys_part(acts, blocks, at, before=(), outs=1, kind=f32):
    rows, kv = len(acts) * acts[0].shape[0] // outs, sum(w.shape[1] for w in blocks[0])
    depth = sum(block[0].shape[0] for block in blocks)
    if at % LANES:
        return [(before[0] + keys_part([a[:, at:] for a in acts], blocks, 0)[0]).astype(kind)]
    pieces = [w for block in blocks for w in block]
    flops = rows * depth * kv if at else 1 << 34
    return pl.pallas_call(
        functools.partial(keys_kernel, len(acts), [len(block) for block in blocks], at),
        out_shape=[jax.ShapeDtypeStruct((rows, kv), kind)] * outs,
        in_specs=[pl.BlockSpec()] * (len(acts) + len(pieces) + len(before)),
        out_specs=[pl.BlockSpec()] * outs,
        compiler_params=pltpu.CompilerParams(vmem_limit_bytes=32 * MIB),
        cost_estimate=pl.CostEstimate(flops=flops, bytes_accessed=rows * kv, transcendentals=0),
    )(*acts, *pieces, *before)


def core_sum_kernel(fsdp, tok, keep, came, to_x, stay_x, stay_f, *to_f):
    half = keep.shape[1] // 2
    total = keep[...] + came[...].astype(f32)
    rows = fsdp * tok
    stay_x[...] = total[:rows, :half]
    to_x[...] = total[rows:, :half].astype(bf16)
    for i in range(PAIR):
        here = slice(i * tok, (i + 1) * tok)
        stay_f[here, :] = total[i * rows : i * rows + tok, half:]
        for s in range(1, fsdp):
            to_f[s - 1][here, :] = total[i * rows + s * tok : i * rows + (s + 1) * tok, half:].astype(bf16)


def second_sum_kernel(fsdp, tok, *refs):
    stay_x, stay_f, from_x, *from_f = refs[: fsdp + 2]
    left, right, to_x, *to_f = refs[fsdp + 2 :]
    first = stay_x[...] + from_x[...].astype(f32)
    left[...] = first[:tok]
    for s in range(1, fsdp):
        to_f[s - 1][...] = first[s * tok : (s + 1) * tok].astype(bf16)
    second = stay_f[...]
    for came in from_f:
        second = second + came[...].astype(f32)
    right[...] = second[:tok]
    to_x[...] = second[tok:].astype(bf16)


def last_sum_kernel(left, right, from_x, *refs):
    *from_f, keys = refs
    half = left.shape[1]
    first = left[...]
    for came in from_f:
        first = first + came[...].astype(f32)
    keys[:, :half] = first.astype(bf16)
    keys[:, half:] = (right[...] + from_x[...].astype(f32)).astype(bf16)


def small_call(kernel, shapes, *args, spec=VMEM, weight=1):
    size = weight * sum(shape.size for shape in shapes)
    return pl.pallas_call(
        kernel,
        out_shape=shapes,
        in_specs=[spec] * len(args),
        out_specs=[spec] * len(shapes),
        compiler_params=pltpu.CompilerParams(vmem_limit_bytes=24 * MIB),
        cost_estimate=pl.CostEstimate(flops=size // 8, bytes_accessed=size // 8, transcendentals=0),
    )(*args)


def join_kernel(starts, *refs):
    *parts, out, done = refs
    copies = []
    for n, part in enumerate(parts):
        width = part.shape[1]
        here = out.at[:, pl.ds(pl.multiple_of(starts[n], width), width)]
        copies.append(pltpu.make_async_copy(part.at[: out.shape[0], :], here, done.at[n]))
    for copy in copies:
        copy.start()
    for copy in copies:
        copy.wait()


def join(parts, starts):
    rows, width = parts[-1].shape
    return pl.pallas_call(
        join_kernel,
        out_shape=jax.ShapeDtypeStruct((rows, width * len(parts)), parts[0].dtype),
        in_specs=[SMEM] + [VMEM] * len(parts),
        out_specs=HBM,
        scratch_shapes=[pltpu.SemaphoreType.DMA((len(parts),))],
        compiler_params=pltpu.CompilerParams(vmem_limit_bytes=16 * MIB),
        cost_estimate=pl.CostEstimate(flops=0, bytes_accessed=4 * rows * width * len(parts), transcendentals=0),
    )(jnp.stack(starts).astype(jnp.int32), *parts)


def local(activations, cotangent, inner_weight, outer_weight, outer_momentum, next_activations):
    fsdp, nz = lax.axis_size("fsdp"), lax.axis_size("z")
    f, z, x, c = (lax.axis_index(a) for a in ("fsdp", "z", "x", "core"))
    tok, d = activations.shape
    kv = cotangent.shape[1]
    width = d // fsdp
    block = width // nz
    share = block // (PAIR * CORES)
    own_weight = inner_weight[0]
    swap = ring(CORES, 1)

    def column(b, i, k, s):
        return ((f + s) % fsdp) * width + b * block + i * CORES * share + ((c + k) % CORES) * share

    def pair_ring(k, s):
        at = lambda i, j: (i % CORES) * fsdp + j % fsdp
        return [(at(i, j), at(i + k, j + s)) for i in range(CORES) for j in range(fsdp)]

    shifts = [(k, s) for s in range(fsdp) for k in range(CORES)]
    stages = [(m + 1, m) for m in range(nz - 2, -1, -2)]

    far = [(i, k, s) for k in range(CORES) for i in range(PAIR) for s in range(fsdp)]
    early = [(0, 1, 0), (1, 0, 0)]
    late = [e for e in far if e not in early]
    index = lambda i, k, s: ((i % PAIR) * CORES + k % CORES) * fsdp + s % fsdp
    every = [(i, k, s) for i in range(PAIR) for k in range(CORES) for s in range(fsdp)]
    mine, nexts = {}, {}

    def next_groups(places):
        return [[column(z ^ m, (x + i) % PAIR, k, s) for m in range(nz)] for i, k, s in places]

    def send_next(i, k, s):
        pairs = [(index(*e), index(e[0] + i, e[1] + k, e[2] + s)) for e in every]
        nexts[i, k, s] = lax.ppermute(mine[i, k, s], ("x", "core", "fsdp"), pairs) if i or k or s else mine[i, k, s]

    cots = {(0, 0): cotangent}
    for s in range(1, fsdp):
        cots[0, s] = lax.ppermute(cotangent, "fsdp", ring(fsdp, s))
    columns = [[column(z ^ m, (x + i) % PAIR, k, s) for m in ms for i in range(PAIR)] for ms in stages for k, s in shifts]
    (packed,), _ = pack([(activations, 1, share, columns)])
    acts = []
    for stage in range(len(stages)):
        came = []
        for (k, s), part in zip(shifts, packed[stage * len(shifts) :]):
            came.append(part if (k, s) == (0, 0) else lax.ppermute(part, ("core", "fsdp"), pair_ring(k, s)))
        acts.append(came)
    other_weight = lax.ppermute(own_weight, "core", swap)
    cots[1, 0] = lax.ppermute(cotangent, "core", swap)
    for s in range(1, fsdp):
        cots[1, s] = lax.ppermute(cots[0, s], "core", swap)

    wanted = [cots[0, s] for s in range(1, fsdp)]
    (parts,), wanted = pack([(next_activations, 1, share, next_groups(far))], wanted, pltpu.HBM)
    cots.update({(0, s): got for s, got in enumerate(wanted, 1)})
    mine.update(zip(far, parts))

    ordered = [cots[k, s] for k, s in shifts]
    across_x, across_z = ring(PAIR, 1), [(i, i ^ 1) for i in range(nz)]
    over_z = {}

    def finish(m, to_z, to_x, keep_left, keep_right):
        from_z, from_x = lax.ppermute(to_z, "z", across_z), lax.ppermute(to_x, "x", across_x)
        return [keep_left, from_z, keep_right, from_x] + over_z.get(m, [])

    for stage, ms in enumerate(stages):
        cut = kv // 2 if ms[1] else 3 * kv // 4
        blocks = [((z ^ m) * PAIR + (x + i) % PAIR) * CORES + c for m in ms for i in range(PAIR)]
        place = jnp.stack(blocks).astype(jnp.int32)
        if not stage:
            place, *held = lax.optimization_barrier((place, *[mine[e] for e in far]))
            mine.update(zip(far, held))
            for e in early:
                send_next(*e)
        if stage:
            place, to_z, to_x = lax.optimization_barrier((place, to_z, to_x))
            m = stages[stage - 1][1]
            inputs = finish(m, to_z, to_x, keep_left, keep_right)
            low = m & -m
        to_x, stay_x, to_z, stay_z = inner_blocks(place, acts[stage], 0, ordered, own_weight, other_weight, share, cut)
        if stage:
            to_x, to_z, inputs[1], inputs[3] = lax.optimization_barrier((to_x, to_z, inputs[1], inputs[3]))
            (block_total,) = small_call(
                block_kernel, [jax.ShapeDtypeStruct((share, kv), bf16)], *inputs, spec=pl.BlockSpec()
            )
            over_z.setdefault(m ^ low, []).append(lax.ppermute(block_total, "z", [(i, i ^ low) for i in range(nz)]))
        if not stage:
            stay_x, *island_cots = lax.optimization_barrier((stay_x, *[cots[0, s] for s in range(fsdp)]))
            grad_rows = lax.dot_general(
                jnp.concatenate(island_cots, axis=0), own_weight, (((1,), (1,)), ((), ())), preferred_element_type=f32
            ).astype(bf16)
            parts = [grad_rows] + [grad_rows[s * tok : (s + 1) * tok] for s in range(1, fsdp)]
            stay_x, *parts = lax.optimization_barrier((stay_x, *parts))
            for s in range(1, fsdp):
                parts[s] = lax.ppermute(parts[s], "fsdp", ring(fsdp, -s))
        from_x, from_z = lax.ppermute(to_x, "x", across_x), lax.ppermute(to_z, "z", across_z)
        to_z, keep_left, to_x, keep_right = small_call(
            functools.partial(middle_kernel, share),
            [jax.ShapeDtypeStruct((share, wide), kind) for wide in (cut, kv - cut) for kind in (bf16, f32)],
            stay_x,
            from_x,
            stay_z,
            from_z,
            spec=pl.BlockSpec(),
        )

    inputs = finish(0, to_z, to_x, keep_left, keep_right)
    inputs[0], inputs[2] = small_call(
        gather_kernel, [jax.ShapeDtypeStruct(part.shape, f32) for part in (keep_left, keep_right)], keep_left, keep_right, *inputs[4:], spec=pl.BlockSpec(), weight=200
    )
    inputs[0], *held = lax.optimization_barrier((inputs[0], *[nexts[e] for e in early]))
    nexts.update(zip(early, held))
    replicas = nz * PAIR * CORES
    inputs = [*inputs[:4], outer_weight, outer_momentum]
    (share_rows,) = small_call(
        functools.partial(share_kernel, replicas),
        [jax.ShapeDtypeStruct((share, kv), bf16)],
        *inputs,
        spec=pl.BlockSpec(),
    )
    share_rows, *inputs = lax.optimization_barrier((share_rows, *inputs))
    new_outer, new_momentum = small_call(
        functools.partial(state_kernel, replicas),
        [jax.ShapeDtypeStruct((share, kv), f32)] * 2,
        *inputs,
        spec=pl.BlockSpec(),
        weight=1 << 17,
    )
    share_rows, *held = lax.optimization_barrier((share_rows, *[mine[e] for e in late]))
    mine.update(zip(late, held))
    for e in late:
        send_next(*e)

    rows = {}
    for m in sorted(range(1, nz), key=lambda m: (m & (m - 1)).bit_count() * nz - m):
        low = m & -m
        pieces = [share_rows] if m == low else list(rows[m ^ low])
        if m == nz - 1:
            pieces[0], new_outer = lax.optimization_barrier((pieces[0], new_outer))
        rows[m] = [lax.ppermute(piece, "z", [(i, i ^ low) for i in range(nz)]) for piece in pieces]
    rows = [[share_rows]] + [rows[m] for m in range(1, nz)]
    input_grad = join(parts, [((f + s) % fsdp) * width for s in range(fsdp)])

    half = len(far) // CORES
    near, away = [nexts[e] for e in far[:half]], [nexts[e] for e in far[half:]]
    give, keep = keys_part(away + near, rows[:-1], 0, outs=2)
    give, keep, input_grad = lax.optimization_barrier((give, keep, input_grad))
    last = (nz - 1) * share
    (give,) = keys_part(away, rows[-1:], last, [give], kind=bf16)
    (keep,) = keys_part(near, rows[-1:], last, [keep])
    came = lax.ppermute(give, "core", swap)
    shape = lambda n, kind: jax.ShapeDtypeStruct((n, kv // 2), kind)
    to_x, stay_x, stay_f, *to_f = small_call(
        functools.partial(core_sum_kernel, fsdp, tok),
        [shape(fsdp * tok, bf16), shape(fsdp * tok, f32), shape(PAIR * tok, f32)] + [shape(PAIR * tok, bf16)] * (fsdp - 1),
        keep,
        came,
    )

    def home(to_x, to_f):
        from_x = lax.ppermute(to_x, "x", ring(PAIR, 1))
        return [from_x] + [lax.ppermute(part, "fsdp", ring(fsdp, -s - 1)) for s, part in enumerate(to_f)]

    left, right, to_x, *to_f = small_call(
        functools.partial(second_sum_kernel, fsdp, tok),
        [shape(tok, f32)] * 2 + [shape(tok, bf16)] * fsdp,
        stay_x,
        stay_f,
        *home(to_x, to_f),
    )
    (keys,) = small_call(
        last_sum_kernel, [jax.ShapeDtypeStruct((tok, kv), bf16)], left, right, *home(to_x, to_f)
    )
    return (input_grad, keys, new_outer, new_momentum)


def solution(mesh):
    fsdp = mesh.shape["fsdp"]
    nz = mesh.shape["island"] // (PAIR * CORES)
    split = Mesh(mesh.devices.reshape(nz, PAIR, CORES, fsdp), ("z", "x", "core", "fsdp"))
    island = ("z", "x", "core")
    tokens = P(island + ("fsdp",), None)
    width = P(("fsdp",) + island, None)
    in_specs = (tokens, tokens, P(island, "fsdp", None), width, width, tokens)
    out_specs = (tokens, tokens, width, width)
    return jax.shard_map(local, mesh=split, in_specs=in_specs, out_specs=out_specs, check_vma=False)
```
